512 devices in a mesh: dp: 128 (over y, z, core), zero: 4 (over x).
Axes of the slice: x: 4, y: 8, z: 8, core: 2. Of those that a mesh axis runs over, the one named last changes fastest.
Arguments:
- patches: bfloat16 [16384, 1280], P('dp'), may hold values from -12 to 12
- cotangent: bfloat16 [16384, 1280], P('dp'), may hold values from -6 to 6
- send_order: int32 [128, 128], P('dp'), may hold values from 0 to 127, each once within a row
- recv_order: int32 [128, 128], P('dp'), may hold values from 0 to 127, each once within a row
- segment_ids: int32 [128, 128], P('dp'), may hold values from 0 to 7, as said below
- ln_gain: float32 [1280], replicated, may hold values from 0.5 to 1.5
- ln_bias: float32 [1280], replicated, may hold values from -3 to 3
- w_qkv: bfloat16 [1280, 8, 3, 80], P(None, 'zero'), may hold values from -1 to 1
- w_out: bfloat16 [8, 80, 1280], P('zero'), may hold values from -0.25 to 0.25
Outputs:
- encoded: bfloat16 [16384, 1280], P('dp', 'zero')
- input_grad: bfloat16 [16384, 1280], P('dp', 'zero')
- w_qkv_grad: float32 [1280, 8, 3, 80], P('dp', 'zero')
- w_out_grad: float32 [8, 80, 1280], P('zero', None, 'dp')
- gain_grad: float32 [1280], P('dp')
- bias_grad: float32 [1280], P('dp')
The draws below stay inside these ranges and needn't reach their ends.
Inputs may be any that keep to these rules, and one draw needn't show every extreme that they name: Each device's row of send_order is a permutation. Each device's row of recv_order is a permutation. `segment_ids`: numbers never fall along a device's rows; every image holds a multiple of one eighth of 128 rows; some device holds one image of all 128 rows.
All inputs are finite; a program needn't handle non-finite values.
Results may differ from the reference program's by a relative error of at most 0.025.
The reference program's roundings to bfloat16 on the way count: a program that leaves them out, or rounds other values in their place, can miss the bound.
Values may be sent and summed in bfloat16 or wider, within the bound.
No kernel may reach another device: no remote copies, remote signals or barrier semaphores. Data moves between devices by JAX's collectives and lax.ppermute only.
A program may use at most 64 MiB of HBM per device.

```python
import jax
import jax.numpy as jnp
from jax import lax

D = 1280
HD = 80
H = 8
ROWS = 128
HG = 2
TOKENS = 16384
N_DP = 128
N_ZERO = 4


def draw_patches(key, part):
    key = jax.random.fold_in(key, 5)
    key_base = jax.random.fold_in(key, 0)
    sample = jax.random.normal(key_base, (TOKENS, D), jnp.float32)
    return jnp.clip(sample, -12.0, 12.0).astype(jnp.bfloat16)


def draw_w_qkv(key, part):
    key = jax.random.fold_in(key, 7)
    key_base = jax.random.fold_in(key, 0)
    base_part = jax.random.normal(key_base, (D, H, 3, HD), jnp.float32) * D ** (-0.5)
    sample = base_part
    return jnp.clip(sample, -1.0, 1.0).astype(jnp.bfloat16)


def draw_segment_ids(key, part):
    key = jax.random.fold_in(key, 11)
    key_cuts, key_lone, key_full = jax.random.split(key, 3)
    cut_flags = jax.random.randint(key_cuts, (N_DP, 7), 0, 2)
    lone_row = jax.random.randint(key_lone, (), 0, N_DP)
    full_row = (lone_row + 1 + jax.random.randint(key_full, (), 0, N_DP - 1)) % N_DP
    device_ids = jnp.arange(N_DP)[:, None]
    cut_flags = jnp.where(device_ids == lone_row, 0, cut_flags)
    cut_flags = jnp.where(device_ids == full_row, 1, cut_flags)
    labels = jnp.concatenate([jnp.zeros((N_DP, 1), jnp.int32), jnp.cumsum(cut_flags, axis=1).astype(jnp.int32)], axis=1)
    return jnp.repeat(labels, ROWS // 8, axis=1).astype(jnp.int32)


def steps_of(stream_key, shape, cuts, smallest, top_value):
    level, own = 1.0, jax.random.fold_in(stream_key, 6)
    for dim, parts in cuts:
        draws = jnp.exp(jax.random.uniform(jax.random.fold_in(own, dim), (parts,), jnp.float32, smallest / len(cuts), top_value / len(cuts)))
        level = level * jnp.repeat(draws, shape[dim] // parts).reshape([-1 if axis == dim else 1 for axis in range(len(shape))])
    return level


def gaussian(stream_key, dims, scale, bound, cuts=(), kind=jnp.bfloat16):
    values = scale * jax.random.normal(stream_key, dims, jnp.float32)
    if cuts:
        values = values * steps_of(stream_key, dims, cuts, -0.22, 0.18)
    return jnp.clip(values, -bound, bound).astype(kind)


def setup_inputs(seed: int = 0) -> dict:
    seeds = jax.random.split(jax.random.key(seed), 10)
    return {
        "patches": draw_patches(jax.random.fold_in(seeds[9], 71), 0),
        "cotangent": gaussian(seeds[1], (TOKENS, D), 1.0, 6.0, ((0, 128),)),
        "send_order": jax.vmap(lambda own: jax.random.permutation(own, ROWS))(jax.random.split(seeds[2], N_DP)).reshape((N_DP, ROWS)).astype(jnp.int32),
        "recv_order": jax.vmap(lambda own: jax.random.permutation(own, ROWS))(jax.random.split(seeds[3], N_DP)).reshape((N_DP, ROWS)).astype(jnp.int32),
        "segment_ids": draw_segment_ids(jax.random.fold_in(seeds[9], 71), 0),
        "ln_gain": jnp.clip(1.0 + 0.1 * jax.random.normal(seeds[5], (D,), jnp.float32), 0.5, 1.5),
        "ln_bias": gaussian(seeds[6], (D,), 0.5, 3.0, (), jnp.float32),
        "w_qkv": draw_w_qkv(jax.random.fold_in(seeds[9], 71), 0),
        "w_out": gaussian(seeds[8], (H, HD, D), (H * HD) ** -0.5, 0.25, ((0, 4),)),
    }


EPS = 1e-06

def rounded(value):
    return lax.optimization_barrier(value.astype(jnp.bfloat16)).astype(jnp.float32)

def layer_device(inputs, grads_in, segment_rows, ln_gain, ln_bias, w_qkv, w_out):
    row_count = inputs.shape[0]
    score_scale = HD ** (-0.5)
    inputs32 = inputs.astype(jnp.float32)
    row_mean = lax.optimization_barrier(jnp.mean(inputs32, axis=1, keepdims=True))
    centred = inputs32 - row_mean
    inv_std = lax.rsqrt(lax.optimization_barrier(jnp.mean(centred * centred, axis=1, keepdims=True)) + EPS)
    x_hat = centred * inv_std
    normed = (x_hat * ln_gain + ln_bias).astype(jnp.bfloat16)
    flat_qkv = w_qkv.reshape(D, H * 3 * HD)
    proj_qkv = rounded(jnp.dot(normed, flat_qkv, preferred_element_type=jnp.float32))
    proj_qkv = proj_qkv.reshape(row_count, H, 3, HD)
    queries = proj_qkv[:, :, 0]
    key_rows = proj_qkv[:, :, 1]
    values = proj_qkv[:, :, 2]
    same_image = (segment_rows[:, None] == segment_rows[None, :])[None]
    scores = jnp.einsum('qhd,khd->hqk', queries, key_rows) * score_scale
    scores = jnp.where(same_image, scores, -1e+30)
    row_max = lax.optimization_barrier(jnp.max(scores, axis=2, keepdims=True))
    exponent = jnp.exp(scores - row_max)
    weights32 = exponent / lax.optimization_barrier(jnp.sum(exponent, axis=2, keepdims=True))
    weights16 = rounded(weights32)
    head_out = rounded(jnp.einsum('hqk,khd->qhd', weights16, values))
    head_flat = head_out.reshape(row_count, H * HD)
    grouped = head_out.reshape(row_count, N_ZERO, HG * HD)
    w_grouped = w_out.reshape(N_ZERO, HG * HD, D).astype(jnp.float32)
    partial_value = rounded(jnp.einsum('rgk,gkd->grd', grouped, w_grouped))
    encoded_rows = (inputs32 + lax.optimization_barrier(jnp.sum(partial_value, axis=0))).astype(jnp.bfloat16)
    grads32 = grads_in.astype(jnp.float32)
    wide_out = w_out.reshape(H * HD, D).astype(jnp.float32)
    head_grad = rounded(jnp.einsum('rd,kd->rk', grads32, wide_out)).reshape(row_count, H, HD)
    out_term = jnp.einsum('rk,rd->kd', head_flat, grads32)
    prob_grad = jnp.einsum('qhd,khd->hqk', head_grad, values)
    row_delta = lax.optimization_barrier(jnp.sum(prob_grad * weights32, axis=2, keepdims=True))
    score_grad = rounded(weights32 * (prob_grad - row_delta) * score_scale)
    query_grad = jnp.einsum('hqk,khd->qhd', score_grad, key_rows)
    key_grad = jnp.einsum('hqk,qhd->khd', score_grad, queries)
    value_grad = jnp.einsum('hqk,qhd->khd', weights16, head_grad)
    qkv_grad = jnp.stack([query_grad, key_grad, value_grad], axis=2).astype(jnp.bfloat16)
    qkv_grad = qkv_grad.reshape(row_count, H * 3 * HD)
    qkv_term = jnp.dot(normed.T, qkv_grad, preferred_element_type=jnp.float32)
    normed_grad = jnp.dot(qkv_grad, flat_qkv.T, preferred_element_type=jnp.float32)
    gain_term = lax.optimization_barrier(jnp.sum(normed_grad * x_hat, axis=0))
    bias_term = lax.optimization_barrier(jnp.sum(normed_grad, axis=0))
    scaled = normed_grad * ln_gain
    row_grads = grads32 + inv_std * (scaled - lax.optimization_barrier(jnp.mean(scaled, axis=1, keepdims=True)) - x_hat * lax.optimization_barrier(jnp.mean(scaled * x_hat, axis=1, keepdims=True)))
    return (encoded_rows, row_grads.astype(jnp.bfloat16), qkv_term, out_term, gain_term, bias_term)

def reference(patches, cotangent, send_order, recv_order, segment_ids, ln_gain, ln_bias, w_qkv, w_out):
    per_peer = ROWS // N_DP
    blocks = send_order.reshape(N_DP, N_DP, per_peer)
    owner_index = (recv_order // per_peer).astype(jnp.int32)
    slot_index = (recv_order % per_peer).astype(jnp.int32)
    encoder_index = jnp.arange(N_DP, dtype=jnp.int32)[:, None] * jnp.ones((1, ROWS), jnp.int32)
    local_row = blocks[owner_index, encoder_index, slot_index]
    source = (owner_index * ROWS + local_row).astype(jnp.int32)
    inputs = patches[source]
    grads_in = cotangent[source]

    def device_step(carried, pieces):
        outcome = layer_device(pieces[0], pieces[1], pieces[2], ln_gain, ln_bias, w_qkv, w_out)
        carried = (carried[0] + outcome[2], carried[1] + outcome[3], carried[2] + outcome[4], carried[3] + outcome[5])
        return (carried, (outcome[0], outcome[1]))
    zeros_init = (jnp.zeros((D, H * 3 * HD), jnp.float32), jnp.zeros((H * HD, D), jnp.float32), jnp.zeros((D,), jnp.float32), jnp.zeros((D,), jnp.float32))
    grad_sums, (encoded_all, grads_all) = lax.scan(device_step, zeros_init, (inputs, grads_in, segment_ids))
    flat_source = source.reshape(-1)
    encoded = jnp.zeros((TOKENS, D), jnp.bfloat16).at[flat_source].set(encoded_all.reshape(-1, D))
    input_grad = jnp.zeros((TOKENS, D), jnp.bfloat16).at[flat_source].set(grads_all.reshape(-1, D))
    return (encoded, input_grad, grad_sums[0].reshape(D, H, 3, HD), grad_sums[1].reshape(H, HD, D), grad_sums[2], grad_sums[3])
```

```python
import jax
import jax.numpy as jnp
import numpy as np
from jax import lax
from jax.experimental import pallas as pl
from jax.experimental.pallas import tpu as pltpu
from jax.sharding import PartitionSpec as P

EPS = 1e-06
R = 128
D = 1280
HD = 80
HG = 2
NQ = HG * 3 * HD
NO = HG * HD
QW = D // 4
QP = 384
F32 = jnp.float32
BF = jnp.bfloat16
GAIN_AT = 64
BIAS_AT = 74
MEAN_AT = 84

_cp = pltpu.CompilerParams(vmem_limit_bytes=24 * 1024 * 1024)


def dg(a, b, ca, cb):
    return lax.dot_general(a, b, (((ca,), (cb,)), ((), ())), preferred_element_type=F32)


def call(body, outs, *args, smem=(), cost=None):
    return pl.pallas_call(
        body,
        out_shape=tuple(jax.ShapeDtypeStruct(s, d) for s, d in outs),
        in_specs=[
            pl.BlockSpec(memory_space=pltpu.SMEM if i in smem else pltpu.VMEM)
            for i in range(len(args))
        ],
        out_specs=tuple(pl.BlockSpec(memory_space=pltpu.VMEM) for _ in outs),
        compiler_params=_cp,
        cost_estimate=cost,
    )(*args)


def lane(shape):
    return lax.broadcasted_iota(jnp.int32, shape, 1)


def sub(shape):
    return lax.broadcasted_iota(jnp.int32, shape, 0)


def gather_body(send_ref, x_ref, o_ref):
    pick = (sub((R, R)) == send_ref[...]).astype(F32).astype(BF)
    o_ref[...] = dg(pick, x_ref[...], 0, 0).astype(BF)


def norm_stats(x):
    mean = jnp.mean(x, axis=1, keepdims=True)
    centred = x - mean
    inv = lax.rsqrt(jnp.mean(centred * centred, axis=1, keepdims=True) + EPS)
    return mean, inv, centred * inv


def fwd_body(
    x_ref, recv_ref, seg_ref, gain_ref, bias_ref, wq_ref, wo_ref,
    p_ref, normed_ref, qkv_ref, w32_ref, ho_ref, stat_ref,
):
    x = x_ref[...].astype(F32)
    mean, inv, xh = norm_stats(x)
    stat_ref[...] = jnp.where(lane((R, R)) < 64, mean, inv)
    normed = (xh * gain_ref[...] + bias_ref[...]).astype(BF)
    normed_ref[...] = normed
    qkv = dg(wq_ref[...], normed, 1, 1).astype(BF)
    qkv_ref[...] = qkv
    place = sub((R, R)) == recv_ref[...]
    seg = jnp.sum(jnp.where(place, seg_ref[...], 0), axis=1, keepdims=True)
    group = (seg == lane((R, R))).astype(F32).astype(BF)
    same = dg(group, group, 1, 1) > 0.5
    outs = []
    for h in range(HG):
        q = qkv[h * 3 * HD : h * 3 * HD + HD]
        k = qkv[h * 3 * HD + HD : h * 3 * HD + 2 * HD]
        v = qkv[h * 3 * HD + 2 * HD : (h + 1) * 3 * HD]
        s = jnp.where(same, dg(q, k, 0, 0) * (HD**-0.5), -1e30)
        e = jnp.exp(s - jnp.max(s, axis=1, keepdims=True))
        w = e / jnp.sum(e, axis=1, keepdims=True)
        w32_ref[h] = w
        outs.append(dg(v, w.astype(BF), 1, 1).astype(BF))
    ho = jnp.concatenate(outs, axis=0)
    ho_ref[...] = ho
    p = dg(ho, wo_ref[...], 0, 0)
    pad = jnp.zeros((R, QP - QW), F32)
    for g in range(4):
        part = jnp.concatenate([p[:, g * QW : (g + 1) * QW], pad], axis=1)
        p_ref[g] = part.astype(BF)


def bwd_body(
    x_ref, g_ref, gain_ref, wq_ref, wo_ref, qkv_ref, w32_ref, sel_ref, place_ref,
    n_ref, qg_ref,
):
    _, _, xh = norm_stats(x_ref[...].astype(F32))
    dh = dg(wo_ref[...], g_ref[...], 1, 1).astype(BF)
    parts = []
    for h in range(HG):
        q = qkv_ref[h * 3 * HD : h * 3 * HD + HD]
        k = qkv_ref[h * 3 * HD + HD : h * 3 * HD + 2 * HD]
        v = qkv_ref[h * 3 * HD + 2 * HD : (h + 1) * 3 * HD]
        dhh = dh[h * HD : (h + 1) * HD]
        w = w32_ref[h]
        pg = dg(dhh, v, 0, 0)
        delta = jnp.sum(pg * w, axis=1, keepdims=True)
        sg = (w * (pg - delta) * (HD**-0.5)).astype(BF)
        parts.append(dg(k, sg, 1, 1).astype(BF))
        parts.append(dg(q, sg, 1, 0).astype(BF))
        parts.append(dg(dhh, w.astype(BF), 1, 0).astype(BF))
    qg = jnp.concatenate(parts, axis=0)
    qg_ref[...] = qg
    n = dg(qg, wq_ref[...], 0, 0)
    nx = n * xh
    u = n * gain_ref[...]
    m1 = jnp.sum(u, axis=1, keepdims=True) * (1.0 / D)
    m2 = jnp.sum(u * xh, axis=1, keepdims=True) * (1.0 / D)
    gain_row = jnp.sum(nx, axis=0, keepdims=True)
    bias_row = jnp.sum(n, axis=0, keepdims=True)
    sel = sel_ref[...].astype(F32)
    extra = dg((sel * gain_row).astype(BF), place_ref[0], 1, 0)
    extra = extra + dg((sel * bias_row).astype(BF), place_ref[1], 1, 0)
    ln = lane((R, R))
    for j, m in enumerate((m1, m2)):
        hi = m.astype(BF).astype(F32)
        extra = jnp.where(ln == MEAN_AT + 2 * j, hi, extra)
        extra = jnp.where(ln == MEAN_AT + 2 * j + 1, m - hi, extra)
    for g in range(4):
        part = jnp.concatenate([n[:, g * QW : (g + 1) * QW], extra[:, 64:]], axis=1)
        n_ref[g] = part.astype(BF)


def wgrad_body(c_ref, normed_ref, g_ref, qg_ref, ho_ref, keep_ref, send_ref):
    left = jnp.concatenate([normed_ref[...], g_ref[...]], axis=0)
    c = c_ref[0]
    for out, head in ((send_ref, 1 - c), (keep_ref, c)):
        a = qg_ref[pl.ds(pl.multiple_of(head * 3 * HD, 3 * HD), 3 * HD), :]
        b = ho_ref[pl.ds(pl.multiple_of(head * HD, HD), HD), :]
        right = jnp.concatenate(
            [
                jnp.concatenate([a, jnp.zeros((3 * HD, R), BF)], axis=1),
                jnp.concatenate([jnp.zeros((HD, R), BF), b], axis=1),
            ],
            axis=0,
        )
        out[...] = dg(left, right, 0, 1).astype(out.dtype)


def post_body(p_ref, n_ref, x_ref, g_ref, stat_ref, gain_ref, o_ref):
    ps = jnp.sum(p_ref[...].astype(F32), axis=0)
    ns = jnp.sum(n_ref[...].astype(F32), axis=0)
    x = x_ref[...].astype(F32)
    mean = stat_ref[:, 0:1]
    inv = stat_ref[:, 64:65]
    xh = (x - mean) * inv
    tile = ns[:, 256:]
    ln = lane((R, R))
    m1 = jnp.sum(jnp.where((ln == MEAN_AT) | (ln == MEAN_AT + 1), tile, 0.0), axis=1, keepdims=True)
    m2 = jnp.sum(
        jnp.where((ln == MEAN_AT + 2) | (ln == MEAN_AT + 3), tile, 0.0), axis=1, keepdims=True
    )
    o_ref[:, :QP] = (x + ps).astype(BF)
    grad = g_ref[...].astype(F32) + inv * (ns * gain_ref[...] - m1 - xh * m2)
    o_ref[:, QP : QP + 256] = grad[:, :256].astype(BF)
    o_ref[:, QP + 256 :] = jnp.where(ln < 64, grad[:, 256:], tile).astype(BF)


def final_body(send_ref, b_ref, e_ref, i_ref, s_ref):
    pick = (sub((R, R)) == send_ref[...]).astype(F32).astype(BF)
    e_ref[...] = dg(b_ref[:, :QP], pick, 0, 1)[:QW].astype(BF)
    i_ref[...] = dg(b_ref[:, QP:], pick, 0, 1)[:QW].astype(BF)
    s_ref[...] = jnp.broadcast_to(
        jnp.sum(b_ref[:, QP + 256 :].astype(F32), axis=0, keepdims=True), (8, R)
    )


_f = np.arange(D)
SEL = (_f[None, :] // 10 == np.arange(R)[:, None]).astype(np.float32)
PLACE = np.stack(
    [(_f[:, None] % 10 + at == np.arange(R)[None, :]).astype(np.float32) for at in (GAIN_AT, BIAS_AT)]
)


def local(patches, cotangent, send_order, recv_order, segment_ids, ln_gain, ln_bias, w_qkv, w_out):
    zero = lax.axis_index("zero")
    core = lax.rem(lax.axis_index("dp"), 2)
    wq = w_qkv.transpose(1, 2, 3, 0).reshape(NQ, D)
    wo = w_out.reshape(NO, D)
    gain = ln_gain.reshape(1, D)
    bias = ln_bias.reshape(1, D)
    sel = jnp.asarray(SEL, BF)
    place = jnp.asarray(PLACE, BF)

    (xs,) = call(gather_body, [((R, D), BF)], send_order, patches)
    (gs,) = call(gather_body, [((R, D), BF)], send_order, cotangent)
    x = lax.all_to_all(xs, "dp", 0, 0, tiled=True)
    g = lax.all_to_all(gs, "dp", 0, 0, tiled=True)

    p4, normed, qkv, w32, ho, stat = call(
        fwd_body,
        [
            ((4, R, QP), BF),
            ((R, D), BF),
            ((NQ, R), BF),
            ((HG, R, R), F32),
            ((NO, R), BF),
            ((R, R), F32),
        ],
        x, recv_order, segment_ids, gain, bias, wq, wo,
    )
    p4 = lax.all_to_all(p4, "zero", 0, 0, tiled=True)
    n4, qg = call(
        bwd_body,
        [((4, R, QP), BF), ((NQ, R), BF)],
        x, g, gain, wq, wo, qkv, w32, sel, place,
    )
    n4 = lax.all_to_all(n4, "zero", 0, 0, tiled=True)
    keep, send = call(
        wgrad_body,
        [((D, 4 * HD), F32), ((D, 4 * HD), BF)],
        core.reshape(1), normed, g, qg, ho,
        smem=(0,),
    )
    got = lax.ppermute(send, "dp", [(i, i ^ 1) for i in range(128)])
    wg = (keep + got.astype(F32)).astype(BF).reshape(R, 40 * HD)
    wg = lax.all_to_all(wg, "dp", 0, 0, tiled=True)

    def quarter(a):
        a = lax.dynamic_slice_in_dim(a, zero * QW, QW, 1)
        return jnp.pad(a, ((0, 0), (0, QP - QW)))

    (back,) = call(
        post_body,
        [((R, 2 * QP), BF)],
        p4, n4, quarter(x), quarter(g), stat, quarter(gain),
    )
    back = lax.all_to_all(back, "dp", 0, 0, tiled=True)
    enc, grad, sums = call(
        final_body,
        [((QW, R), BF), ((QW, R), BF), ((8, R), F32)],
        send_order, back,
    )
    wsum = jnp.sum(wg.reshape(64, 2, 10, 4 * HD).astype(F32), axis=0)
    qkv_share = wsum[:, :, : 3 * HD].reshape(2, 10, 3, HD).transpose(1, 0, 2, 3)
    out_share = wsum[:, :, 3 * HD :].transpose(0, 2, 1)
    return (
        enc.T,
        grad.T,
        qkv_share,
        out_share,
        sums[0, GAIN_AT : GAIN_AT + 10],
        sums[0, BIAS_AT : BIAS_AT + 10],
    )


def solution(mesh):
    return jax.shard_map(
        local,
        mesh=mesh,
        in_specs=(
            P("dp", None),
            P("dp", None),
            P("dp", None),
            P("dp", None),
            P("dp", None),
            P(),
            P(),
            P(None, "zero", None, None),
            P("zero", None, None),
        ),
        out_specs=(
            P("dp", "zero"),
            P("dp", "zero"),
            P("dp", "zero", None, None),
            P("zero", None, "dp"),
            P("dp"),
            P("dp"),
        ),
        check_vma=False,
    )
```

```python
import jax
import jax.numpy as jnp
import numpy as np
from jax import lax
from jax.experimental import pallas as pl
from jax.experimental.pallas import tpu as pltpu
from jax.sharding import PartitionSpec as P

EPS = 1e-06
R = 128
D = 1280
HD = 80
HG = 2
NQ = HG * 3 * HD
NO = HG * HD
QW = D // 4
QP = 384
F32 = jnp.float32
BF = jnp.bfloat16
GAIN_AT = 64
BIAS_AT = 74
MEAN_AT = 84
WG = 1664

_cp = pltpu.CompilerParams(vmem_limit_bytes=24 * 1024 * 1024)


def dg(a, b, ca, cb):
    return lax.dot_general(a, b, (((ca,), (cb,)), ((), ())), preferred_element_type=F32)


def call(body, outs, *args, smem=(), cost=None):
    return pl.pallas_call(
        body,
        out_shape=tuple(jax.ShapeDtypeStruct(s, d) for s, d in outs),
        in_specs=[
            pl.BlockSpec(memory_space=pltpu.SMEM if i in smem else pltpu.VMEM)
            for i in range(len(args))
        ],
        out_specs=tuple(pl.BlockSpec(memory_space=pltpu.VMEM) for _ in outs),
        compiler_params=_cp,
        cost_estimate=cost,
    )(*args)


def lane(shape):
    return lax.broadcasted_iota(jnp.int32, shape, 1)


def sub(shape):
    return lax.broadcasted_iota(jnp.int32, shape, 0)


def gather_body(send_ref, x_ref, g_ref, o_ref):
    pick = (sub((R, R)) == send_ref[...]).astype(F32).astype(BF)
    o_ref[:, :D] = dg(pick, x_ref[...], 0, 0).astype(BF)
    o_ref[:, D:] = dg(pick, g_ref[...], 0, 0).astype(BF)


def norm_stats(x):
    mean = jnp.mean(x, axis=1, keepdims=True)
    centred = x - mean
    inv = lax.rsqrt(jnp.mean(centred * centred, axis=1, keepdims=True) + EPS)
    return mean, inv, centred * inv


def block_body(
    xg_ref, recv_ref, seg_ref, gain_ref, bias_ref, wq_ref, wo_ref, sel_ref, place_ref,
    pn_ref, normed_ref, qg_ref, ho_ref, stat_ref,
):
    x = xg_ref[:, :D].astype(F32)
    g = xg_ref[:, D:]
    mean, inv, xh = norm_stats(x)
    stat_ref[...] = jnp.where(lane((R, R)) < 64, mean, inv)
    normed = (xh * gain_ref[...] + bias_ref[...]).astype(BF)
    normed_ref[...] = normed
    qkv = dg(wq_ref[...], normed, 1, 1).astype(BF)
    dh = dg(wo_ref[...], g, 1, 1).astype(BF)
    place = sub((R, R)) == recv_ref[...]
    seg = jnp.sum(jnp.where(place, seg_ref[...], 0), axis=1, keepdims=True)
    group = (seg == lane((R, R))).astype(F32).astype(BF)
    same = dg(group, group, 1, 1) > 0.5
    outs, parts = [], []
    for h in range(HG):
        q = qkv[h * 3 * HD : h * 3 * HD + HD]
        k = qkv[h * 3 * HD + HD : h * 3 * HD + 2 * HD]
        v = qkv[h * 3 * HD + 2 * HD : (h + 1) * 3 * HD]
        dhh = dh[h * HD : (h + 1) * HD]
        s = jnp.where(same, dg(q, k, 0, 0) * (HD**-0.5), -1e30)
        e = jnp.exp(s - jnp.max(s, axis=1, keepdims=True))
        w = e / jnp.sum(e, axis=1, keepdims=True)
        w16 = w.astype(BF)
        outs.append(dg(v, w16, 1, 1).astype(BF))
        pg = dg(dhh, v, 0, 0)
        delta = jnp.sum(pg * w, axis=1, keepdims=True)
        sg = (w * (pg - delta) * (HD**-0.5)).astype(BF)
        parts.append(dg(k, sg, 1, 1).astype(BF))
        parts.append(dg(q, sg, 1, 0).astype(BF))
        parts.append(dg(dhh, w16, 1, 0).astype(BF))
    ho = jnp.concatenate(outs, axis=0)
    ho_ref[...] = ho
    qg = jnp.concatenate(parts, axis=0)
    qg_ref[...] = qg
    p = dg(ho, wo_ref[...], 0, 0)
    n = dg(qg, wq_ref[...], 0, 0)
    u = n * gain_ref[...]
    m1 = jnp.sum(u, axis=1, keepdims=True) * (1.0 / D)
    m2 = jnp.sum(u * xh, axis=1, keepdims=True) * (1.0 / D)
    gain_row = jnp.sum(n * xh, axis=0, keepdims=True)
    bias_row = jnp.sum(n, axis=0, keepdims=True)
    sel = sel_ref[...].astype(F32)
    extra = dg((sel * gain_row).astype(BF), place_ref[0], 1, 0)
    extra = extra + dg((sel * bias_row).astype(BF), place_ref[1], 1, 0)
    ln = lane((R, R))
    for j, m in enumerate((m1, m2)):
        hi = m.astype(BF).astype(F32)
        extra = jnp.where(ln == MEAN_AT + 2 * j, hi, extra)
        extra = jnp.where(ln == MEAN_AT + 2 * j + 1, m - hi, extra)
    pad = jnp.zeros((R, QP - QW), F32)
    for i in range(4):
        part = jnp.concatenate([p[:, i * QW : (i + 1) * QW], pad], axis=1)
        pn_ref[i, :, :QP] = part.astype(BF)
        part = jnp.concatenate([n[:, i * QW : (i + 1) * QW], extra[:, 64:]], axis=1)
        pn_ref[i, :, QP:] = part.astype(BF)


def wgrad_body(c_ref, normed_ref, xg_ref, qg_ref, ho_ref, keep_ref, send_ref):
    c = c_ref[0]
    for out, head in ((send_ref, 1 - c), (keep_ref, c)):
        a = qg_ref[pl.ds(pl.multiple_of(head * 3 * HD, 3 * HD), 3 * HD), :]
        b = ho_ref[pl.ds(pl.multiple_of(head * HD, HD), HD), :]
        out[: 3 * HD, :] = dg(a, normed_ref[...], 1, 0).astype(out.dtype)
        out[3 * HD :, :] = dg(b, xg_ref[:, D:], 1, 0).astype(out.dtype)


def pair_body(c_ref, keep_ref, got_ref, own_ref, sz_ref, sy_ref):
    z = c_ref[1]
    y = c_ref[2]

    def rows(j):
        at = pl.ds(pl.multiple_of(j * HD, HD), HD)
        return keep_ref[at, :] + got_ref[at, :].astype(F32)

    sz_ref[...] = rows(1 - z).astype(BF)
    sy_ref[...] = rows(3 - y).astype(BF)
    own_ref[:HD, :] = rows(z)
    own_ref[HD:, :] = rows(2 + y)


def post_body(
    pn_ref, x_ref, g_ref, stat_ref, gain_ref, own_ref, gz_ref, gy_ref, order_ref, o_ref
):
    pn = jnp.sum(pn_ref[...].astype(F32), axis=0)
    ps = pn[:, :QP]
    ns = pn[:, QP:]
    x = x_ref[...].astype(F32)
    mean = stat_ref[:, 0:1]
    inv = stat_ref[:, 64:65]
    xh = (x - mean) * inv
    tile = ns[:, 256:]
    ln = lane((R, R))
    m1 = jnp.sum(jnp.where((ln == MEAN_AT) | (ln == MEAN_AT + 1), tile, 0.0), axis=1, keepdims=True)
    m2 = jnp.sum(
        jnp.where((ln == MEAN_AT + 2) | (ln == MEAN_AT + 3), tile, 0.0), axis=1, keepdims=True
    )
    enc = x + ps
    grad = g_ref[...].astype(F32) + inv * (ns * gain_ref[...] - m1 - xh * m2)
    got = jnp.concatenate([gz_ref[...], gy_ref[...]], axis=0).astype(F32)
    wg = (own_ref[...] + got).astype(BF)
    wg = dg(order_ref[...], wg, 1, 1)
    slabs = [wg[i * R : (i + 1) * R] for i in range(10)]
    o_ref[...] = jnp.concatenate(
        slabs + [tile[:, 64:], enc[:, :QW], grad[:, :QW]], axis=1
    ).astype(BF)


def final_body(send_ref, b_ref, e_ref, i_ref, a_ref, w_ref, gain_ref, bias_ref):
    pick = (sub((R, R)) == send_ref[...]).astype(F32).astype(BF)
    rows = dg(b_ref[:, WG:], pick, 0, 1).astype(BF)
    e_ref[...] = rows[:QW]
    i_ref[...] = rows[QW:]
    row = sub((16, R))
    src = lane((16, R))
    half = (row // 2) % 2
    c_ok = src % 2 == row % 2
    z_ok = (src // 2) % 2 == half
    y_ok = (src // 16) % 2 == half
    mask = ((row < 4) & c_ok & z_ok) | ((row >= 4) & (row < 8) & c_ok & y_ok) | (row == 8)
    sums = dg(mask.astype(F32).astype(BF), b_ref[:, :WG], 1, 0)
    for i in range(10):
        at = i * 2 * HD
        a_ref[i, 0] = sums[0:2, at : at + HD]
        a_ref[i, 1] = sums[2:4, at : at + HD]
        a_ref[i, 2] = sums[4:6, at + HD : at + 2 * HD]
        w_ref[i] = sums[6:8, at + HD : at + 2 * HD]
    gain_ref[...] = sums[8:9, WG - 64 : WG - 54]
    bias_ref[...] = sums[8:9, WG - 54 : WG - 44]


_f = np.arange(D)
SEL = (_f[None, :] // 10 == np.arange(R)[:, None]).astype(np.float32)
PLACE = np.stack(
    [(_f[:, None] % 10 + at == np.arange(R)[None, :]).astype(np.float32) for at in (GAIN_AT, BIAS_AT)]
)


ORDER = np.zeros((D, D), np.float32)
ORDER[np.arange(D), (np.arange(D) % R) * 10 + np.arange(D) // R] = 1.0


def local(patches, cotangent, send_order, recv_order, segment_ids, ln_gain, ln_bias, w_qkv, w_out):
    zero = lax.axis_index("zero")
    dp = lax.axis_index("dp")
    bits = jnp.stack([dp & 1, (dp >> 1) & 1, (dp >> 4) & 1])
    wq = w_qkv.transpose(1, 2, 3, 0).reshape(NQ, D)
    wo = w_out.reshape(NO, D)
    gain = ln_gain.reshape(1, D)
    bias = ln_bias.reshape(1, D)
    sel = jnp.asarray(SEL, BF)
    place = jnp.asarray(PLACE, BF)
    order = jnp.asarray(ORDER, BF)

    def swap(a, bit):
        return lax.ppermute(a, "dp", [(i, i ^ bit) for i in range(128)])

    (xg,) = call(gather_body, [((R, 2 * D), BF)], send_order, patches, cotangent)
    xg = lax.all_to_all(xg, "dp", 0, 0, tiled=True)
    pn, normed, qg, ho, stat = call(
        block_body,
        [((4, R, 2 * QP), BF), ((R, D), BF), ((NQ, R), BF), ((NO, R), BF), ((R, R), F32)],
        xg, recv_order, segment_ids, gain, bias, wq, wo, sel, place,
    )
    pn = lax.all_to_all(pn, "zero", 0, 0, tiled=True)
    keep, send = call(
        wgrad_body,
        [((4 * HD, D), F32), ((4 * HD, D), BF)],
        bits, normed, xg, qg, ho,
        smem=(0,),
    )
    own, sz, sy = call(
        pair_body,
        [((2 * HD, D), F32), ((HD, D), BF), ((HD, D), BF)],
        bits, keep, swap(send, 1),
        smem=(0,),
    )
    gz = swap(sz, 2)
    gy = swap(sy, 16)

    def quarter(a, at=0):
        a = lax.dynamic_slice_in_dim(a, at + zero * QW, QW, 1)
        return jnp.pad(a, ((0, 0), (0, QP - QW)))

    (back,) = call(
        post_body,
        [((R, WG + 2 * QW), BF)],
        pn, quarter(xg), quarter(xg, D), stat, quarter(gain), own, gz, gy, order,
    )
    back = lax.all_to_all(back, "dp", 0, 0, tiled=True)
    enc, grad, qkv_share, out_share, gain_grad, bias_grad = call(
        final_body,
        [
            ((QW, R), BF),
            ((QW, R), BF),
            ((10, 3, 2, HD), F32),
            ((10, 2, HD), F32),
            ((1, 10), F32),
            ((1, 10), F32),
        ],
        send_order, back,
    )
    return (
        enc.T,
        grad.T,
        qkv_share.transpose(0, 2, 1, 3),
        out_share.transpose(1, 2, 0),
        gain_grad.reshape(10),
        bias_grad.reshape(10),
    )


def solution(mesh):
    return jax.shard_map(
        local,
        mesh=mesh,
        in_specs=(
            P("dp", None),
            P("dp", None),
            P("dp", None),
            P("dp", None),
            P("dp", None),
            P(),
            P(),
            P(None, "zero", None, None),
            P("zero", None, None),
        ),
        out_specs=(
            P("dp", "zero"),
            P("dp", "zero"),
            P("dp", "zero", None, None),
            P("zero", None, "dp"),
            P("dp"),
            P("dp"),
        ),
        check_vma=False,
    )
```

```python
import jax
import jax.numpy as jnp
import numpy as np
from jax import lax
from jax.experimental import pallas as pl
from jax.experimental.pallas import tpu as pltpu
from jax.sharding import PartitionSpec as P

EPS = 1e-06
R = 128
D = 1280
HD = 80
HG = 2
NQ = HG * 3 * HD
NO = HG * HD
QW = D // 4
QP = 384
F32 = jnp.float32
BF = jnp.bfloat16
GAIN_AT = 64
BIAS_AT = 74
MEAN_AT = 84
WG = 1664
HALF = (WG + 2 * QW) // 2

_cp = pltpu.CompilerParams(vmem_limit_bytes=16 * 1024 * 1024)


def dg(a, b, ca, cb):
    return lax.dot_general(a, b, (((ca,), (cb,)), ((), ())), preferred_element_type=F32)


def call(body, outs, *args, smem=(), hbm=()):
    def space(i):
        return pltpu.SMEM if i in smem else pltpu.HBM if i in hbm else pltpu.VMEM

    scratch = [pltpu.VMEM(args[i].shape, args[i].dtype) for i in hbm]
    if hbm:
        scratch.append(pltpu.SemaphoreType.DMA((len(hbm),)))
    return pl.pallas_call(
        body,
        out_shape=tuple(jax.ShapeDtypeStruct(s, d) for s, d in outs),
        in_specs=[pl.BlockSpec(memory_space=space(i)) for i in range(len(args))],
        out_specs=tuple(pl.BlockSpec(memory_space=pltpu.VMEM) for _ in outs),
        scratch_shapes=scratch,
        compiler_params=_cp,
    )(*args)


def fetch(sems, *pairs):
    copies = [pltpu.make_async_copy(a, b, sems.at[i]) for i, (a, b) in enumerate(pairs)]
    for copy in copies:
        copy.start()
    return copies


def lane(shape):
    return lax.broadcasted_iota(jnp.int32, shape, 1)


def sub(shape):
    return lax.broadcasted_iota(jnp.int32, shape, 0)


def one_hot(cond):
    return cond.astype(F32).astype(BF)


def pair_picks(send_ref):
    spread = one_hot(lane((R, 2 * R)) // 2 == sub((R, 2 * R)))
    rows = jnp.broadcast_to(send_ref[...], (8, R)).astype(F32).astype(BF)
    target = dg(rows, spread, 1, 0)[0:1].astype(jnp.int32)
    hit = sub((R, 2 * R)) == target
    odd = lane((R, 2 * R)) % 2
    return one_hot(hit & (odd == 0)), one_hot(hit & (odd == 1))


def gather_body(send_ref, x_ref, g_ref, o_ref, x_buf, g_buf, sems):
    copies = fetch(sems, (x_ref, x_buf), (g_ref, g_buf))
    even, odd = pair_picks(send_ref)
    copies[0].wait()
    rows = dg(even, x_buf[...], 0, 0)
    copies[1].wait()
    rows = rows + dg(odd, g_buf[...], 0, 0)
    o_ref[...] = rows.astype(BF).reshape(R, 2, D)


def norm_stats(x):
    mean = jnp.mean(x, axis=1, keepdims=True)
    centred = x - mean
    inv = lax.rsqrt(jnp.mean(centred * centred, axis=1, keepdims=True) + EPS)
    return mean, inv, centred * inv


def block_body(
    bits_ref, xg_ref, recv_ref, seg_ref, gain_ref, bias_ref, wq_ref, wo_ref, sel_ref, place_ref,
    pn_ref, send_ref, normed_ref, g_out_ref, qg_ref, ho_ref, stat_ref, xq_ref, gq_ref, gainq_ref,
    wq_buf, wo_buf, sel_buf, place_buf, sems,
):
    copies = fetch(
        sems, (wq_ref, wq_buf), (wo_ref, wo_buf), (sel_ref, sel_buf), (place_ref, place_buf)
    )
    xg = xg_ref[...].reshape(2 * R, D)
    at = lane((R, 2 * R)) - 2 * sub((R, 2 * R))
    x = dg(one_hot(at == 0), xg, 1, 0)
    g32 = dg(one_hot(at == 1), xg, 1, 0)
    g = g32.astype(BF)
    g_out_ref[...] = g
    mean, inv, xh = norm_stats(x)
    stat_ref[...] = jnp.where(lane((R, R)) < 64, mean, inv)
    normed = (xh * gain_ref[...] + bias_ref[...]).astype(BF)
    normed_ref[...] = normed
    for i in range(4):

        @pl.when(bits_ref[3] == i)
        def _(i=i):
            cols = slice(i * QW, (i + 1) * QW)
            xq_ref[...] = x[:, cols]
            gq_ref[...] = g32[:, cols]
            gainq_ref[...] = gain_ref[:, cols]

    copies[0].wait()
    copies[1].wait()
    wq_ref, wo_ref, sel_ref, place_ref = wq_buf, wo_buf, sel_buf, place_buf
    qkv = dg(wq_ref[...], normed, 1, 1).astype(BF)
    dh = dg(wo_ref[...], g, 1, 1).astype(BF)
    place = sub((R, R)) == recv_ref[...]
    seg = jnp.sum(jnp.where(place, seg_ref[...], 0), axis=1, keepdims=True)
    group = (seg == lane((R, R))).astype(F32).astype(BF)
    same = dg(group, group, 1, 1) > 0.5
    outs, parts = [], []
    for h in range(HG):
        q = qkv[h * 3 * HD : h * 3 * HD + HD]
        k = qkv[h * 3 * HD + HD : h * 3 * HD + 2 * HD]
        v = qkv[h * 3 * HD + 2 * HD : (h + 1) * 3 * HD]
        dhh = dh[h * HD : (h + 1) * HD]
        s = jnp.where(same, dg(q, k, 0, 0) * (HD**-0.5), -1e30)
        e = jnp.exp(s - jnp.max(s, axis=1, keepdims=True))
        w = e / jnp.sum(e, axis=1, keepdims=True)
        w16 = w.astype(BF)
        outs.append(dg(v, w16, 1, 1).astype(BF))
        pg = dg(dhh, v, 0, 0)
        delta = jnp.sum(pg * w, axis=1, keepdims=True)
        sg = (w * (pg - delta) * (HD**-0.5)).astype(BF)
        parts.append(dg(k, sg, 1, 1).astype(BF))
        parts.append(dg(q, sg, 1, 0).astype(BF))
        parts.append(dg(dhh, w16, 1, 0).astype(BF))
    ho = jnp.concatenate(outs, axis=0)
    ho_ref[...] = ho
    qg = jnp.concatenate(parts, axis=0)
    qg_ref[...] = qg
    other = 1 - bits_ref[0]
    a = qg_ref[pl.ds(pl.multiple_of(other * 3 * HD, 3 * HD), 3 * HD), :]
    b = ho_ref[pl.ds(pl.multiple_of(other * HD, HD), HD), :]
    send_ref[: 3 * HD, :] = dg(a, normed, 1, 0).astype(BF)
    send_ref[3 * HD :, :] = dg(b, g, 1, 0).astype(BF)
    p = dg(ho, wo_ref[...], 0, 0)
    n = dg(qg, wq_ref[...], 0, 0)
    u = n * gain_ref[...]
    m1 = jnp.sum(u, axis=1, keepdims=True) * (1.0 / D)
    m2 = jnp.sum(u * xh, axis=1, keepdims=True) * (1.0 / D)
    gain_row = jnp.sum(n * xh, axis=0, keepdims=True)
    bias_row = jnp.sum(n, axis=0, keepdims=True)
    copies[2].wait()
    copies[3].wait()
    sel = sel_ref[...].astype(F32)
    extra = dg((sel * gain_row).astype(BF), place_ref[0], 1, 0)
    extra = extra + dg((sel * bias_row).astype(BF), place_ref[1], 1, 0)
    ln = lane((R, R))
    for j, m in enumerate((m1, m2)):
        hi = m.astype(BF).astype(F32)
        extra = jnp.where(ln == MEAN_AT + 2 * j, hi, extra)
        extra = jnp.where(ln == MEAN_AT + 2 * j + 1, m - hi, extra)
    pad = jnp.zeros((R, QP - QW), F32)
    for i in range(4):
        part = jnp.concatenate([p[:, i * QW : (i + 1) * QW], pad], axis=1)
        pn_ref[i, :, :QP] = part.astype(BF)
        part = jnp.concatenate([n[:, i * QW : (i + 1) * QW], extra[:, 64:]], axis=1)
        pn_ref[i, :, QP:] = part.astype(BF)


def own_rows(c, part, normed, g, qg_ref, ho_ref):
    first, choose_out = part
    a = qg_ref[pl.ds(pl.multiple_of((c * 3 + first) * HD, HD), HD), :]
    if choose_out is None:
        return dg(a, normed, 1, 0)
    b = ho_ref[pl.ds(pl.multiple_of(c * HD, HD), HD), :]
    pick = choose_out.astype(F32)
    left = jnp.concatenate([a.astype(F32) * (1.0 - pick), b.astype(F32) * pick], axis=1).astype(BF)
    return dg(left, jnp.concatenate([normed, g], axis=0), 1, 0)


def part_rows(ref, j):
    return ref[pl.ds(pl.multiple_of(j * HD, HD), HD), :].astype(F32)


def pair_body(bits_ref, normed_ref, g_ref, qg_ref, ho_ref, got_ref, sz_ref, sy_ref, got, sems):
    copies = fetch(sems, (got_ref, got))
    c, z, y = bits_ref[0], bits_ref[1], bits_ref[2]
    normed, g = normed_ref[...], g_ref[...]
    a = own_rows(c, (1 - z, None), normed, g, qg_ref, ho_ref)
    b = own_rows(c, (2, 1 - y), normed, g, qg_ref, ho_ref)
    copies[0].wait()
    sz_ref[...] = (a + part_rows(got, 1 - z)).astype(BF)
    sy_ref[...] = (b + part_rows(got, 3 - y)).astype(BF)


def post_body(
    bits_ref, pn_ref, x_ref, g_ref, stat_ref, gain_ref,
    normed_ref, gall_ref, qg_ref, ho_ref, order_ref, got_ref, gz_ref, gy_ref,
    o_ref,
    got, gz, gy, sems,
):
    copies = fetch(sems, (got_ref, got), (gz_ref, gz), (gy_ref, gy))
    c, z, y = bits_ref[0], bits_ref[1], bits_ref[2]
    normed, gall = normed_ref[...], gall_ref[...]
    own_a = own_rows(c, (z, None), normed, gall, qg_ref, ho_ref)
    own_b = own_rows(c, (2, y), normed, gall, qg_ref, ho_ref)
    pn = jnp.sum(pn_ref[...].astype(F32), axis=0)
    ps = pn[:, :QW]
    ns = pn[:, QP : QP + QW]
    x = x_ref[...]
    mean = stat_ref[:, 0:1]
    inv = stat_ref[:, 64:65]
    xh = (x - mean) * inv
    tile = pn[:, QP + 256 :]
    ln = lane((R, R))
    m1 = jnp.sum(jnp.where((ln == MEAN_AT) | (ln == MEAN_AT + 1), tile, 0.0), axis=1, keepdims=True)
    m2 = jnp.sum(
        jnp.where((ln == MEAN_AT + 2) | (ln == MEAN_AT + 3), tile, 0.0), axis=1, keepdims=True
    )
    enc = x + ps
    grad = g_ref[...] + inv * (ns * gain_ref[...] - m1 - xh * m2)
    for copy in copies:
        copy.wait()
    wg = jnp.concatenate(
        [
            own_a + part_rows(got, z) + gz[...].astype(F32),
            own_b + part_rows(got, 2 + y) + gy[...].astype(F32),
        ],
        axis=0,
    ).astype(BF)
    wg = dg(order_ref[...], wg, 1, 1)
    slabs = [wg[i * R : (i + 1) * R] for i in range(10)]
    row = jnp.concatenate(slabs + [tile[:, 64:], enc, grad], axis=1).astype(BF)
    at = sub((2 * R, R)) - 2 * lane((2 * R, R))
    both = dg(one_hot(at == 0), row[:, :HALF], 1, 0) + dg(one_hot(at == 1), row[:, HALF:], 1, 0)
    o_ref[...] = both.astype(BF).reshape(R, 2, HALF)


def final_body(send_ref, b_ref, e_ref, i_ref, a_ref, w_ref, gain_ref, bias_ref):
    _, odd = pair_picks(send_ref)
    back = b_ref[...].reshape(2 * R, HALF)
    rows = dg(back[:, WG - HALF :], odd, 0, 1).astype(BF)
    e_ref[...] = rows[:QW]
    i_ref[...] = rows[QW:]
    row = sub((16, 2 * R))
    src = lane((16, 2 * R)) // 2
    half = (row // 2) % 2
    c_ok = src % 2 == row % 2
    z_ok = (src // 2) % 2 == half
    y_ok = (src // 16) % 2 == half
    mask = ((row < 4) & c_ok & z_ok) | ((row >= 4) & (row < 8) & c_ok & y_ok) | (row == 8)
    first = lane((16, 2 * R)) % 2 == 0
    sums = jnp.concatenate(
        [
            dg(one_hot(mask & first), back, 1, 0),
            dg(one_hot(mask & ~first), back[:, : WG - HALF], 1, 0),
        ],
        axis=1,
    )
    for i in range(10):
        at = i * 2 * HD
        a_ref[i, 0] = sums[0:2, at : at + HD]
        a_ref[i, 1] = sums[2:4, at : at + HD]
        a_ref[i, 2] = sums[4:6, at + HD : at + 2 * HD]
        w_ref[i] = sums[6:8, at + HD : at + 2 * HD]
    gain_ref[...] = sums[8:9, WG - 64 : WG - 54]
    bias_ref[...] = sums[8:9, WG - 54 : WG - 44]


_f = np.arange(D)
SEL = (_f[None, :] // 10 == np.arange(R)[:, None]).astype(np.float32)
PLACE = np.stack(
    [(_f[:, None] % 10 + at == np.arange(R)[None, :]).astype(np.float32) for at in (GAIN_AT, BIAS_AT)]
)


ORDER = np.zeros((D, D), np.float32)
ORDER[np.arange(D), (np.arange(D) % R) * 10 + np.arange(D) // R] = 1.0


def local(patches, cotangent, send_order, recv_order, segment_ids, ln_gain, ln_bias, w_qkv, w_out):
    zero = lax.axis_index("zero")
    dp = lax.axis_index("dp")
    bits = jnp.stack([dp & 1, (dp >> 1) & 1, (dp >> 4) & 1, zero])
    wq = w_qkv.transpose(1, 2, 3, 0).reshape(NQ, D)
    wo = w_out.reshape(NO, D)
    gain = ln_gain.reshape(1, D)
    bias = ln_bias.reshape(1, D)
    sel = jnp.asarray(SEL, BF)
    place = jnp.asarray(PLACE, BF)
    order = jnp.asarray(ORDER, BF)

    def swap(a, bit):
        return lax.ppermute(a, "dp", [(i, i ^ bit) for i in range(128)])

    (xg,) = call(gather_body, [((R, 2, D), BF)], send_order, patches, cotangent, hbm=(1, 2))
    xg = lax.all_to_all(xg, "dp", 0, 0, tiled=True)
    pn, send, normed, g, qg, ho, stat, xq, gq, gainq = call(
        block_body,
        [
            ((4, R, 2 * QP), BF),
            ((4 * HD, D), BF),
            ((R, D), BF),
            ((R, D), BF),
            ((NQ, R), BF),
            ((NO, R), BF),
            ((R, R), F32),
            ((R, QW), F32),
            ((R, QW), F32),
            ((1, QW), F32),
        ],
        bits, xg, recv_order, segment_ids, gain, bias, wq, wo, sel, place,
        smem=(0,),
        hbm=(6, 7, 8, 9),
    )
    got = swap(send, 1)
    pn = lax.all_to_all(pn, "zero", 0, 0, tiled=True)
    sz, sy = call(
        pair_body,
        [((HD, D), BF), ((HD, D), BF)],
        bits, normed, g, qg, ho, got,
        smem=(0,),
        hbm=(5,),
    )
    gz = swap(sz, 2)
    gy = swap(sy, 16)
    (back,) = call(
        post_body,
        [((R, 2, HALF), BF)],
        bits, pn, xq, gq, stat, gainq, normed, g, qg, ho, order, got, gz, gy,
        smem=(0,),
        hbm=(11, 12, 13),
    )
    back = lax.all_to_all(back, "dp", 0, 0, tiled=True)
    enc, grad, qkv_share, out_share, gain_grad, bias_grad = call(
        final_body,
        [
            ((QW, R), BF),
            ((QW, R), BF),
            ((10, 3, 2, HD), F32),
            ((10, 2, HD), F32),
            ((1, 10), F32),
            ((1, 10), F32),
        ],
        send_order, back,
    )
    return (
        enc.T,
        grad.T,
        qkv_share.transpose(0, 2, 1, 3),
        out_share.transpose(1, 2, 0),
        gain_grad.reshape(10),
        bias_grad.reshape(10),
    )


def solution(mesh):
    return jax.shard_map(
        local,
        mesh=mesh,
        in_specs=(
            P("dp", None),
            P("dp", None),
            P("dp", None),
            P("dp", None),
            P("dp", None),
            P(),
            P(),
            P(None, "zero", None, None),
            P("zero", None, None),
        ),
        out_specs=(
            P("dp", "zero"),
            P("dp", "zero"),
            P("dp", "zero", None, None),
            P("zero", None, "dp"),
            P("dp"),
            P("dp"),
        ),
        check_vma=False,
    )
```

```python
import jax
import jax.numpy as jnp
from jax import lax
from jax.experimental import pallas as pl
from jax.experimental.pallas import tpu as pltpu
from jax.sharding import PartitionSpec as P

EPS = 1e-06
R = 128
D = 1280
HD = 80
HG = 2
NQ = HG * 3 * HD
NO = HG * HD
QW = D // 4
QP = 384
F32 = jnp.float32
BF = jnp.bfloat16
GAIN_AT = 64
BIAS_AT = 74
MEAN_AT = 84
WG = 1664
HALF = (WG + 2 * QW) // 2

MIB = 1024 * 1024
MIB_HOLD, MIB_BLOCK, MIB_PAIR, MIB_POST = 16, 50, 50, 50


def dg(a, b, ca, cb):
    return lax.dot_general(a, b, (((ca,), (cb,)), ((), ())), preferred_element_type=F32)


def call(body, outs, *args, smem=(), hbm=(), scratch=(), mib=50):
    def space(i):
        return pltpu.SMEM if i in smem else pltpu.HBM if i in hbm else pltpu.VMEM

    scratch = list(scratch) + [pltpu.VMEM(args[i].shape, args[i].dtype) for i in hbm]
    if hbm:
        scratch.append(pltpu.SemaphoreType.DMA((len(hbm),)))
    return pl.pallas_call(
        body,
        out_shape=tuple(jax.ShapeDtypeStruct(s, d) for s, d in outs),
        in_specs=[pl.BlockSpec(memory_space=space(i)) for i in range(len(args))],
        out_specs=tuple(pl.BlockSpec(memory_space=pltpu.VMEM) for _ in outs),
        scratch_shapes=scratch,
        compiler_params=pltpu.CompilerParams(vmem_limit_bytes=mib * MIB),
    )(*args)


def fetch(sems, *pairs):
    copies = [pltpu.make_async_copy(a, b, sems.at[i]) for i, (a, b) in enumerate(pairs)]
    for copy in copies:
        copy.start()
    return copies


def lane(shape):
    return lax.broadcasted_iota(jnp.int32, shape, 1)


def sub(shape):
    return lax.broadcasted_iota(jnp.int32, shape, 0)


def one_hot(cond):
    return cond.astype(F32).astype(BF)


def pair_picks(send_ref):
    spread = one_hot(lane((R, 2 * R)) // 2 == sub((R, 2 * R)))
    rows = jnp.broadcast_to(send_ref[...], (8, R)).astype(F32).astype(BF)
    target = dg(rows, spread, 1, 0)[0:1].astype(jnp.int32)
    hit = sub((R, 2 * R)) == target
    odd = lane((R, 2 * R)) % 2
    return one_hot(hit & (odd == 0)), one_hot(hit & (odd == 1))


def gather_body(send_ref, x_ref, g_ref, o_ref, x_buf, g_buf, sems):
    copies = fetch(sems, (x_ref, x_buf), (g_ref, g_buf))
    even, odd = pair_picks(send_ref)
    copies[0].wait()
    rows = dg(even, x_buf[...], 0, 0)
    copies[1].wait()
    rows = rows + dg(odd, g_buf[...], 0, 0)
    o_ref[...] = rows.astype(BF).reshape(R, 2, D)


def norm_stats(x):
    mean = jnp.mean(x, axis=1, keepdims=True)
    centred = x - mean
    inv = lax.rsqrt(jnp.mean(centred * centred, axis=1, keepdims=True) + EPS)
    return mean, inv, centred * inv


def hold_body(
    recv_ref, seg_ref, gain_ref, bias_ref, wo_ref, same_ref, gain_out, bias_out, wo_out
):
    hit = sub((R, R)) == recv_ref[...]
    seg = jnp.sum(jnp.where(hit, seg_ref[...], 0), axis=1, keepdims=True)
    group = one_hot(seg == lane((R, R)))
    same_ref[...] = dg(group, group, 1, 1)
    gain_out[...] = gain_ref[...]
    bias_out[...] = bias_ref[...]
    wo_out[...] = wo_ref[...]


def block_body(
    bits_ref, xg_ref, same_ref, gain_ref, bias_ref, wo_ref, wq_hbm,
    pn_ref, send_ref, ng_ref, heads_ref, aux_ref,
    wq_ref, sems,
):
    copies = fetch(sems, (wq_hbm, wq_ref))
    xg = xg_ref[...].reshape(2 * R, D)
    at = lane((R, 2 * R)) - 2 * sub((R, 2 * R))
    x = dg(one_hot(at == 0), xg, 1, 0)
    g32 = dg(one_hot(at == 1), xg, 1, 0)
    g = g32.astype(BF)
    ng_ref[R:, :] = g
    mean, inv, xh = norm_stats(x)
    normed = (xh * gain_ref[...] + bias_ref[...]).astype(BF)
    ng_ref[:R, :] = normed
    for i in range(4):

        @pl.when(bits_ref[3] == i)
        def _(i=i):
            cols = slice(i * QW, (i + 1) * QW)
            tail = (R, QP - QW)
            rows = [
                x[:, cols], jnp.broadcast_to(mean, tail),
                g32[:, cols], jnp.broadcast_to(inv, tail),
                jnp.broadcast_to(gain_ref[:, cols], (R, QW)), jnp.zeros(tail, F32),
            ]
            aux_ref[...] = jnp.concatenate(rows, axis=1)

    copies[0].wait()
    qkv = dg(wq_ref[...], normed, 1, 1).astype(BF)
    dh = dg(wo_ref[...], g, 1, 1).astype(BF)
    same = same_ref[...] > 0.5
    rows = []
    for h in range(HG):
        q = qkv[h * 3 * HD : h * 3 * HD + HD]
        k = qkv[h * 3 * HD + HD : h * 3 * HD + 2 * HD]
        v = qkv[h * 3 * HD + 2 * HD : (h + 1) * 3 * HD]
        dhh = dh[h * HD : (h + 1) * HD]
        s = jnp.where(same, dg(q, k, 0, 0) * (HD**-0.5), -1e30)
        e = jnp.exp(s - jnp.max(s, axis=1, keepdims=True))
        w = e / jnp.sum(e, axis=1, keepdims=True)
        w16 = w.astype(BF)
        pg = dg(dhh, v, 0, 0)
        delta = jnp.sum(pg * w, axis=1, keepdims=True)
        sg = (w * (pg - delta) * (HD**-0.5)).astype(BF)
        rows.append(dg(k, sg, 1, 1).astype(BF))
        rows.append(dg(q, sg, 1, 0).astype(BF))
        rows.append(dg(dhh, w16, 1, 0).astype(BF))
        rows.append(dg(v, w16, 1, 1).astype(BF))
    heads_ref[...] = jnp.concatenate(rows, axis=0)
    qg = jnp.concatenate(rows[0:3] + rows[4:7], axis=0)
    ho = jnp.concatenate([rows[3], rows[7]], axis=0)
    other = (1 - bits_ref[0]) * 4 * HD
    a = heads_ref[pl.ds(pl.multiple_of(other, 4 * HD), 3 * HD), :]
    b = heads_ref[pl.ds(pl.multiple_of(other + 3 * HD, HD), HD), :]
    send_ref[: 3 * HD, :] = dg(a, normed, 1, 0).astype(BF)
    send_ref[3 * HD :, :] = dg(b, g, 1, 0).astype(BF)
    p = dg(ho, wo_ref[...], 0, 0)
    n = dg(qg, wq_ref[...], 0, 0)
    u = n * gain_ref[...]
    m1 = jnp.sum(u, axis=1, keepdims=True) * (1.0 / D)
    m2 = jnp.sum(u * xh, axis=1, keepdims=True) * (1.0 / D)
    gain_row = jnp.sum(n * xh, axis=0, keepdims=True)
    bias_row = jnp.sum(n, axis=0, keepdims=True)
    first = lane((R, D)) - 10 * sub((R, D))
    sel = (first >= 0) & (first < 10)
    both = jnp.concatenate(
        [jnp.where(sel, gain_row, 0.0).astype(BF), jnp.where(sel, bias_row, 0.0).astype(BF)], axis=0
    )
    f = sub((D, R)).astype(F32)
    k = f - 10.0 * jnp.floor((f + 0.5) * 0.1)
    both = dg(both, one_hot(k == (lane((D, R)) - GAIN_AT).astype(F32)), 1, 0)
    extra = both[:R] + pltpu.roll(both[R:], BIAS_AT - GAIN_AT, 1)
    ln = lane((R, R))
    for j, m in enumerate((m1, m2)):
        hi = m.astype(BF).astype(F32)
        extra = jnp.where(ln == MEAN_AT + 2 * j, hi, extra)
        extra = jnp.where(ln == MEAN_AT + 2 * j + 1, m - hi, extra)
    pad = jnp.zeros((R, QP - QW), F32)
    for i in range(4):
        part = jnp.concatenate([p[:, i * QW : (i + 1) * QW], pad], axis=1)
        pn_ref[i, :, :QP] = part.astype(BF)
        part = jnp.concatenate([n[:, i * QW : (i + 1) * QW], extra[:, 64:]], axis=1)
        pn_ref[i, :, QP:] = part.astype(BF)


def own_rows(c, first, choose_out, ng_ref, heads_ref):
    a = heads_ref[pl.ds(pl.multiple_of((c * 4 + first) * HD, HD), HD), :]
    if choose_out is None:
        return dg(a, ng_ref[:R, :], 1, 0)
    b = heads_ref[pl.ds(pl.multiple_of((c * 4 + 3) * HD, HD), HD), :]
    pick = choose_out.astype(F32)
    left = jnp.concatenate([a.astype(F32) * (1.0 - pick), b.astype(F32) * pick], axis=1).astype(BF)
    return dg(left, ng_ref[...], 1, 0)


def part_rows(ref, j):
    return ref[pl.ds(pl.multiple_of(j * HD, HD), HD), :].astype(F32)


def pair_body(bits_ref, ng_ref, heads_ref, got_ref, sz_ref, sy_ref):
    c, z, y = bits_ref[0], bits_ref[1], bits_ref[2]
    a = own_rows(c, 1 - z, None, ng_ref, heads_ref)
    b = own_rows(c, 2, 1 - y, ng_ref, heads_ref)
    sz_ref[...] = (a + part_rows(got_ref, 1 - z)).astype(BF)
    sy_ref[...] = (b + part_rows(got_ref, 3 - y)).astype(BF)


def post_body(
    bits_ref, pn_ref, aux_ref, ng_ref, heads_ref, got_ref, gz_ref, gy_ref, o_ref, wz_ref, wy_ref
):
    c, z, y = bits_ref[0], bits_ref[1], bits_ref[2]
    wz = own_rows(c, z, None, ng_ref, heads_ref) + part_rows(got_ref, z)
    wz_ref[:, :HD] = (wz + gz_ref[...].astype(F32)).T
    wy = own_rows(c, 2, y, ng_ref, heads_ref) + part_rows(got_ref, 2 + y)
    wy_ref[:, :HD] = (wy + gy_ref[...].astype(F32)).T
    slabs = []
    for i in range(10):
        for ref in (wz_ref, wy_ref):
            slabs.append(ref[pl.ds(i, R, stride=10), :][:, :HD])
    pn = jnp.sum(pn_ref[...].astype(F32), axis=0)
    ps = pn[:, :QW]
    ns = pn[:, QP : QP + QW]
    x = aux_ref[:, :QW]
    mean = aux_ref[:, QW : QW + 1]
    inv = aux_ref[:, QP + QW : QP + QW + 1]
    xh = (x - mean) * inv
    tile = pn[:, QP + 256 :]
    ln = lane((R, R))
    m1 = jnp.sum(jnp.where((ln == MEAN_AT) | (ln == MEAN_AT + 1), tile, 0.0), axis=1, keepdims=True)
    m2 = jnp.sum(
        jnp.where((ln == MEAN_AT + 2) | (ln == MEAN_AT + 3), tile, 0.0), axis=1, keepdims=True
    )
    enc = x + ps
    grad = aux_ref[:, QP : QP + QW] + inv * (ns * aux_ref[:, 2 * QP : 2 * QP + QW] - m1 - xh * m2)
    row = jnp.concatenate(slabs + [tile[:, 64:], enc, grad], axis=1).astype(BF)
    at = sub((2 * R, R)) - 2 * lane((2 * R, R))
    both = dg(one_hot(at == 0), row[:, :HALF], 1, 0) + dg(one_hot(at == 1), row[:, HALF:], 1, 0)
    o_ref[...] = both.astype(BF).reshape(R, 2, HALF)


def final_body(send_ref, b_ref, e_ref, i_ref, a_ref, w_ref, gain_ref, bias_ref):
    _, odd = pair_picks(send_ref)
    back = b_ref[...].reshape(2 * R, HALF)
    rows = dg(back[:, WG - HALF :], odd, 0, 1).astype(BF)
    e_ref[...] = rows[:QW]
    i_ref[...] = rows[QW:]
    row = sub((16, 2 * R))
    src = lane((16, 2 * R)) // 2
    half = (row // 2) % 2
    c_ok = src % 2 == row % 2
    z_ok = (src // 2) % 2 == half
    y_ok = (src // 16) % 2 == half
    mask = ((row < 4) & c_ok & z_ok) | ((row >= 4) & (row < 8) & c_ok & y_ok) | (row == 8)
    first = lane((16, 2 * R)) % 2 == 0
    sums = jnp.concatenate(
        [
            dg(one_hot(mask & first), back, 1, 0),
            dg(one_hot(mask & ~first), back[:, : WG - HALF], 1, 0),
        ],
        axis=1,
    )
    for i in range(10):
        at = i * 2 * HD
        a_ref[i, 0] = sums[0:2, at : at + HD]
        a_ref[i, 1] = sums[2:4, at : at + HD]
        a_ref[i, 2] = sums[4:6, at + HD : at + 2 * HD]
        w_ref[i] = sums[6:8, at + HD : at + 2 * HD]
    gain_ref[...] = sums[8:9, WG - 64 : WG - 54]
    bias_ref[...] = sums[8:9, WG - 54 : WG - 44]


def local(patches, cotangent, send_order, recv_order, segment_ids, ln_gain, ln_bias, w_qkv, w_out):
    zero = lax.axis_index("zero")
    dp = lax.axis_index("dp")
    bits = jnp.stack([dp & 1, (dp >> 1) & 1, (dp >> 4) & 1, zero])
    wq = w_qkv.transpose(1, 2, 3, 0).reshape(NQ, D)
    wo = w_out.reshape(NO, D)
    gain = ln_gain.reshape(1, D)
    bias = ln_bias.reshape(1, D)

    def swap(a, bit):
        return lax.ppermute(a, "dp", [(i, i ^ bit) for i in range(128)])

    (xg,) = call(gather_body, [((R, 2, D), BF)], send_order, patches, cotangent, hbm=(1, 2), mib=58)
    same, gain, bias, wo = call(
        hold_body,
        [((R, R), F32), ((1, D), F32), ((1, D), F32), ((NO, D), BF)],
        recv_order, segment_ids, gain, bias, wo,
        mib=MIB_HOLD,
    )
    xg = lax.all_to_all(xg, "dp", 0, 0, tiled=True)
    pn, send, ng, heads, aux = call(
        block_body,
        [
            ((4, R, 2 * QP), BF),
            ((4 * HD, D), BF),
            ((2 * R, D), BF),
            ((8 * HD, R), BF),
            ((R, 3 * QP), F32),
        ],
        bits, xg, same, gain, bias, wo, wq,
        smem=(0,),
        hbm=(6,),
        mib=MIB_BLOCK,
    )
    got = swap(send, 1)
    pn = lax.all_to_all(pn, "zero", 0, 0, tiled=True)
    sz, sy = call(
        pair_body,
        [((HD, D), BF), ((HD, D), BF)],
        bits, ng, heads, got,
        smem=(0,),
        mib=MIB_PAIR,
    )
    gz = swap(sz, 2)
    gy = swap(sy, 16)
    (back,) = call(
        post_body,
        [((R, 2, HALF), BF)],
        bits, pn, aux, ng, heads, got, gz, gy,
        smem=(0,),
        scratch=[pltpu.VMEM((D, R), F32)] * 2,
        mib=MIB_POST,
    )
    back = lax.all_to_all(back, "dp", 0, 0, tiled=True)
    enc, grad, qkv_share, out_share, gain_grad, bias_grad = call(
        final_body,
        [
            ((QW, R), BF),
            ((QW, R), BF),
            ((10, 3, 2, HD), F32),
            ((10, 2, HD), F32),
            ((1, 10), F32),
            ((1, 10), F32),
        ],
        send_order, back,
    )
    return (
        enc.T,
        grad.T,
        qkv_share.transpose(0, 2, 1, 3),
        out_share.transpose(1, 2, 0),
        gain_grad.reshape(10),
        bias_grad.reshape(10),
    )


def solution(mesh):
    return jax.shard_map(
        local,
        mesh=mesh,
        in_specs=(
            P("dp", None),
            P("dp", None),
            P("dp", None),
            P("dp", None),
            P("dp", None),
            P(),
            P(),
            P(None, "zero", None, None),
            P("zero", None, None),
        ),
        out_specs=(
            P("dp", "zero"),
            P("dp", "zero"),
            P("dp", "zero", None, None),
            P("zero", None, "dp"),
            P("dp"),
            P("dp"),
        ),
        check_vma=False,
    )
```

```python
import jax
import jax.numpy as jnp
from jax import lax
from jax.experimental import pallas as pl
from jax.experimental.pallas import tpu as pltpu
from jax.sharding import PartitionSpec as P

EPS = 1e-06
R = 128
D = 1280
HD = 80
HG = 2
NQ = HG * 3 * HD
NO = HG * HD
QW = D // 4
QP = 384
F32 = jnp.float32
BF = jnp.bfloat16
GAIN_AT = 64
BIAS_AT = 74
MEAN_AT = 84
WG = 896
HALF = (WG + 2 * QW) // 2

MIB = 1024 * 1024
GATHER_PARTS = 2
MIB_HOLD, MIB_BLOCK, MIB_PAIR, MIB_POST = 16, 50, 50, 50


def dg(a, b, ca, cb):
    return lax.dot_general(a, b, (((ca,), (cb,)), ((), ())), preferred_element_type=F32)


def call(body, outs, *args, smem=(), hbm=(), out_hbm=(), scratch=(), mib=50):
    def space(i):
        return pltpu.SMEM if i in smem else pltpu.HBM if i in hbm else pltpu.VMEM

    scratch = list(scratch) + [pltpu.VMEM(args[i].shape, args[i].dtype) for i in hbm]
    scratch += [pltpu.VMEM(*outs[i]) for i in out_hbm]
    if hbm or out_hbm:
        scratch.append(pltpu.SemaphoreType.DMA((8,)))
    return pl.pallas_call(
        body,
        out_shape=tuple(jax.ShapeDtypeStruct(s, d) for s, d in outs),
        in_specs=[pl.BlockSpec(memory_space=space(i)) for i in range(len(args))],
        out_specs=tuple(
            pl.BlockSpec(memory_space=pltpu.HBM if i in out_hbm else pltpu.VMEM)
            for i in range(len(outs))
        ),
        scratch_shapes=scratch,
        compiler_params=pltpu.CompilerParams(vmem_limit_bytes=mib * MIB),
    )(*args)


def start(sem, a, b):
    copy = pltpu.make_async_copy(a, b, sem)
    copy.start()
    return copy


def lane(shape):
    return lax.broadcasted_iota(jnp.int32, shape, 1)


def sub(shape):
    return lax.broadcasted_iota(jnp.int32, shape, 0)


def one_hot(cond):
    return cond.astype(F32).astype(BF)


def pair_picks(send_ref):
    spread = one_hot(lane((R, 2 * R)) // 2 == sub((R, 2 * R)))
    rows = jnp.broadcast_to(send_ref[...], (8, R)).astype(F32).astype(BF)
    target = dg(rows, spread, 1, 0)[0:1].astype(jnp.int32)
    hit = sub((R, 2 * R)) == target
    odd = lane((R, 2 * R)) % 2
    return one_hot(hit & (odd == 0)), one_hot(hit & (odd == 1))


def gather_body(send_ref, x_hbm, g_hbm, o_hbm, x_ref, g_ref, o_ref, sems):
    copies = [start(sems.at[0], x_hbm, x_ref), start(sems.at[1], g_hbm, g_ref)]
    even, odd = pair_picks(send_ref)
    for copy in copies:
        copy.wait()
    copies = []
    step = R // GATHER_PARTS
    for i in range(GATHER_PARTS):
        rows = slice(2 * step * i, 2 * step * (i + 1))
        part = dg(even[:, rows], x_ref[...], 0, 0) + dg(odd[:, rows], g_ref[...], 0, 0)
        at = pl.ds(step * i, step)
        o_ref[at] = part.astype(BF).reshape(step, 2, D)
        copies.append(start(sems.at[2 + i], o_ref.at[at], o_hbm.at[at]))
    for copy in copies:
        copy.wait()


def norm_stats(x):
    mean = jnp.mean(x, axis=1, keepdims=True)
    centred = x - mean
    inv = lax.rsqrt(jnp.mean(centred * centred, axis=1, keepdims=True) + EPS)
    return mean, inv, centred * inv


def hold_body(
    recv_ref, seg_ref, gain_ref, bias_ref, wo_ref, same_ref, gain_out, bias_out, wo_out
):
    hit = sub((R, R)) == recv_ref[...]
    seg = jnp.sum(jnp.where(hit, seg_ref[...], 0), axis=1, keepdims=True)
    group = one_hot(seg == lane((R, R)))
    same_ref[...] = dg(group, group, 1, 1)
    gain_out[...] = gain_ref[...]
    bias_out[...] = bias_ref[...]
    wo_out[...] = wo_ref[...]


def block_body(
    bits_ref, xg_ref, same_ref, gain_ref, bias_ref, wo_ref, wq_hbm,
    pn_hbm, send_hbm, ng_ref, heads_ref, aux_ref,
    wq_ref, pn_ref, send_ref, sems,
):
    copies = [start(sems.at[0], wq_hbm, wq_ref)]
    xg = xg_ref[...].reshape(2 * R, D)
    at = lane((R, 2 * R)) - 2 * sub((R, 2 * R))
    x = dg(one_hot(at == 0), xg, 1, 0)
    g32 = dg(one_hot(at == 1), xg, 1, 0)
    g = g32.astype(BF)
    ng_ref[R:, :] = g
    mean, inv, xh = norm_stats(x)
    normed = (xh * gain_ref[...] + bias_ref[...]).astype(BF)
    ng_ref[:R, :] = normed
    for i in range(4):

        @pl.when(bits_ref[3] == i)
        def _(i=i):
            cols = slice(i * QW, (i + 1) * QW)
            tail = (R, QP - QW)
            rows = [
                x[:, cols], jnp.broadcast_to(mean, tail),
                g32[:, cols], jnp.broadcast_to(inv, tail),
                jnp.broadcast_to(gain_ref[:, cols], (R, QW)), jnp.zeros(tail, F32),
            ]
            aux_ref[...] = jnp.concatenate(rows, axis=1)

    copies[0].wait()
    qkv = dg(wq_ref[...], normed, 1, 1).astype(BF)
    dh = dg(wo_ref[...], g, 1, 1).astype(BF)
    same = same_ref[...] > 0.5
    rows = []
    for h in range(HG):
        q = qkv[h * 3 * HD : h * 3 * HD + HD]
        k = qkv[h * 3 * HD + HD : h * 3 * HD + 2 * HD]
        v = qkv[h * 3 * HD + 2 * HD : (h + 1) * 3 * HD]
        dhh = dh[h * HD : (h + 1) * HD]
        s = jnp.where(same, dg(q, k, 0, 0) * (HD**-0.5), -1e30)
        e = jnp.exp(s - jnp.max(s, axis=1, keepdims=True))
        w = e / jnp.sum(e, axis=1, keepdims=True)
        w16 = w.astype(BF)
        pg = dg(dhh, v, 0, 0)
        delta = jnp.sum(pg * w, axis=1, keepdims=True)
        sg = (w * (pg - delta) * (HD**-0.5)).astype(BF)
        rows.append(dg(k, sg, 1, 1).astype(BF))
        rows.append(dg(q, sg, 1, 0).astype(BF))
        rows.append(dg(dhh, w16, 1, 0).astype(BF))
        rows.append(dg(v, w16, 1, 1).astype(BF))
    heads_ref[...] = jnp.concatenate(rows, axis=0)
    qg = jnp.concatenate(rows[0:3] + rows[4:7], axis=0)
    ho = jnp.concatenate([rows[3], rows[7]], axis=0)
    other = (1 - bits_ref[0]) * 4 * HD
    a = heads_ref[pl.ds(pl.multiple_of(other, 4 * HD), 3 * HD), :]
    b = heads_ref[pl.ds(pl.multiple_of(other + 3 * HD, HD), HD), :]
    send_ref[: 3 * HD, :] = dg(a, normed, 1, 0).astype(BF)
    send_ref[3 * HD :, :] = dg(b, g, 1, 0).astype(BF)
    copies[0] = start(sems.at[1], send_ref, send_hbm)
    p = dg(ho, wo_ref[...], 0, 0)
    n = dg(qg, wq_ref[...], 0, 0)
    u = n * gain_ref[...]
    m1 = jnp.sum(u, axis=1, keepdims=True) * (1.0 / D)
    m2 = jnp.sum(u * xh, axis=1, keepdims=True) * (1.0 / D)
    gain_row = jnp.sum(n * xh, axis=0, keepdims=True)
    bias_row = jnp.sum(n, axis=0, keepdims=True)
    first = lane((R, D)) - 10 * sub((R, D))
    sel = (first >= 0) & (first < 10)
    both = jnp.concatenate(
        [jnp.where(sel, gain_row, 0.0).astype(BF), jnp.where(sel, bias_row, 0.0).astype(BF)], axis=0
    )
    f = sub((D, R)).astype(F32)
    k = f - 10.0 * jnp.floor((f + 0.5) * 0.1)
    both = dg(both, one_hot(k == (lane((D, R)) - GAIN_AT).astype(F32)), 1, 0)
    extra = both[:R] + pltpu.roll(both[R:], BIAS_AT - GAIN_AT, 1)
    ln = lane((R, R))
    for j, m in enumerate((m1, m2)):
        hi = m.astype(BF).astype(F32)
        extra = jnp.where(ln == MEAN_AT + 2 * j, hi, extra)
        extra = jnp.where(ln == MEAN_AT + 2 * j + 1, m - hi, extra)
    pad = jnp.zeros((R, QP - QW), F32)
    for i in range(4):
        part = jnp.concatenate([p[:, i * QW : (i + 1) * QW], pad], axis=1)
        pn_ref[i, :, :QP] = part.astype(BF)
        part = jnp.concatenate([n[:, i * QW : (i + 1) * QW], extra[:, 64:]], axis=1)
        pn_ref[i, :, QP:] = part.astype(BF)
        copies.append(start(sems.at[2 + i], pn_ref.at[i], pn_hbm.at[i]))
    for copy in copies:
        copy.wait()


def own_rows(c, first, choose_out, ng_ref, heads_ref):
    a = heads_ref[pl.ds(pl.multiple_of((c * 4 + first) * HD, HD), HD), :]
    if choose_out is None:
        return dg(a, ng_ref[:R, :], 1, 0)
    b = heads_ref[pl.ds(pl.multiple_of((c * 4 + 3) * HD, HD), HD), :]
    pick = choose_out.astype(F32)
    left = jnp.concatenate([a.astype(F32) * (1.0 - pick), b.astype(F32) * pick], axis=1).astype(BF)
    return dg(left, ng_ref[...], 1, 0)


def part_rows(ref, j):
    return ref[pl.ds(pl.multiple_of(j * HD, HD), HD), :].astype(F32)


def pair_body(bits_ref, ng_ref, heads_ref, got_ref, sz_ref, sy_ref):
    c, z, y = bits_ref[0], bits_ref[1], bits_ref[2]
    a = own_rows(c, 1 - z, None, ng_ref, heads_ref)
    b = own_rows(c, 2, 1 - y, ng_ref, heads_ref)
    sz_ref[...] = (a + part_rows(got_ref, 1 - z)).astype(BF)
    sy_ref[...] = (b + part_rows(got_ref, 3 - y)).astype(BF)


def second_body(
    bits_ref, ng_ref, heads_ref, got_ref, gz_ref, gy_ref, keep_ref, sy_ref, sz_ref
):
    c, z, y = bits_ref[0], bits_ref[1], bits_ref[2]
    wz = own_rows(c, z, None, ng_ref, heads_ref) + part_rows(got_ref, z)
    wz = wz + gz_ref[...].astype(F32)
    wy = own_rows(c, 2, y, ng_ref, heads_ref) + part_rows(got_ref, 2 + y)
    wy = wy + gy_ref[...].astype(F32)
    low, high = slice(0, HD // 2), slice(HD // 2, HD)
    keep_ref[low] = jnp.where(y == 0, wz[low], wz[high])
    keep_ref[high] = jnp.where(z == 0, wy[low], wy[high])
    sy_ref[...] = jnp.where(y == 0, wz[high], wz[low]).astype(BF)
    sz_ref[...] = jnp.where(z == 0, wy[high], wy[low]).astype(BF)


def post_body(pn_ref, aux_ref, keep_ref, gy_ref, gz_ref, o_ref, w_ref):
    got = jnp.concatenate([gy_ref[...].astype(F32), gz_ref[...].astype(F32)], axis=0)
    w_ref[:, :HD] = (keep_ref[...] + got).T
    slabs = [w_ref[pl.ds(i, R, stride=10), :][:, :HD] for i in range(10)]
    slabs.append(jnp.zeros((R, WG - 64 - 10 * HD), F32))
    pn = jnp.sum(pn_ref[...].astype(F32), axis=0)
    ps = pn[:, :QW]
    ns = pn[:, QP : QP + QW]
    x = aux_ref[:, :QW]
    mean = aux_ref[:, QW : QW + 1]
    inv = aux_ref[:, QP + QW : QP + QW + 1]
    xh = (x - mean) * inv
    tile = pn[:, QP + 256 :]
    ln = lane((R, R))
    m1 = jnp.sum(jnp.where((ln == MEAN_AT) | (ln == MEAN_AT + 1), tile, 0.0), axis=1, keepdims=True)
    m2 = jnp.sum(
        jnp.where((ln == MEAN_AT + 2) | (ln == MEAN_AT + 3), tile, 0.0), axis=1, keepdims=True
    )
    enc = x + ps
    grad = aux_ref[:, QP : QP + QW] + inv * (ns * aux_ref[:, 2 * QP : 2 * QP + QW] - m1 - xh * m2)
    row = jnp.concatenate(slabs + [tile[:, 64:], enc, grad], axis=1).astype(BF)
    at = sub((2 * R, R)) - 2 * lane((2 * R, R))
    both = dg(one_hot(at == 0), row[:, :HALF], 1, 0) + dg(one_hot(at == 1), row[:, HALF:], 1, 0)
    o_ref[...] = both.astype(BF).reshape(R, 2, HALF)


def final_body(send_ref, b_ref, e_ref, i_ref, a_ref, w_ref, gain_ref, bias_ref):
    _, odd = pair_picks(send_ref)
    back = b_ref[...].reshape(2 * R, HALF)
    rows = dg(back[:, WG - HALF :], odd, 0, 1).astype(BF)
    e_ref[...] = rows[:QW]
    i_ref[...] = rows[QW:]
    row = sub((16, 2 * R))
    src = lane((16, 2 * R)) // 2
    bits = ((src // 2) % 2) * 4 + ((src // 16) % 2) * 2 + src % 2
    mask = (row == bits) | (row == 8)
    first = lane((16, 2 * R)) % 2 == 0
    sums = jnp.concatenate(
        [
            dg(one_hot(mask & first), back, 1, 0),
            dg(one_hot(mask & ~first), back[:, : WG - HALF], 1, 0),
        ],
        axis=1,
    )
    for i in range(10):
        a = sums[:, i * HD : i * HD + HD // 2]
        b = sums[:, i * HD + HD // 2 : (i + 1) * HD]
        a_ref[i, 0] = jnp.concatenate([a[0:2], a[2:4]], axis=1)
        a_ref[i, 1] = jnp.concatenate([a[4:6], a[6:8]], axis=1)
        a_ref[i, 2] = jnp.concatenate([b[0:2], b[4:6]], axis=1)
        w_ref[i] = jnp.concatenate([b[2:4], b[6:8]], axis=1)
    gain_ref[...] = sums[8:9, WG - 64 : WG - 54]
    bias_ref[...] = sums[8:9, WG - 54 : WG - 44]


def local(patches, cotangent, send_order, recv_order, segment_ids, ln_gain, ln_bias, w_qkv, w_out):
    zero = lax.axis_index("zero")
    dp = lax.axis_index("dp")
    bits = jnp.stack([dp & 1, (dp >> 1) & 1, (dp >> 4) & 1, zero])
    wq = w_qkv.transpose(1, 2, 3, 0).reshape(NQ, D)
    wo = w_out.reshape(NO, D)
    gain = ln_gain.reshape(1, D)
    bias = ln_bias.reshape(1, D)

    def swap(a, bit):
        return lax.ppermute(a, "dp", [(i, i ^ bit) for i in range(128)])

    (xg,) = call(gather_body, [((R, 2, D), BF)], send_order, patches, cotangent, hbm=(1, 2), out_hbm=(0,), mib=58)
    same, gain, bias, wo = call(
        hold_body,
        [((R, R), F32), ((1, D), F32), ((1, D), F32), ((NO, D), BF)],
        recv_order, segment_ids, gain, bias, wo,
        mib=MIB_HOLD,
    )
    xg = lax.all_to_all(xg, "dp", 0, 0, tiled=True)
    pn, send, ng, heads, aux = call(
        block_body,
        [
            ((4, R, 2 * QP), BF),
            ((4 * HD, D), BF),
            ((2 * R, D), BF),
            ((8 * HD, R), BF),
            ((R, 3 * QP), F32),
        ],
        bits, xg, same, gain, bias, wo, wq,
        smem=(0,),
        hbm=(6,),
        out_hbm=(0, 1),
        mib=MIB_BLOCK,
    )
    got = swap(send, 1)
    pn = lax.all_to_all(pn, "zero", 0, 0, tiled=True)
    sz, sy = call(
        pair_body,
        [((HD, D), BF), ((HD, D), BF)],
        bits, ng, heads, got,
        smem=(0,),
        mib=MIB_PAIR,
    )
    gz = swap(sz, 2)
    gy = swap(sy, 16)
    keep, sy, sz = call(
        second_body,
        [((HD, D), F32), ((HD // 2, D), BF), ((HD // 2, D), BF)],
        bits, ng, heads, got, gz, gy,
        smem=(0,),
        mib=MIB_PAIR,
    )
    (back,) = call(
        post_body,
        [((R, 2, HALF), BF)],
        pn, aux, keep, swap(sy, 16), swap(sz, 2),
        scratch=[pltpu.VMEM((D, R), F32)],
        mib=MIB_POST,
    )
    back = lax.all_to_all(back, "dp", 0, 0, tiled=True)
    enc, grad, qkv_share, out_share, gain_grad, bias_grad = call(
        final_body,
        [
            ((QW, R), BF),
            ((QW, R), BF),
            ((10, 3, 2, HD), F32),
            ((10, 2, HD), F32),
            ((1, 10), F32),
            ((1, 10), F32),
        ],
        send_order, back,
    )
    return (
        enc.T,
        grad.T,
        qkv_share.transpose(0, 2, 1, 3),
        out_share.transpose(1, 2, 0),
        gain_grad.reshape(10),
        bias_grad.reshape(10),
    )


def solution(mesh):
    return jax.shard_map(
        local,
        mesh=mesh,
        in_specs=(
            P("dp", None),
            P("dp", None),
            P("dp", None),
            P("dp", None),
            P("dp", None),
            P(),
            P(),
            P(None, "zero", None, None),
            P("zero", None, None),
        ),
        out_specs=(
            P("dp", "zero"),
            P("dp", "zero"),
            P("dp", "zero", None, None),
            P("zero", None, "dp"),
            P("dp"),
            P("dp"),
        ),
        check_vma=False,
    )
```

```python
import jax
import jax.numpy as jnp
from jax import lax
from jax.experimental import pallas as pl
from jax.experimental.pallas import tpu as pltpu
from jax.sharding import PartitionSpec as P

EPS = 1e-06
R = 128
D = 1280
HD = 80
HG = 2
NQ = HG * 3 * HD
NO = HG * HD
QW = D // 4
QP = 384
F32 = jnp.float32
BF = jnp.bfloat16
PN = 5 * R
PNE = PN + 32
STEP = 2 * HD + 2
WG = 1664
HALF = (WG + 2 * QW) // 2

MIB = 1024 * 1024
GATHER_PARTS = 2
MIB_HOLD, MIB_BLOCK, MIB_PAIR, MIB_POST = 16, 50, 50, 50


def dg(a, b, ca, cb):
    return lax.dot_general(a, b, (((ca,), (cb,)), ((), ())), preferred_element_type=F32)


def call(body, outs, *args, smem=(), hbm=(), out_hbm=(), scratch=(), mib=50):
    def space(i):
        return pltpu.SMEM if i in smem else pltpu.HBM if i in hbm else pltpu.VMEM

    scratch = list(scratch) + [pltpu.VMEM(args[i].shape, args[i].dtype) for i in hbm]
    scratch += [pltpu.VMEM(*outs[i]) for i in out_hbm]
    if hbm or out_hbm:
        scratch.append(pltpu.SemaphoreType.DMA((10,)))
    return pl.pallas_call(
        body,
        out_shape=tuple(jax.ShapeDtypeStruct(s, d) for s, d in outs),
        in_specs=[pl.BlockSpec(memory_space=space(i)) for i in range(len(args))],
        out_specs=tuple(
            pl.BlockSpec(memory_space=pltpu.HBM if i in out_hbm else pltpu.VMEM)
            for i in range(len(outs))
        ),
        scratch_shapes=scratch,
        compiler_params=pltpu.CompilerParams(vmem_limit_bytes=mib * MIB),
    )(*args)


def start(sem, a, b):
    copy = pltpu.make_async_copy(a, b, sem)
    copy.start()
    return copy


def lane(shape):
    return lax.broadcasted_iota(jnp.int32, shape, 1)


def sub(shape):
    return lax.broadcasted_iota(jnp.int32, shape, 0)


def place_bits():
    dp = lax.axis_index("dp")
    return lax.rem(dp, 2), lax.rem(dp // 2, 2), lax.rem(dp // 16, 2)


def one_hot(cond):
    return cond.astype(F32).astype(BF)


def pair_picks(send_ref):
    spread = one_hot(lane((R, 2 * R)) // 2 == sub((R, 2 * R)))
    rows = jnp.broadcast_to(send_ref[...], (8, R)).astype(F32).astype(BF)
    target = dg(rows, spread, 1, 0)[0:1].astype(jnp.int32)
    hit = sub((R, 2 * R)) == target
    odd = lane((R, 2 * R)) % 2
    return one_hot(hit & (odd == 0)), one_hot(hit & (odd == 1))


def gather_body(send_hbm, x_hbm, g_hbm, o_hbm, send_ref, x_ref, g_ref, o_ref, sems):
    first = start(sems.at[7], send_hbm, send_ref)
    copies = [start(sems.at[0], x_hbm, x_ref), start(sems.at[1], g_hbm, g_ref)]
    first.wait()
    even, odd = pair_picks(send_ref)
    for copy in copies:
        copy.wait()
    copies = []
    step = R // GATHER_PARTS
    for i in range(GATHER_PARTS):
        rows = slice(2 * step * i, 2 * step * (i + 1))
        part = dg(even[:, rows], x_ref[...], 0, 0) + dg(odd[:, rows], g_ref[...], 0, 0)
        at = pl.ds(step * i, step)
        o_ref[at] = part.astype(BF).reshape(step, 2, D)
        copies.append(start(sems.at[2 + i], o_ref.at[at], o_hbm.at[at]))
    for copy in copies:
        copy.wait()


def norm_stats(x):
    mean = jnp.mean(x, axis=1, keepdims=True)
    centred = x - mean
    inv = lax.rsqrt(jnp.mean(centred * centred, axis=1, keepdims=True) + EPS)
    return mean, inv, centred * inv


def hold_body(
    recv_ref, seg_ref, gain_ref, bias_ref, wo_ref, same_ref, gain_out, bias_out, wo_out
):
    hit = sub((R, R)) == recv_ref[...]
    seg = jnp.sum(jnp.where(hit, seg_ref[...], 0), axis=1, keepdims=True)
    group = one_hot(seg == lane((R, R)))
    same_ref[...] = dg(group, group, 1, 1)
    gain_out[...] = gain_ref[...]
    bias_out[...] = bias_ref[...]
    wo_out[...] = wo_ref[...]


def block_body(
    xg_ref, same_ref, gain_ref, bias_ref, wo_ref, wq_hbm,
    pn_hbm, send_hbm, ng_ref, heads_ref, stat_ref,
    wq_ref, pn_ref, send_ref, sems,
):
    copies = [start(sems.at[0], wq_hbm, wq_ref)]
    xg = xg_ref[...].reshape(2 * R, D)
    at = lane((R, 2 * R)) - 2 * sub((R, 2 * R))
    x = dg(one_hot(at == 0), xg, 1, 0)
    g32 = dg(one_hot(at == 1), xg, 1, 0)
    g = g32.astype(BF)
    ng_ref[R:, :] = g
    mean, inv, xh = norm_stats(x)
    normed = (xh * gain_ref[...] + bias_ref[...]).astype(BF)
    ng_ref[:R, :] = normed
    for i in range(4):

        @pl.when(lax.axis_index("zero") == i)
        def _(i=i):
            cols = slice(i * QW, (i + 1) * QW)
            pad = jnp.zeros((R, QP - QW), F32)
            both = jnp.concatenate([x[:, cols], pad, g32[:, cols], pad], axis=1).astype(BF)
            for t in range(6):
                heads_ref[(5 + t) * R : (6 + t) * R] = both[:, t * R : (t + 1) * R]
            stat_ref[R:, :QW] = jnp.broadcast_to(gain_ref[:, cols], (8, QW))

    stat_ref[:R, :R] = jnp.where(lane((R, R)) < 64, mean, inv)
    dh = dg(wo_ref[...], g, 1, 1).astype(BF)
    copies.pop().wait()
    qkv = dg(wq_ref[...], normed, 1, 1).astype(BF)
    same = same_ref[...] > 0.5
    rows = []
    for h in range(HG):
        q = qkv[h * 3 * HD : h * 3 * HD + HD]
        k = qkv[h * 3 * HD + HD : h * 3 * HD + 2 * HD]
        v = qkv[h * 3 * HD + 2 * HD : (h + 1) * 3 * HD]
        dhh = dh[h * HD : (h + 1) * HD]
        s = jnp.where(same, dg(q, k, 0, 0) * (HD**-0.5), -1e30)
        e = jnp.exp(s - jnp.max(s, axis=1, keepdims=True))
        w = e / jnp.sum(e, axis=1, keepdims=True)
        w16 = w.astype(BF)
        pg = dg(dhh, v, 0, 0)
        delta = jnp.sum(pg * w, axis=1, keepdims=True)
        sg = (w * (pg - delta) * (HD**-0.5)).astype(BF)
        rows.append(dg(k, sg, 1, 1).astype(BF))
        rows.append(dg(q, sg, 1, 0).astype(BF))
        rows.append(dg(dhh, w16, 1, 0).astype(BF))
        rows.append(dg(v, w16, 1, 1).astype(BF))
    heads_ref[: 8 * HD] = jnp.concatenate(rows, axis=0)
    qg = jnp.concatenate(rows[0:3] + rows[4:7], axis=0)
    ho = jnp.concatenate([rows[3], rows[7]], axis=0)
    other = (1 - place_bits()[0]) * 4 * HD
    a = heads_ref[pl.ds(pl.multiple_of(other, 4 * HD), 3 * HD), :]
    b = heads_ref[pl.ds(pl.multiple_of(other + 3 * HD, HD), HD), :]
    send_ref[: 3 * HD, :] = dg(a, normed, 1, 0).astype(BF)
    send_ref[3 * HD :, :] = dg(b, g, 1, 0).astype(BF)
    copies.append(start(sems.at[9], send_ref, send_hbm))
    p = dg(ho, wo_ref[...], 0, 0)
    for i in range(4):
        for t in range(2):
            pn_ref[i, t * R : (t + 1) * R] = p[:, i * QW + t * R : i * QW + (t + 1) * R].astype(BF)
        rows = pl.ds(0, 2 * R)
        copies.append(start(sems.at[1 + i], pn_ref.at[i, rows], pn_hbm.at[i, rows]))
    n = dg(qg, wq_ref[...], 0, 0)
    u = n * gain_ref[...]
    m1 = jnp.sum(u, axis=1, keepdims=True) * (1.0 / D)
    m2 = jnp.sum(u * xh, axis=1, keepdims=True) * (1.0 / D)
    gain_row = jnp.sum(n * xh, axis=0, keepdims=True)
    bias_row = jnp.sum(n, axis=0, keepdims=True)
    extra = [r[:, t * R : (t + 1) * R] for r in (gain_row, bias_row) for t in range(10)]
    diagonal = sub((R, R)) == lane((R, R))
    for m in (m1, m2):
        row = jnp.sum(jnp.where(diagonal, m, 0.0), axis=0, keepdims=True)
        high = row.astype(BF).astype(F32)
        extra += [high, row - high]
    extra.append(jnp.zeros((8, R), F32))
    extra = jnp.concatenate(extra, axis=0).astype(BF)
    for i in range(4):
        at = i * QW
        mixed = jnp.concatenate([p[:, at + 2 * R : at + QW], n[:, at : at + 64]], axis=1)
        pn_ref[i, 2 * R : 3 * R] = mixed.astype(BF)
        for t in range(2):
            cols = slice(at + 64 + t * R, at + 64 + (t + 1) * R)
            pn_ref[i, (3 + t) * R : (4 + t) * R] = n[:, cols].astype(BF)
        pn_ref[i, PN:] = extra
        rows = pl.ds(2 * R, PNE - 2 * R)
        copies.append(start(sems.at[5 + i], pn_ref.at[i, rows], pn_hbm.at[i, rows]))
    for copy in copies:
        copy.wait()


def own_rows(c, first, choose_out, ng_ref, heads_ref):
    a = heads_ref[pl.ds(pl.multiple_of((c * 4 + first) * HD, HD), HD), :]
    if choose_out is None:
        return dg(a, ng_ref[:R, :], 1, 0)
    b = heads_ref[pl.ds(pl.multiple_of((c * 4 + 3) * HD, HD), HD), :]
    pick = choose_out.astype(F32)
    left = jnp.concatenate([a.astype(F32) * (1.0 - pick), b.astype(F32) * pick], axis=1).astype(BF)
    return dg(left, ng_ref[...], 1, 0)


def part_rows(ref, j):
    return ref[pl.ds(pl.multiple_of(j * HD, HD), HD), :].astype(F32)


def pair_body(ng_ref, heads_ref, got_ref, sz_ref, sy_ref):
    c, z, y = place_bits()
    a = own_rows(c, 1 - z, None, ng_ref, heads_ref)
    b = own_rows(c, 2, 1 - y, ng_ref, heads_ref)
    sz_ref[...] = (a + part_rows(got_ref, 1 - z)).astype(BF)
    sy_ref[...] = (b + part_rows(got_ref, 3 - y)).astype(BF)


def post_body(
    pn_ref, stat_ref, ng_ref, heads_ref, got_ref, gz_ref, gy_ref, o_ref, wz_ref, wy_ref
):
    c, z, y = place_bits()
    pn = jnp.sum(pn_ref[:, :PN].astype(F32), axis=0)
    extra = jnp.sum(pn_ref[:, PN:].astype(F32), axis=0)
    gain_row = jnp.concatenate([extra[t : t + 1] for t in range(10)], axis=1)
    bias_row = jnp.concatenate([extra[t : t + 1] for t in range(10, 20)], axis=1)
    wz = own_rows(c, z, None, ng_ref, heads_ref) + part_rows(got_ref, z)
    wz = wz + gz_ref[...].astype(F32)
    wz = jnp.concatenate([wz, gain_row, bias_row, jnp.zeros((6, D), F32)], axis=0)
    wz_ref[:, : HD + 8] = wz.T
    wy = own_rows(c, 2, y, ng_ref, heads_ref) + part_rows(got_ref, 2 + y)
    wy_ref[:, :HD] = (wy + gy_ref[...].astype(F32)).T
    slabs = []
    for i in range(10):
        rows = pl.ds(i, R, stride=10)
        slabs += [wz_ref[rows, :][:, : HD + 2], wy_ref[rows, :][:, :HD]]
    slabs.append(jnp.zeros((R, WG - 10 * STEP), F32))
    tiles = [pn[t * R : (t + 1) * R] for t in range(5)]
    both = jnp.concatenate(tiles, axis=1)
    diagonal = sub((R, R)) == lane((R, R))
    m1 = jnp.sum(jnp.where(diagonal, extra[20:21] + extra[21:22], 0.0), axis=1, keepdims=True)
    m2 = jnp.sum(jnp.where(diagonal, extra[22:23] + extra[23:24], 0.0), axis=1, keepdims=True)
    quarters = [heads_ref[(5 + t) * R : (6 + t) * R].astype(F32) for t in range(6)]
    x = jnp.concatenate(quarters[:3], axis=1)[:, :QW]
    g = jnp.concatenate(quarters[3:], axis=1)[:, :QW]
    mean = stat_ref[:R, 0:1]
    inv = stat_ref[:R, 64:65]
    xh = (x - mean) * inv
    enc = x + both[:, :QW]
    grad = both[:, QW:] * stat_ref[R : R + 1, :QW] - m1 - xh * m2
    grad = g + inv * grad
    row = jnp.concatenate(slabs + [enc, grad], axis=1).astype(BF)
    at = sub((2 * R, R)) - 2 * lane((2 * R, R))
    both = dg(one_hot(at == 0), row[:, :HALF], 1, 0) + dg(one_hot(at == 1), row[:, HALF:], 1, 0)
    o_ref[...] = both.astype(BF).reshape(R, 2, HALF)


def final_body(send_ref, b_ref, e_ref, i_ref, a_ref, w_ref, gain_ref, bias_ref):
    _, odd = pair_picks(send_ref)
    back = b_ref[...].reshape(2 * R, HALF)
    rows = dg(back[:, WG - HALF :], odd, 0, 1).astype(BF)
    e_ref[...] = rows[:QW]
    i_ref[...] = rows[QW:]
    row = sub((16, 2 * R))
    src = lane((16, 2 * R)) // 2
    half = (row // 2) % 2
    c_ok = src % 2 == row % 2
    z_ok = (src // 2) % 2 == half
    y_ok = (src // 16) % 2 == half
    mask = ((row < 4) & c_ok & z_ok) | ((row >= 4) & (row < 8) & c_ok & y_ok) | (row == 8)
    first = lane((16, 2 * R)) % 2 == 0
    sums = jnp.concatenate(
        [
            dg(one_hot(mask & first), back, 1, 0),
            dg(one_hot(mask & ~first), back[:, : WG - HALF], 1, 0),
        ],
        axis=1,
    )
    for i in range(10):
        at = i * STEP
        a_ref[i, 0] = sums[0:2, at : at + HD]
        a_ref[i, 1] = sums[2:4, at : at + HD]
        gain_ref[:, i : i + 1] = sums[8:9, at + HD : at + HD + 1]
        bias_ref[:, i : i + 1] = sums[8:9, at + HD + 1 : at + HD + 2]
        a_ref[i, 2] = sums[4:6, at + HD + 2 : at + STEP]
        w_ref[i] = sums[6:8, at + HD + 2 : at + STEP]


def local(patches, cotangent, send_order, recv_order, segment_ids, ln_gain, ln_bias, w_qkv, w_out):
    wq = w_qkv.transpose(1, 2, 3, 0).reshape(NQ, D)
    wo = w_out.reshape(NO, D)
    gain = ln_gain.reshape(1, D)
    bias = ln_bias.reshape(1, D)

    def swap(a, bit):
        return lax.ppermute(a, "dp", [(i, i ^ bit) for i in range(128)])

    (xg,) = call(gather_body, [((R, 2, D), BF)], send_order, patches, cotangent, hbm=(0, 1, 2), out_hbm=(0,), mib=58)
    same, gain, bias, wo = call(
        hold_body,
        [((R, R), F32), ((1, D), F32), ((1, D), F32), ((NO, D), BF)],
        recv_order, segment_ids, gain, bias, wo,
        mib=MIB_HOLD,
    )
    xg = lax.all_to_all(xg, "dp", 0, 0, tiled=True)
    pn, send, ng, heads, stat = call(
        block_body,
        [
            ((4, PNE, R), BF),
            ((4 * HD, D), BF),
            ((2 * R, D), BF),
            ((8 * HD + 6 * R, R), BF),
            ((R + 8, QP), F32),
        ],
        xg, same, gain, bias, wo, wq,
        hbm=(5,),
        out_hbm=(0, 1),
        mib=MIB_BLOCK,
    )
    got = swap(send, 1)
    pn = lax.all_to_all(pn, "zero", 0, 0, tiled=True)
    sz, sy = call(
        pair_body,
        [((HD, D), BF), ((HD, D), BF)],
        ng, heads, got,
        mib=MIB_PAIR,
    )
    gz = swap(sz, 2)
    gy = swap(sy, 16)
    (back,) = call(
        post_body,
        [((R, 2, HALF), BF)],
        pn, stat, ng, heads, got, gz, gy,
        scratch=[pltpu.VMEM((D, R), F32)] * 2,
        mib=MIB_POST,
    )
    back = lax.all_to_all(back, "dp", 0, 0, tiled=True)
    enc, grad, qkv_share, out_share, gain_grad, bias_grad = call(
        final_body,
        [
            ((QW, R), BF),
            ((QW, R), BF),
            ((10, 3, 2, HD), F32),
            ((10, 2, HD), F32),
            ((1, 10), F32),
            ((1, 10), F32),
        ],
        send_order, back,
    )
    return (
        enc.T,
        grad.T,
        qkv_share.transpose(0, 2, 1, 3),
        out_share.transpose(1, 2, 0),
        gain_grad.reshape(10),
        bias_grad.reshape(10),
    )


def solution(mesh):
    return jax.shard_map(
        local,
        mesh=mesh,
        in_specs=(
            P("dp", None),
            P("dp", None),
            P("dp", None),
            P("dp", None),
            P("dp", None),
            P(),
            P(),
            P(None, "zero", None, None),
            P("zero", None, None),
        ),
        out_specs=(
            P("dp", "zero"),
            P("dp", "zero"),
            P("dp", "zero", None, None),
            P("zero", None, "dp"),
            P("dp"),
            P("dp"),
        ),
        check_vma=False,
    )
```

```python
import jax
import jax.numpy as jnp
from jax import lax
from jax.experimental import pallas as pl
from jax.experimental.pallas import tpu as pltpu
from jax.sharding import PartitionSpec as P

EPS = 1e-06
R = 128
D = 1280
HD = 80
HG = 2
NQ = HG * 3 * HD
NO = HG * HD
QW = D // 4
QP = 384
F32 = jnp.float32
BF = jnp.bfloat16
PN = 5 * R
PNE = PN + 32
STEP = 2 * HD + 2
WG = 1664
HALF = (WG + 2 * QW) // 2


def dg(a, b, ca, cb):
    return lax.dot_general(a, b, (((ca,), (cb,)), ((), ())), preferred_element_type=F32)


def call(body, outs, *args, scratch=()):
    vmem = pl.BlockSpec(memory_space=pltpu.VMEM)
    return pl.pallas_call(
        body,
        out_shape=tuple(jax.ShapeDtypeStruct(s, d) for s, d in outs),
        in_specs=[vmem] * len(args),
        out_specs=(vmem,) * len(outs),
        scratch_shapes=scratch,
        compiler_params=pltpu.CompilerParams(vmem_limit_bytes=16 * 1024 * 1024),
    )(*args)


def lane(shape):
    return lax.broadcasted_iota(jnp.int32, shape, 1)


def sub(shape):
    return lax.broadcasted_iota(jnp.int32, shape, 0)


def place_bits():
    dp = lax.axis_index("dp")
    return lax.rem(dp, 2), lax.rem(dp // 2, 2), lax.rem(dp // 16, 2)


def one_hot(cond):
    return cond.astype(F32).astype(BF)


def pair_picks(send_ref):
    spread = one_hot(lane((R, 2 * R)) // 2 == sub((R, 2 * R)))
    rows = jnp.broadcast_to(send_ref[...], (8, R)).astype(F32).astype(BF)
    target = dg(rows, spread, 1, 0)[0:1].astype(jnp.int32)
    hit = sub((R, 2 * R)) == target
    odd = lane((R, 2 * R)) % 2
    return one_hot(hit & (odd == 0)), one_hot(hit & (odd == 1))


def gather_body(
    send_ref, xg_ref, recv_ref, seg_ref, gain_ref, bias_ref, wo_ref,
    o_ref, same_ref, gain_out, bias_out, wo_out,
):
    even, odd = pair_picks(send_ref)
    pick = jnp.concatenate([even, odd], axis=0)
    o_ref[...] = dg(pick, xg_ref[...], 0, 0).astype(BF).reshape(R, 2, D)
    hit = sub((R, R)) == recv_ref[...]
    seg = jnp.sum(jnp.where(hit, seg_ref[...], 0), axis=1, keepdims=True)
    group = one_hot(seg == lane((R, R)))
    same_ref[...] = dg(group, group, 1, 1)
    gain_out[...] = gain_ref[...].reshape(1, D)
    bias_out[...] = bias_ref[...].reshape(1, D)
    wo_out[...] = wo_ref[...]


def norm_stats(x):
    mean = jnp.mean(x, axis=1, keepdims=True)
    centred = x - mean
    inv = lax.rsqrt(jnp.mean(centred * centred, axis=1, keepdims=True) + EPS)
    return mean, inv, centred * inv


def block_body(
    xg_ref, same_ref, gain_ref, bias_ref, wo_ref, wq_ref,
    pn_ref, ng_ref, heads_ref, stat_ref,
):
    xg = xg_ref[...].reshape(2 * R, D)
    at = lane((R, 2 * R)) - 2 * sub((R, 2 * R))
    x = dg(one_hot(at == 0), xg, 1, 0)
    g32 = dg(one_hot(at == 1), xg, 1, 0)
    g = g32.astype(BF)
    ng_ref[R:, :] = g
    mean, inv, xh = norm_stats(x)
    normed = (xh * gain_ref[...] + bias_ref[...]).astype(BF)
    ng_ref[:R, :] = normed
    for i in range(4):

        @pl.when(lax.axis_index("zero") == i)
        def _(i=i):
            cols = slice(i * QW, (i + 1) * QW)
            pad = jnp.zeros((R, QP - QW), F32)
            both = jnp.concatenate([x[:, cols], pad, g32[:, cols], pad], axis=1).astype(BF)
            for t in range(6):
                heads_ref[(5 + t) * R : (6 + t) * R] = both[:, t * R : (t + 1) * R]
            stat_ref[R:, :QW] = jnp.broadcast_to(gain_ref[:, cols], (8, QW))

    stat_ref[:R, :R] = jnp.where(lane((R, R)) < 64, mean, inv)
    dh = dg(wo_ref[...], g, 1, 1).astype(BF)
    qkv = dg(wq_ref[...], normed, 1, 1).astype(BF)
    same = same_ref[...] > 0.5
    rows = []
    for h in range(HG):
        q = qkv[h * 3 * HD : h * 3 * HD + HD]
        k = qkv[h * 3 * HD + HD : h * 3 * HD + 2 * HD]
        v = qkv[h * 3 * HD + 2 * HD : (h + 1) * 3 * HD]
        dhh = dh[h * HD : (h + 1) * HD]
        s = jnp.where(same, dg(q, k, 0, 0) * (HD**-0.5), -1e30)
        e = jnp.exp(s - jnp.max(s, axis=1, keepdims=True))
        w = e / jnp.sum(e, axis=1, keepdims=True)
        w16 = w.astype(BF)
        pg = dg(dhh, v, 0, 0)
        delta = jnp.sum(pg * w, axis=1, keepdims=True)
        sg = (w * (pg - delta) * (HD**-0.5)).astype(BF)
        rows.append(dg(k, sg, 1, 1).astype(BF))
        rows.append(dg(q, sg, 1, 0).astype(BF))
        rows.append(dg(dhh, w16, 1, 0).astype(BF))
        rows.append(dg(v, w16, 1, 1).astype(BF))
    heads_ref[: 8 * HD] = jnp.concatenate(rows, axis=0)
    qg = jnp.concatenate(rows[0:3] + rows[4:7], axis=0)
    ho = jnp.concatenate([rows[3], rows[7]], axis=0)
    p = dg(ho, wo_ref[...], 0, 0)
    for i in range(4):
        for t in range(2):
            pn_ref[i, t * R : (t + 1) * R] = p[:, i * QW + t * R : i * QW + (t + 1) * R].astype(BF)
    n = dg(qg, wq_ref[...], 0, 0)
    u = n * gain_ref[...]
    m1 = jnp.sum(u, axis=1, keepdims=True) * (1.0 / D)
    m2 = jnp.sum(u * xh, axis=1, keepdims=True) * (1.0 / D)
    gain_row = jnp.sum(n * xh, axis=0, keepdims=True)
    bias_row = jnp.sum(n, axis=0, keepdims=True)
    extra = [r[:, t * R : (t + 1) * R] for r in (gain_row, bias_row) for t in range(10)]
    diagonal = sub((R, R)) == lane((R, R))
    for m in (m1, m2):
        row = jnp.sum(jnp.where(diagonal, m, 0.0), axis=0, keepdims=True)
        high = row.astype(BF).astype(F32)
        extra += [high, row - high]
    extra.append(jnp.zeros((8, R), F32))
    extra = jnp.concatenate(extra, axis=0).astype(BF)
    for i in range(4):
        at = i * QW
        mixed = jnp.concatenate([p[:, at + 2 * R : at + QW], n[:, at : at + 64]], axis=1)
        pn_ref[i, 2 * R : 3 * R] = mixed.astype(BF)
        for t in range(2):
            cols = slice(at + 64 + t * R, at + 64 + (t + 1) * R)
            pn_ref[i, (3 + t) * R : (4 + t) * R] = n[:, cols].astype(BF)
        pn_ref[i, PN:] = extra


def other_body(ng_ref, heads_ref, send_ref):
    other = (1 - place_bits()[0]) * 4 * HD
    a = heads_ref[pl.ds(pl.multiple_of(other, 4 * HD), 3 * HD), :]
    b = heads_ref[pl.ds(pl.multiple_of(other + 3 * HD, HD), HD), :]
    send_ref[: 3 * HD, :] = dg(a, ng_ref[:R, :], 1, 0).astype(BF)
    send_ref[3 * HD :, :] = dg(b, ng_ref[R:, :], 1, 0).astype(BF)


def own_rows(c, first, choose_out, ng_ref, heads_ref):
    a = heads_ref[pl.ds(pl.multiple_of((c * 4 + first) * HD, HD), HD), :]
    if choose_out is None:
        return dg(a, ng_ref[:R, :], 1, 0)
    b = heads_ref[pl.ds(pl.multiple_of((c * 4 + 3) * HD, HD), HD), :]
    pick = choose_out.astype(F32)
    left = jnp.concatenate([a.astype(F32) * (1.0 - pick), b.astype(F32) * pick], axis=1).astype(BF)
    return dg(left, ng_ref[...], 1, 0)


def part_rows(ref, j):
    return ref[pl.ds(pl.multiple_of(j * HD, HD), HD), :].astype(F32)


def pair_body(ng_ref, heads_ref, got_ref, sz_ref, sy_ref):
    c, z, y = place_bits()
    a = own_rows(c, 1 - z, None, ng_ref, heads_ref)
    b = own_rows(c, 2, 1 - y, ng_ref, heads_ref)
    sz_ref[...] = (a + part_rows(got_ref, 1 - z)).astype(BF)
    sy_ref[...] = (b + part_rows(got_ref, 3 - y)).astype(BF)


def post_body(
    pn_ref, stat_ref, ng_ref, heads_ref, got_ref, gz_ref, gy_ref, o_ref, wz_ref, wy_ref
):
    c, z, y = place_bits()
    pn = jnp.sum(pn_ref[:, :PN].astype(F32), axis=0)
    extra = jnp.sum(pn_ref[:, PN:].astype(F32), axis=0)
    gain_row = jnp.concatenate([extra[t : t + 1] for t in range(10)], axis=1)
    bias_row = jnp.concatenate([extra[t : t + 1] for t in range(10, 20)], axis=1)
    wz = own_rows(c, z, None, ng_ref, heads_ref) + part_rows(got_ref, z)
    wz = wz + gz_ref[...].astype(F32)
    wz = jnp.concatenate([wz, gain_row, bias_row, jnp.zeros((6, D), F32)], axis=0)
    wz_ref[:, : HD + 8] = wz.T
    wy = own_rows(c, 2, y, ng_ref, heads_ref) + part_rows(got_ref, 2 + y)
    wy_ref[:, :HD] = (wy + gy_ref[...].astype(F32)).T
    slabs = []
    for i in range(10):
        rows = pl.ds(i, R, stride=10)
        slabs += [wz_ref[rows, :][:, : HD + 2], wy_ref[rows, :][:, :HD]]
    slabs.append(jnp.zeros((R, WG - 10 * STEP), F32))
    tiles = [pn[t * R : (t + 1) * R] for t in range(5)]
    both = jnp.concatenate(tiles, axis=1)
    diagonal = sub((R, R)) == lane((R, R))
    m1 = jnp.sum(jnp.where(diagonal, extra[20:21] + extra[21:22], 0.0), axis=1, keepdims=True)
    m2 = jnp.sum(jnp.where(diagonal, extra[22:23] + extra[23:24], 0.0), axis=1, keepdims=True)
    quarters = [heads_ref[(5 + t) * R : (6 + t) * R].astype(F32) for t in range(6)]
    x = jnp.concatenate(quarters[:3], axis=1)[:, :QW]
    g = jnp.concatenate(quarters[3:], axis=1)[:, :QW]
    mean = stat_ref[:R, 0:1]
    inv = stat_ref[:R, 64:65]
    xh = (x - mean) * inv
    enc = x + both[:, :QW]
    grad = both[:, QW:] * stat_ref[R : R + 1, :QW] - m1 - xh * m2
    grad = g + inv * grad
    row = jnp.concatenate(slabs + [enc, grad], axis=1).astype(BF)
    at = sub((2 * R, R)) - 2 * lane((2 * R, R))
    both = dg(one_hot(at == 0), row[:, :HALF], 1, 0) + dg(one_hot(at == 1), row[:, HALF:], 1, 0)
    o_ref[...] = both.astype(BF).reshape(R, 2, HALF)


def final_body(send_ref, b_ref, e_ref, i_ref, a_ref, w_ref, gain_ref, bias_ref):
    _, odd = pair_picks(send_ref)
    back = b_ref[...].reshape(2 * R, HALF)
    rows = dg(back[:, WG - HALF :], odd, 0, 1).astype(BF)
    e_ref[...] = rows[:QW]
    i_ref[...] = rows[QW:]
    row = sub((16, 2 * R))
    src = lane((16, 2 * R)) // 2
    half = (row // 2) % 2
    c_ok = src % 2 == row % 2
    z_ok = (src // 2) % 2 == half
    y_ok = (src // 16) % 2 == half
    mask = ((row < 4) & c_ok & z_ok) | ((row >= 4) & (row < 8) & c_ok & y_ok) | (row == 8)
    first = lane((16, 2 * R)) % 2 == 0
    sums = jnp.concatenate(
        [
            dg(one_hot(mask & first), back, 1, 0),
            dg(one_hot(mask & ~first), back[:, : WG - HALF], 1, 0),
        ],
        axis=1,
    )
    for i in range(10):
        at = i * STEP
        a_ref[i, 0] = sums[0:2, at : at + HD]
        a_ref[i, 1] = sums[2:4, at : at + HD]
        gain_ref[:, i : i + 1] = sums[8:9, at + HD : at + HD + 1]
        bias_ref[:, i : i + 1] = sums[8:9, at + HD + 1 : at + HD + 2]
        a_ref[i, 2] = sums[4:6, at + HD + 2 : at + STEP]
        w_ref[i] = sums[6:8, at + HD + 2 : at + STEP]


def local(patches, cotangent, send_order, recv_order, segment_ids, ln_gain, ln_bias, w_qkv, w_out):
    wq = w_qkv.transpose(1, 2, 3, 0).reshape(NQ, D)
    wo = w_out.reshape(NO, D)

    def swap(a, bit):
        return lax.ppermute(a, "dp", [(i, i ^ bit) for i in range(128)])

    xg = jnp.concatenate([patches, cotangent], axis=0)
    xg, same, gain, bias, wo = call(
        gather_body,
        [((R, 2, D), BF), ((R, R), F32), ((1, D), F32), ((1, D), F32), ((NO, D), BF)],
        send_order, xg, recv_order, segment_ids, ln_gain, ln_bias, wo,
    )
    xg = lax.all_to_all(xg, "dp", 0, 0, tiled=True)
    pn, ng, heads, stat = call(
        block_body,
        [
            ((4, PNE, R), BF),
            ((2 * R, D), BF),
            ((8 * HD + 6 * R, R), BF),
            ((R + 8, QP), F32),
        ],
        xg, same, gain, bias, wo, wq,
    )
    (send,) = call(other_body, [((4 * HD, D), BF)], ng, heads)
    got = swap(send, 1)
    pn = lax.all_to_all(pn, "zero", 0, 0, tiled=True)
    sz, sy = call(
        pair_body,
        [((HD, D), BF), ((HD, D), BF)],
        ng, heads, got,
    )
    gz = swap(sz, 2)
    gy = swap(sy, 16)
    (back,) = call(
        post_body,
        [((R, 2, HALF), BF)],
        pn, stat, ng, heads, got, gz, gy,
        scratch=[pltpu.VMEM((D, R), F32)] * 2,
    )
    back = lax.all_to_all(back, "dp", 0, 0, tiled=True)
    enc, grad, qkv_share, out_share, gain_grad, bias_grad = call(
        final_body,
        [
            ((QW, R), BF),
            ((QW, R), BF),
            ((10, 3, 2, HD), F32),
            ((10, 2, HD), F32),
            ((1, 10), F32),
            ((1, 10), F32),
        ],
        send_order, back,
    )
    return (
        enc.T,
        grad.T,
        qkv_share.transpose(0, 2, 1, 3),
        out_share.transpose(1, 2, 0),
        gain_grad.reshape(10),
        bias_grad.reshape(10),
    )


def solution(mesh):
    return jax.shard_map(
        local,
        mesh=mesh,
        in_specs=(
            P("dp", None),
            P("dp", None),
            P("dp", None),
            P("dp", None),
            P("dp", None),
            P(),
            P(),
            P(None, "zero", None, None),
            P("zero", None, None),
        ),
        out_specs=(
            P("dp", "zero"),
            P("dp", "zero"),
            P("dp", "zero", None, None),
            P("zero", None, "dp"),
            P("dp"),
            P("dp"),
        ),
        check_vma=False,
    )
```

```python
import jax
import jax.numpy as jnp
from jax import lax
from jax.experimental import pallas as pl
from jax.experimental.pallas import tpu as pltpu
from jax.sharding import PartitionSpec as P

EPS = 1e-06
R = 128
D = 1280
HD = 80
HG = 2
NQ = HG * 3 * HD
NO = HG * HD
QW = D // 4
QP = 384
F32 = jnp.float32
BF = jnp.bfloat16
PN = 5 * R
PNE = PN + 32
STEP = 2 * HD + 2
WG = 1664
HALF = (WG + 2 * QW) // 2


def dg(a, b, ca, cb):
    return lax.dot_general(a, b, (((ca,), (cb,)), ((), ())), preferred_element_type=F32)


def call(body, outs, *args, scratch=()):
    vmem = pl.BlockSpec(memory_space=pltpu.VMEM)
    return pl.pallas_call(
        body,
        out_shape=tuple(jax.ShapeDtypeStruct(s, d) for s, d in outs),
        in_specs=[vmem] * len(args),
        out_specs=(vmem,) * len(outs),
        scratch_shapes=scratch,
        compiler_params=pltpu.CompilerParams(vmem_limit_bytes=16 * 1024 * 1024),
    )(*args)


def lane(shape):
    return lax.broadcasted_iota(jnp.int32, shape, 1)


def sub(shape):
    return lax.broadcasted_iota(jnp.int32, shape, 0)


def place_bits():
    dp = lax.axis_index("dp")
    core = lax.rem(dp, 2)
    return core, jnp.where(core == 0, lax.rem(dp // 2, 2), lax.rem(dp // 16, 2))


def partner(i):
    return i ^ (2 if i % 2 == 0 else 16)


def one_hot(cond):
    return cond.astype(F32).astype(BF)


def pair_picks(send_ref):
    spread = one_hot(lane((R, 2 * R)) // 2 == sub((R, 2 * R)))
    rows = jnp.broadcast_to(send_ref[...], (8, R)).astype(F32).astype(BF)
    target = dg(rows, spread, 1, 0)[0:1].astype(jnp.int32)
    hit = sub((R, 2 * R)) == target
    odd = lane((R, 2 * R)) % 2
    return one_hot(hit & (odd == 0)), one_hot(hit & (odd == 1))


def gather_body(
    send_ref, xg_ref, recv_ref, seg_ref, gain_ref, bias_ref, wo_ref,
    o_ref, same_ref, gain_out, bias_out, wo_out,
):
    even, odd = pair_picks(send_ref)
    pick = jnp.concatenate([even, odd], axis=0)
    o_ref[...] = dg(pick, xg_ref[...], 0, 0).astype(BF).reshape(R, 2, D)
    hit = sub((R, R)) == recv_ref[...]
    seg = jnp.sum(jnp.where(hit, seg_ref[...], 0), axis=1, keepdims=True)
    group = one_hot(seg == lane((R, R)))
    same_ref[...] = dg(group, group, 1, 1)
    gain_out[...] = gain_ref[...].reshape(1, D)
    bias_out[...] = bias_ref[...].reshape(1, D)
    wo_out[...] = wo_ref[...]


def norm_stats(x):
    mean = jnp.mean(x, axis=1, keepdims=True)
    centred = x - mean
    inv = lax.rsqrt(jnp.mean(centred * centred, axis=1, keepdims=True) + EPS)
    return mean, inv, centred * inv


def block_body(
    xg_ref, same_ref, gain_ref, bias_ref, wo_ref, wq_ref,
    pn_ref, ng_ref, heads_ref, stat_ref,
):
    xg = xg_ref[...].reshape(2 * R, D)
    at = lane((R, 2 * R)) - 2 * sub((R, 2 * R))
    x = dg(one_hot(at == 0), xg, 1, 0)
    g32 = dg(one_hot(at == 1), xg, 1, 0)
    g = g32.astype(BF)
    ng_ref[R:, :] = g
    mean, inv, xh = norm_stats(x)
    normed = (xh * gain_ref[...] + bias_ref[...]).astype(BF)
    ng_ref[:R, :] = normed
    for i in range(4):

        @pl.when(lax.axis_index("zero") == i)
        def _(i=i):
            cols = slice(i * QW, (i + 1) * QW)
            pad = jnp.zeros((R, QP - QW), F32)
            both = jnp.concatenate([x[:, cols], pad, g32[:, cols], pad], axis=1).astype(BF)
            for t in range(6):
                heads_ref[(5 + t) * R : (6 + t) * R] = both[:, t * R : (t + 1) * R]
            stat_ref[R:, :QW] = jnp.broadcast_to(gain_ref[:, cols], (8, QW))

    stat_ref[:R, :R] = jnp.where(lane((R, R)) < 64, mean, inv)
    dh = dg(wo_ref[...], g, 1, 1).astype(BF)
    qkv = dg(wq_ref[...], normed, 1, 1).astype(BF)
    same = same_ref[...] > 0.5
    rows = []
    for h in range(HG):
        q = qkv[h * 3 * HD : h * 3 * HD + HD]
        k = qkv[h * 3 * HD + HD : h * 3 * HD + 2 * HD]
        v = qkv[h * 3 * HD + 2 * HD : (h + 1) * 3 * HD]
        dhh = dh[h * HD : (h + 1) * HD]
        s = jnp.where(same, dg(q, k, 0, 0) * (HD**-0.5), -1e30)
        e = jnp.exp(s - jnp.max(s, axis=1, keepdims=True))
        w = e / jnp.sum(e, axis=1, keepdims=True)
        w16 = w.astype(BF)
        pg = dg(dhh, v, 0, 0)
        delta = jnp.sum(pg * w, axis=1, keepdims=True)
        sg = (w * (pg - delta) * (HD**-0.5)).astype(BF)
        rows.append(dg(k, sg, 1, 1).astype(BF))
        rows.append(dg(q, sg, 1, 0).astype(BF))
        rows.append(dg(dhh, w16, 1, 0).astype(BF))
        rows.append(dg(v, w16, 1, 1).astype(BF))
    heads_ref[: 8 * HD] = jnp.concatenate(rows, axis=0)
    qg = jnp.concatenate(rows[0:3] + rows[4:7], axis=0)
    ho = jnp.concatenate([rows[3], rows[7]], axis=0)
    p = dg(ho, wo_ref[...], 0, 0)
    for i in range(4):
        for t in range(2):
            pn_ref[i, t * R : (t + 1) * R] = p[:, i * QW + t * R : i * QW + (t + 1) * R].astype(BF)
    n = dg(qg, wq_ref[...], 0, 0)
    u = n * gain_ref[...]
    m1 = jnp.sum(u, axis=1, keepdims=True) * (1.0 / D)
    m2 = jnp.sum(u * xh, axis=1, keepdims=True) * (1.0 / D)
    gain_row = jnp.sum(n * xh, axis=0, keepdims=True)
    bias_row = jnp.sum(n, axis=0, keepdims=True)
    extra = [r[:, t * R : (t + 1) * R] for r in (gain_row, bias_row) for t in range(10)]
    diagonal = sub((R, R)) == lane((R, R))
    for m in (m1, m2):
        row = jnp.sum(jnp.where(diagonal, m, 0.0), axis=0, keepdims=True)
        high = row.astype(BF).astype(F32)
        extra += [high, row - high]
    extra.append(jnp.zeros((8, R), F32))
    extra = jnp.concatenate(extra, axis=0).astype(BF)
    for i in range(4):
        at = i * QW
        mixed = jnp.concatenate([p[:, at + 2 * R : at + QW], n[:, at : at + 64]], axis=1)
        pn_ref[i, 2 * R : 3 * R] = mixed.astype(BF)
        for t in range(2):
            cols = slice(at + 64 + t * R, at + 64 + (t + 1) * R)
            pn_ref[i, (3 + t) * R : (4 + t) * R] = n[:, cols].astype(BF)
        pn_ref[i, PN:] = extra


def other_body(ng_ref, heads_ref, send_ref):
    other = (1 - place_bits()[0]) * 4 * HD
    a = heads_ref[pl.ds(pl.multiple_of(other, 4 * HD), 3 * HD), :]
    b = heads_ref[pl.ds(pl.multiple_of(other + 3 * HD, HD), HD), :]
    send_ref[: 3 * HD, :] = dg(a, ng_ref[:R, :], 1, 0).astype(BF)
    send_ref[3 * HD :, :] = dg(b, ng_ref[R:, :], 1, 0).astype(BF)


def half_rows(c, half, ng_ref, heads_ref, got_ref):
    rows = heads_ref[pl.ds(pl.multiple_of((c * 2 + half) * 2 * HD, 2 * HD), 2 * HD), :]
    out = half.astype(F32) * (sub((2 * HD, R)) >= HD).astype(F32)
    rows = rows.astype(F32)
    left = jnp.concatenate([rows * (1.0 - out), rows * out], axis=1).astype(BF)
    got = got_ref[pl.ds(pl.multiple_of(half * 2 * HD, 2 * HD), 2 * HD), :]
    return dg(left, ng_ref[...], 1, 0) + got.astype(F32)


def pair_body(ng_ref, heads_ref, got_ref, send_ref):
    c, half = place_bits()
    send_ref[...] = half_rows(c, 1 - half, ng_ref, heads_ref, got_ref).astype(BF)


def post_body(
    pn_ref, stat_ref, ng_ref, heads_ref, got_ref, pair_ref, o_ref, wz_ref, wy_ref
):
    c, half = place_bits()
    pn = jnp.sum(pn_ref[:, :PN].astype(F32), axis=0)
    extra = jnp.sum(pn_ref[:, PN:].astype(F32), axis=0)
    gain_row = jnp.concatenate([extra[t : t + 1] for t in range(10)], axis=1)
    bias_row = jnp.concatenate([extra[t : t + 1] for t in range(10, 20)], axis=1)
    wg = half_rows(c, half, ng_ref, heads_ref, got_ref) + pair_ref[...].astype(F32)
    wz = jnp.concatenate([wg[:HD], gain_row, bias_row, jnp.zeros((6, D), F32)], axis=0)
    wz_ref[:, : HD + 8] = wz.T
    wy_ref[:, :HD] = wg[HD:].T
    slabs = []
    for i in range(10):
        rows = pl.ds(i, R, stride=10)
        slabs += [wz_ref[rows, :][:, : HD + 2], wy_ref[rows, :][:, :HD]]
    slabs.append(jnp.zeros((R, WG - 10 * STEP), F32))
    tiles = [pn[t * R : (t + 1) * R] for t in range(5)]
    both = jnp.concatenate(tiles, axis=1)
    diagonal = sub((R, R)) == lane((R, R))
    m1 = jnp.sum(jnp.where(diagonal, extra[20:21] + extra[21:22], 0.0), axis=1, keepdims=True)
    m2 = jnp.sum(jnp.where(diagonal, extra[22:23] + extra[23:24], 0.0), axis=1, keepdims=True)
    quarters = [heads_ref[(5 + t) * R : (6 + t) * R].astype(F32) for t in range(6)]
    x = jnp.concatenate(quarters[:3], axis=1)[:, :QW]
    g = jnp.concatenate(quarters[3:], axis=1)[:, :QW]
    mean = stat_ref[:R, 0:1]
    inv = stat_ref[:R, 64:65]
    xh = (x - mean) * inv
    enc = x + both[:, :QW]
    grad = both[:, QW:] * stat_ref[R : R + 1, :QW] - m1 - xh * m2
    grad = g + inv * grad
    row = jnp.concatenate(slabs + [enc, grad], axis=1).astype(BF)
    at = sub((2 * R, R)) - 2 * lane((2 * R, R))
    both = dg(one_hot(at == 0), row[:, :HALF], 1, 0) + dg(one_hot(at == 1), row[:, HALF:], 1, 0)
    o_ref[...] = both.astype(BF).reshape(R, 2, HALF)


def final_body(send_ref, b_ref, e_ref, i_ref, a_ref, w_ref, gain_ref, bias_ref):
    _, odd = pair_picks(send_ref)
    back = b_ref[...].reshape(2 * R, HALF)
    rows = dg(back[:, WG - HALF :], odd, 0, 1).astype(BF)
    e_ref[...] = rows[:QW]
    i_ref[...] = rows[QW:]
    row = sub((16, 2 * R))
    src = lane((16, 2 * R)) // 2
    half = jnp.where(src % 2 == 0, (src // 2) % 2, (src // 16) % 2)
    mask = (row == 2 * half + src % 2) | (row == 8)
    first = lane((16, 2 * R)) % 2 == 0
    sums = jnp.concatenate(
        [
            dg(one_hot(mask & first), back, 1, 0),
            dg(one_hot(mask & ~first), back[:, : WG - HALF], 1, 0),
        ],
        axis=1,
    )
    for i in range(10):
        at = i * STEP
        a_ref[i, 0] = sums[0:2, at : at + HD]
        a_ref[i, 1] = sums[0:2, at + HD + 2 : at + STEP]
        a_ref[i, 2] = sums[2:4, at : at + HD]
        w_ref[i] = sums[2:4, at + HD + 2 : at + STEP]
        gain_ref[:, i : i + 1] = sums[8:9, at + HD : at + HD + 1]
        bias_ref[:, i : i + 1] = sums[8:9, at + HD + 1 : at + HD + 2]


def local(patches, cotangent, send_order, recv_order, segment_ids, ln_gain, ln_bias, w_qkv, w_out):
    wq = w_qkv.transpose(1, 2, 3, 0).reshape(NQ, D)
    wo = w_out.reshape(NO, D)

    def swap(a, other):
        return lax.ppermute(a, "dp", [(i, other(i)) for i in range(128)])

    xg = jnp.concatenate([patches, cotangent], axis=0)
    xg, same, gain, bias, wo = call(
        gather_body,
        [((R, 2, D), BF), ((R, R), F32), ((1, D), F32), ((1, D), F32), ((NO, D), BF)],
        send_order, xg, recv_order, segment_ids, ln_gain, ln_bias, wo,
    )
    xg = lax.all_to_all(xg, "dp", 0, 0, tiled=True)
    pn, ng, heads, stat = call(
        block_body,
        [
            ((4, PNE, R), BF),
            ((2 * R, D), BF),
            ((8 * HD + 6 * R, R), BF),
            ((R + 8, QP), F32),
        ],
        xg, same, gain, bias, wo, wq,
    )
    (send,) = call(other_body, [((4 * HD, D), BF)], ng, heads)
    got = swap(send, lambda i: i ^ 1)
    pn = lax.all_to_all(pn, "zero", 0, 0, tiled=True)
    (pair,) = call(pair_body, [((2 * HD, D), BF)], ng, heads, got)
    pair = swap(pair, partner)
    (back,) = call(
        post_body,
        [((R, 2, HALF), BF)],
        pn, stat, ng, heads, got, pair,
        scratch=[pltpu.VMEM((D, R), F32)] * 2,
    )
    back = lax.all_to_all(back, "dp", 0, 0, tiled=True)
    enc, grad, qkv_share, out_share, gain_grad, bias_grad = call(
        final_body,
        [
            ((QW, R), BF),
            ((QW, R), BF),
            ((10, 3, 2, HD), F32),
            ((10, 2, HD), F32),
            ((1, 10), F32),
            ((1, 10), F32),
        ],
        send_order, back,
    )
    return (
        enc.T,
        grad.T,
        qkv_share.transpose(0, 2, 1, 3),
        out_share.transpose(1, 2, 0),
        gain_grad.reshape(10),
        bias_grad.reshape(10),
    )


def solution(mesh):
    return jax.shard_map(
        local,
        mesh=mesh,
        in_specs=(
            P("dp", None),
            P("dp", None),
            P("dp", None),
            P("dp", None),
            P("dp", None),
            P(),
            P(),
            P(None, "zero", None, None),
            P("zero", None, None),
        ),
        out_specs=(
            P("dp", "zero"),
            P("dp", "zero"),
            P("dp", "zero", None, None),
            P("zero", None, "dp"),
            P("dp"),
            P("dp"),
        ),
        check_vma=False,
    )
```

```python
import jax
import jax.numpy as jnp
from jax import lax
from jax.experimental import pallas as pl
from jax.experimental.pallas import tpu as pltpu
from jax.sharding import PartitionSpec as P

EPS = 1e-06
R = 128
D = 1280
HD = 80
HG = 2
NQ = HG * 3 * HD
NO = HG * HD
QW = D // 4
QP = 384
F32 = jnp.float32
BF = jnp.bfloat16
PN = 5 * R
PNE = PN + 48
SUMS = 20 * HD
WG = SUMS + 64
HALF = (WG + 2 * QW) // 2


def dg(a, b, ca, cb):
    return lax.dot_general(a, b, (((ca,), (cb,)), ((), ())), preferred_element_type=F32)


def call(body, outs, *args, scratch=()):
    vmem = pl.BlockSpec(memory_space=pltpu.VMEM)
    return pl.pallas_call(
        body,
        out_shape=tuple(jax.ShapeDtypeStruct(s, d) for s, d in outs),
        in_specs=[vmem] * len(args),
        out_specs=(vmem,) * len(outs),
        scratch_shapes=scratch,
        compiler_params=pltpu.CompilerParams(vmem_limit_bytes=16 * 1024 * 1024),
    )(*args)


def lane(shape):
    return lax.broadcasted_iota(jnp.int32, shape, 1)


def sub(shape):
    return lax.broadcasted_iota(jnp.int32, shape, 0)


def place_bits():
    dp = lax.axis_index("dp")
    core = lax.rem(dp, 2)
    return core, jnp.where(core == 0, lax.rem(dp // 2, 2), lax.rem(dp // 16, 2))


def partner(i):
    return i ^ (2 if i % 2 == 0 else 16)


def one_hot(cond):
    return cond.astype(F32).astype(BF)


def pair_picks(send_ref):
    spread = one_hot(lane((R, 2 * R)) // 2 == sub((R, 2 * R)))
    rows = jnp.broadcast_to(send_ref[...], (8, R)).astype(F32).astype(BF)
    target = dg(rows, spread, 1, 0)[0:1].astype(jnp.int32)
    hit = sub((R, 2 * R)) == target
    odd = lane((R, 2 * R)) % 2
    return one_hot(hit & (odd == 0)), one_hot(hit & (odd == 1))


def high_low(value):
    high = value.astype(BF).astype(F32)
    return [high, value - high]


def gather_body(
    send_ref, xg_ref, recv_ref, seg_ref, gain_ref, bias_ref, wo_ref,
    o_ref, odd_ref, same_ref, gain_out, bias_out, wo_out,
):
    even, odd = pair_picks(send_ref)
    odd_ref[...] = odd
    pick = jnp.concatenate([even, odd], axis=0)
    o_ref[...] = dg(pick, xg_ref[...], 0, 0).astype(BF).reshape(R, 2, D)
    hit = sub((R, R)) == recv_ref[...]
    seg = jnp.sum(jnp.where(hit, seg_ref[...], 0), axis=1, keepdims=True)
    group = one_hot(seg == lane((R, R)))
    same_ref[...] = dg(group, group, 1, 1)
    gain_out[...] = gain_ref[...].reshape(1, D)
    bias_out[...] = bias_ref[...].reshape(1, D)
    wo_out[...] = wo_ref[...]


def norm_stats(x):
    mean = jnp.mean(x, axis=1, keepdims=True)
    centred = x - mean
    inv = lax.rsqrt(jnp.mean(centred * centred, axis=1, keepdims=True) + EPS)
    return mean, inv, centred * inv


def block_body(
    xg_ref, same_ref, gain_ref, bias_ref, wo_ref, wq_ref,
    pn_ref, ng_ref, heads_ref, stat_ref,
):
    xg = xg_ref[...].reshape(2 * R, D)
    at = lane((R, 2 * R)) - 2 * sub((R, 2 * R))
    x = dg(one_hot(at == 0), xg, 1, 0)
    g32 = dg(one_hot(at == 1), xg, 1, 0)
    g = g32.astype(BF)
    ng_ref[R:, :] = g
    mean, inv, xh = norm_stats(x)
    normed = (xh * gain_ref[...] + bias_ref[...]).astype(BF)
    ng_ref[:R, :] = normed
    for i in range(4):

        @pl.when(lax.axis_index("zero") == i)
        def _(i=i):
            cols = slice(i * QW, (i + 1) * QW)
            pad = jnp.zeros((R, QP - QW), F32)
            both = jnp.concatenate([x[:, cols], pad, g32[:, cols], pad], axis=1).astype(BF)
            for t in range(6):
                heads_ref[(5 + t) * R : (6 + t) * R] = both[:, t * R : (t + 1) * R]
            line = jnp.concatenate([gain_ref[:, cols], jnp.zeros((1, QP - QW), F32)], axis=1)
            for t in range(3):
                stat_ref[R + t : R + t + 1] = line[:, t * R : (t + 1) * R]

    stat_ref[:R] = jnp.where(lane((R, R)) < 64, mean, inv)
    dh = dg(wo_ref[...], g, 1, 1).astype(BF)
    qkv = dg(wq_ref[...], normed, 1, 1).astype(BF)
    same = same_ref[...] > 0.5
    rows = []
    for h in range(HG):
        q = qkv[h * 3 * HD : h * 3 * HD + HD]
        k = qkv[h * 3 * HD + HD : h * 3 * HD + 2 * HD]
        v = qkv[h * 3 * HD + 2 * HD : (h + 1) * 3 * HD]
        dhh = dh[h * HD : (h + 1) * HD]
        s = jnp.where(same, dg(q, k, 0, 0) * (HD**-0.5), -1e30)
        e = jnp.exp(s - jnp.max(s, axis=1, keepdims=True))
        w = e / jnp.sum(e, axis=1, keepdims=True)
        w16 = w.astype(BF)
        pg = dg(dhh, v, 0, 0)
        delta = jnp.sum(pg * w, axis=1, keepdims=True)
        sg = (w * (pg - delta) * (HD**-0.5)).astype(BF)
        rows.append(dg(k, sg, 1, 1).astype(BF))
        rows.append(dg(q, sg, 1, 0).astype(BF))
        rows.append(dg(dhh, w16, 1, 0).astype(BF))
        rows.append(dg(v, w16, 1, 1).astype(BF))
    heads_ref[: 8 * HD] = jnp.concatenate(rows, axis=0)
    qg = jnp.concatenate(rows[0:3] + rows[4:7], axis=0)
    ho = jnp.concatenate([rows[3], rows[7]], axis=0)
    p = dg(ho, wo_ref[...], 0, 0)
    for i in range(4):
        for t in range(2):
            pn_ref[i, t * R : (t + 1) * R] = p[:, i * QW + t * R : i * QW + (t + 1) * R].astype(BF)
    n = dg(qg, wq_ref[...], 0, 0)
    u = n * gain_ref[...]
    m1 = jnp.sum(u, axis=1, keepdims=True) * (1.0 / D)
    m2 = jnp.sum(u * xh, axis=1, keepdims=True) * (1.0 / D)
    gain_row = jnp.sum(n * xh, axis=0, keepdims=True)
    bias_row = jnp.sum(n, axis=0, keepdims=True)
    extra = []
    for row in high_low(gain_row) + high_low(bias_row):
        extra += [row[:, t * R : (t + 1) * R] for t in range(10)]
    diagonal = sub((R, R)) == lane((R, R))
    for m in (m1, m2):
        extra += high_low(jnp.sum(jnp.where(diagonal, m, 0.0), axis=0, keepdims=True))
    extra.append(jnp.zeros((PNE - PN - 44, R), F32))
    extra = jnp.concatenate(extra, axis=0).astype(BF)
    for i in range(4):
        at = i * QW
        mixed = jnp.concatenate([p[:, at + 2 * R : at + QW], n[:, at : at + 64]], axis=1)
        pn_ref[i, 2 * R : 3 * R] = mixed.astype(BF)
        for t in range(2):
            cols = slice(at + 64 + t * R, at + 64 + (t + 1) * R)
            pn_ref[i, (3 + t) * R : (4 + t) * R] = n[:, cols].astype(BF)
        pn_ref[i, PN:] = extra


def other_body(ng_ref, heads_ref, send_ref):
    other = (1 - place_bits()[0]) * 4 * HD
    a = heads_ref[pl.ds(pl.multiple_of(other, 4 * HD), 3 * HD), :]
    b = heads_ref[pl.ds(pl.multiple_of(other + 3 * HD, HD), HD), :]
    send_ref[: 3 * HD, :] = dg(a, ng_ref[:R, :], 1, 0).astype(BF)
    send_ref[3 * HD :, :] = dg(b, ng_ref[R:, :], 1, 0).astype(BF)


def half_rows(c, half, ng_ref, heads_ref, got_ref):
    rows = heads_ref[pl.ds(pl.multiple_of((c * 2 + half) * 2 * HD, 2 * HD), 2 * HD), :]
    out = half.astype(F32) * (sub((2 * HD, R)) >= HD).astype(F32)
    rows = rows.astype(F32)
    left = jnp.concatenate([rows * (1.0 - out), rows * out], axis=1).astype(BF)
    got = got_ref[pl.ds(pl.multiple_of(half * 2 * HD, 2 * HD), 2 * HD), :]
    return dg(left, ng_ref[...], 1, 0) + got.astype(F32)


def pair_body(ng_ref, heads_ref, got_ref, send_ref):
    c, half = place_bits()
    send_ref[...] = half_rows(c, 1 - half, ng_ref, heads_ref, got_ref).astype(BF)


def weights_body(ng_ref, heads_ref, got_ref, pair_ref, o_ref, first_ref, second_ref):
    c, half = place_bits()
    wg = half_rows(c, half, ng_ref, heads_ref, got_ref) + pair_ref[...].astype(F32)
    first_ref[:, :HD] = wg[:HD].T
    second_ref[:, :HD] = wg[HD:].T
    slabs = []
    for i in range(10):
        rows = pl.ds(i, R, stride=10)
        slabs += [first_ref[rows, :][:, :HD], second_ref[rows, :][:, :HD]]
    slabs.append(jnp.zeros((R, 2 * HALF - SUMS), F32))
    row = jnp.concatenate(slabs, axis=1).astype(BF)
    both = jnp.concatenate([row[:, :HALF], row[:, HALF:]], axis=0)
    out = sub((2 * R, 2 * R))
    both = dg(one_hot(lane((2 * R, 2 * R)) == out // 2 + R * (out % 2)), both, 1, 0)
    o_ref[...] = both.astype(BF)


def post_body(pn_ref, stat_ref, heads_ref, wg_ref, o_ref, sum_ref):
    pn = jnp.sum(pn_ref[:, :PN].astype(F32), axis=0)
    extra = jnp.sum(pn_ref[:, PN:].astype(F32), axis=0)
    sums = [jnp.concatenate([extra[t : t + 1] for t in range(k, k + 10)], axis=1) for k in (0, 10, 20, 30)]
    rows = high_low(sums[0] + sums[1]) + high_low(sums[2] + sums[3])
    sum_ref[:, :8] = jnp.concatenate(rows + [jnp.zeros((4, D), F32)], axis=0).T
    sums = [sum_ref[pl.ds(i, R, stride=10), :][:, :4] for i in range(10)]
    tiles = [pn[t * R : (t + 1) * R] for t in range(5)]
    both = jnp.concatenate(tiles, axis=1)
    diagonal = sub((R, R)) == lane((R, R))
    m1 = jnp.sum(jnp.where(diagonal, extra[40:41] + extra[41:42], 0.0), axis=1, keepdims=True)
    m2 = jnp.sum(jnp.where(diagonal, extra[42:43] + extra[43:44], 0.0), axis=1, keepdims=True)
    quarters = [heads_ref[(5 + t) * R : (6 + t) * R].astype(F32) for t in range(6)]
    x = jnp.concatenate(quarters[:3], axis=1)[:, :QW]
    g = jnp.concatenate(quarters[3:], axis=1)[:, :QW]
    mean = stat_ref[:R, 0:1]
    inv = stat_ref[:R, 64:65]
    xh = (x - mean) * inv
    enc = x + both[:, :QW]
    gain = jnp.concatenate([stat_ref[R + t : R + t + 1] for t in range(3)], axis=1)[:, :QW]
    grad = both[:, QW:] * gain - m1 - xh * m2
    grad = g + inv * grad
    at = SUMS - HALF - 64
    gap = jnp.zeros((R, 64), F32)
    row = jnp.concatenate([gap] + sums + [gap[:, :24], enc, grad], axis=1).astype(BF)
    odd = one_hot(sub((2 * R, R)) == 2 * lane((2 * R, R)) + 1)
    tail = dg(odd, row, 1, 0) + wg_ref[:, at:].astype(F32)
    o_ref[...] = jnp.concatenate([wg_ref[:, :at], tail.astype(BF)], axis=1).reshape(R, 2, HALF)


def final_body(odd_ref, b_ref, e_ref, i_ref, a_ref, w_ref, gain_ref, bias_ref):
    back = b_ref[...].reshape(2 * R, HALF)
    rows = dg(back[:, WG - HALF :], odd_ref[...], 0, 1).astype(BF)
    e_ref[...] = rows[:QW]
    i_ref[...] = rows[QW:]
    row = sub((16, 2 * R))
    src = lane((16, 2 * R)) // 2
    half = jnp.where(src % 2 == 0, (src // 2) % 2, (src // 16) % 2)
    mask = (row == 2 * half + src % 2) | (row == 8)
    first = lane((16, 2 * R)) % 2 == 0
    sums = jnp.concatenate(
        [
            dg(one_hot(mask & first), back, 1, 0),
            dg(one_hot(mask & ~first), back[:, : WG - HALF], 1, 0),
        ],
        axis=1,
    )
    for i in range(10):
        at = i * 2 * HD
        a_ref[i, 0] = sums[0:2, at : at + HD]
        a_ref[i, 1] = sums[0:2, at + HD : at + 2 * HD]
        a_ref[i, 2] = sums[2:4, at : at + HD]
        w_ref[i] = sums[2:4, at + HD : at + 2 * HD]
        at = SUMS + 4 * i
        gain_ref[:, i : i + 1] = sums[8:9, at : at + 1] + sums[8:9, at + 1 : at + 2]
        bias_ref[:, i : i + 1] = sums[8:9, at + 2 : at + 3] + sums[8:9, at + 3 : at + 4]


def local(patches, cotangent, send_order, recv_order, segment_ids, ln_gain, ln_bias, w_qkv, w_out):
    wq = w_qkv.transpose(1, 2, 3, 0).reshape(NQ, D)
    wo = w_out.reshape(NO, D)

    def swap(a, other):
        return lax.ppermute(a, "dp", [(i, other(i)) for i in range(128)])

    xg = jnp.concatenate([patches, cotangent], axis=0)
    xg, odd, same, gain, bias, wo = call(
        gather_body,
        [((R, 2, D), BF), ((R, 2 * R), BF), ((R, R), F32), ((1, D), F32), ((1, D), F32), ((NO, D), BF)],
        send_order, xg, recv_order, segment_ids, ln_gain, ln_bias, wo,
    )
    xg = lax.all_to_all(xg, "dp", 0, 0, tiled=True)
    pn, ng, heads, stat = call(
        block_body,
        [
            ((4, PNE, R), BF),
            ((2 * R, D), BF),
            ((8 * HD + 6 * R, R), BF),
            ((R + 8, R), F32),
        ],
        xg, same, gain, bias, wo, wq,
    )
    (send,) = call(other_body, [((4 * HD, D), BF)], ng, heads)
    got = swap(send, lambda i: i ^ 1)
    pn = lax.all_to_all(pn, "zero", 0, 0, tiled=True)
    (pair,) = call(pair_body, [((2 * HD, D), BF)], ng, heads, got)
    pair = swap(pair, partner)
    scratch = pltpu.VMEM((D, R), F32)
    (wg,) = call(
        weights_body, [((2 * R, HALF), BF)], ng, heads, got, pair, scratch=[scratch] * 2
    )
    (back,) = call(
        post_body, [((R, 2, HALF), BF)], pn, stat, heads, wg, scratch=[scratch]
    )
    back = lax.all_to_all(back, "dp", 0, 0, tiled=True)
    enc, grad, qkv_share, out_share, gain_grad, bias_grad = call(
        final_body,
        [
            ((QW, R), BF),
            ((QW, R), BF),
            ((10, 3, 2, HD), F32),
            ((10, 2, HD), F32),
            ((1, 10), F32),
            ((1, 10), F32),
        ],
        odd, back,
    )
    return (
        enc.T,
        grad.T,
        qkv_share.transpose(0, 2, 1, 3),
        out_share.transpose(1, 2, 0),
        gain_grad.reshape(10),
        bias_grad.reshape(10),
    )


def solution(mesh):
    return jax.shard_map(
        local,
        mesh=mesh,
        in_specs=(
            P("dp", None),
            P("dp", None),
            P("dp", None),
            P("dp", None),
            P("dp", None),
            P(),
            P(),
            P(None, "zero", None, None),
            P("zero", None, None),
        ),
        out_specs=(
            P("dp", "zero"),
            P("dp", "zero"),
            P("dp", "zero", None, None),
            P("zero", None, "dp"),
            P("dp"),
            P("dp"),
        ),
        check_vma=False,
    )
```

```python
import jax
import jax.numpy as jnp
from jax import lax
from jax.experimental import pallas as pl
from jax.experimental.pallas import tpu as pltpu
from jax.sharding import PartitionSpec as P

EPS = 1e-06
R = 128
D = 1280
HD = 80
HG = 2
NQ = HG * 3 * HD
NO = HG * HD
QW = D // 4
QP = 384
F32 = jnp.float32
BF = jnp.bfloat16
PN = 5 * R
PNE = PN + 48
SUMS = 20 * HD
WG = SUMS + 64
HALF = (WG + 2 * QW) // 2


def dg(a, b, ca, cb):
    return lax.dot_general(a, b, (((ca,), (cb,)), ((), ())), preferred_element_type=F32)


def call(body, outs, *args, scratch=()):
    vmem = pl.BlockSpec(memory_space=pltpu.VMEM)
    return pl.pallas_call(
        body,
        out_shape=tuple(jax.ShapeDtypeStruct(s, d) for s, d in outs),
        in_specs=[vmem] * len(args),
        out_specs=(vmem,) * len(outs),
        scratch_shapes=scratch,
        compiler_params=pltpu.CompilerParams(vmem_limit_bytes=16 * 1024 * 1024),
    )(*args)


def lane(shape):
    return lax.broadcasted_iota(jnp.int32, shape, 1)


def sub(shape):
    return lax.broadcasted_iota(jnp.int32, shape, 0)


def place_bits():
    dp = lax.axis_index("dp")
    core = lax.rem(dp, 2)
    return core, jnp.where(core == 0, lax.rem(dp // 2, 2), lax.rem(dp // 16, 2))


def partner(i):
    return i ^ (2 if i % 2 == 0 else 16)


def one_hot(cond):
    return cond.astype(F32).astype(BF)


def pair_picks(send_ref):
    spread = one_hot(lane((R, 2 * R)) // 2 == sub((R, 2 * R)))
    rows = jnp.broadcast_to(send_ref[...], (8, R)).astype(F32).astype(BF)
    target = dg(rows, spread, 1, 0)[0:1].astype(jnp.int32)
    hit = sub((R, 2 * R)) == target
    odd = lane((R, 2 * R)) % 2
    return one_hot(hit & (odd == 0)), one_hot(hit & (odd == 1))


def high_low(value):
    high = value.astype(BF).astype(F32)
    return [high, value - high]


def gather_body(
    send_ref, xg_ref, recv_ref, seg_ref, gain_ref, bias_ref, wo_ref,
    o_ref, odd_ref, same_ref, gain_out, bias_out, wo_out,
):
    even, odd = pair_picks(send_ref)
    odd_ref[...] = odd
    pick = jnp.concatenate([even, odd], axis=0)
    o_ref[...] = dg(pick, xg_ref[...], 0, 0).astype(BF).reshape(R, 2, D)
    hit = sub((R, R)) == recv_ref[...]
    seg = jnp.sum(jnp.where(hit, seg_ref[...], 0), axis=1, keepdims=True)
    group = one_hot(seg == lane((R, R)))
    same_ref[...] = dg(group, group, 1, 1)
    gain_out[...] = gain_ref[...].reshape(1, D)
    bias_out[...] = bias_ref[...].reshape(1, D)
    wo_out[...] = wo_ref[...]


def norm_stats(x):
    mean = jnp.mean(x, axis=1, keepdims=True)
    centred = x - mean
    inv = lax.rsqrt(jnp.mean(centred * centred, axis=1, keepdims=True) + EPS)
    return mean, inv, centred * inv


def block_body(
    xg_ref, same_ref, gain_ref, bias_ref, wo_ref, wq_ref,
    pn_ref, ng_ref, heads_ref, stat_ref,
):
    xg = xg_ref[...].reshape(2 * R, D)
    at = lane((R, 2 * R)) - 2 * sub((R, 2 * R))
    x = dg(one_hot(at == 0), xg, 1, 0)
    g32 = dg(one_hot(at == 1), xg, 1, 0)
    g = g32.astype(BF)
    dh = dg(wo_ref[...], g, 1, 1).astype(BF)
    ng_ref[R:, :] = g
    mean, inv, xh = norm_stats(x)
    normed = (xh * gain_ref[...] + bias_ref[...]).astype(BF)
    ng_ref[:R, :] = normed
    for i in range(4):

        @pl.when(lax.axis_index("zero") == i)
        def _(i=i):
            cols = slice(i * QW, (i + 1) * QW)
            pad = jnp.zeros((R, QP - QW), F32)
            both = jnp.concatenate([x[:, cols], pad, g32[:, cols], pad], axis=1).astype(BF)
            for t in range(6):
                heads_ref[(5 + t) * R : (6 + t) * R] = both[:, t * R : (t + 1) * R]
            line = jnp.concatenate([gain_ref[:, cols], jnp.zeros((1, QP - QW), F32)], axis=1)
            for t in range(3):
                stat_ref[R + t : R + t + 1] = line[:, t * R : (t + 1) * R]

    stat_ref[:R] = jnp.where(lane((R, R)) < 64, mean, inv)
    qkv = dg(wq_ref[...], normed, 1, 1).astype(BF)
    same = same_ref[...] > 0.5
    heads = range(HG)
    q = [qkv[h * 3 * HD : h * 3 * HD + HD] for h in heads]
    k = [qkv[h * 3 * HD + HD : h * 3 * HD + 2 * HD] for h in heads]
    v = [qkv[h * 3 * HD + 2 * HD : (h + 1) * 3 * HD] for h in heads]
    dhh = [dh[h * HD : (h + 1) * HD] for h in heads]
    s = [dg(q[h], k[h], 0, 0) for h in heads]
    pg = [dg(dhh[h], v[h], 0, 0) for h in heads]
    s = [jnp.where(same, s[h] * (HD**-0.5), -1e30) for h in heads]
    e = [jnp.exp(s[h] - jnp.max(s[h], axis=1, keepdims=True)) for h in heads]
    w = [e[h] / jnp.sum(e[h], axis=1, keepdims=True) for h in heads]
    w16 = [w[h].astype(BF) for h in heads]
    delta = [jnp.sum(pg[h] * w[h], axis=1, keepdims=True) for h in heads]
    sg = [(w[h] * (pg[h] - delta[h]) * (HD**-0.5)).astype(BF) for h in heads]
    ho = [dg(v[h], w16[h], 1, 1).astype(BF) for h in heads]
    dv = [dg(dhh[h], w16[h], 1, 0).astype(BF) for h in heads]
    dq = [dg(k[h], sg[h], 1, 1).astype(BF) for h in heads]
    dk = [dg(q[h], sg[h], 1, 0).astype(BF) for h in heads]
    rows = [part for h in heads for part in (dq[h], dk[h], dv[h], ho[h])]
    heads_ref[: 8 * HD] = jnp.concatenate(rows, axis=0)
    qg = jnp.concatenate(rows[0:3] + rows[4:7], axis=0)
    ho = jnp.concatenate([rows[3], rows[7]], axis=0)
    p = dg(ho, wo_ref[...], 0, 0)
    for i in range(4):
        for t in range(2):
            pn_ref[i, t * R : (t + 1) * R] = p[:, i * QW + t * R : i * QW + (t + 1) * R].astype(BF)
    n = dg(qg, wq_ref[...], 0, 0)
    u = n * gain_ref[...]
    m1 = jnp.sum(u, axis=1, keepdims=True) * (1.0 / D)
    m2 = jnp.sum(u * xh, axis=1, keepdims=True) * (1.0 / D)
    gain_row = jnp.sum(n * xh, axis=0, keepdims=True)
    bias_row = jnp.sum(n, axis=0, keepdims=True)
    extra = []
    for row in high_low(gain_row) + high_low(bias_row):
        extra += [row[:, t * R : (t + 1) * R] for t in range(10)]
    diagonal = sub((R, R)) == lane((R, R))
    for m in (m1, m2):
        extra += high_low(jnp.sum(jnp.where(diagonal, m, 0.0), axis=0, keepdims=True))
    extra.append(jnp.zeros((PNE - PN - 44, R), F32))
    extra = jnp.concatenate(extra, axis=0).astype(BF)
    for i in range(4):
        at = i * QW
        mixed = jnp.concatenate([p[:, at + 2 * R : at + QW], n[:, at : at + 64]], axis=1)
        pn_ref[i, 2 * R : 3 * R] = mixed.astype(BF)
        for t in range(2):
            cols = slice(at + 64 + t * R, at + 64 + (t + 1) * R)
            pn_ref[i, (3 + t) * R : (4 + t) * R] = n[:, cols].astype(BF)
        pn_ref[i, PN:] = extra


def other_body(ng_ref, heads_ref, send_ref):
    other = (1 - place_bits()[0]) * 4 * HD
    a = heads_ref[pl.ds(pl.multiple_of(other, 4 * HD), 3 * HD), :]
    b = heads_ref[pl.ds(pl.multiple_of(other + 3 * HD, HD), HD), :]
    send_ref[: 3 * HD, :] = dg(a, ng_ref[:R, :], 1, 0).astype(BF)
    send_ref[3 * HD :, :] = dg(b, ng_ref[R:, :], 1, 0).astype(BF)


def half_rows(c, half, ng_ref, heads_ref, got_ref):
    rows = heads_ref[pl.ds(pl.multiple_of((c * 2 + half) * 2 * HD, 2 * HD), 2 * HD), :]
    out = half.astype(F32) * (sub((2 * HD, R)) >= HD).astype(F32)
    rows = rows.astype(F32)
    left = jnp.concatenate([rows * (1.0 - out), rows * out], axis=1).astype(BF)
    got = got_ref[pl.ds(pl.multiple_of(half * 2 * HD, 2 * HD), 2 * HD), :]
    return dg(left, ng_ref[...], 1, 0) + got.astype(F32)


def pair_body(ng_ref, heads_ref, got_ref, send_ref):
    c, half = place_bits()
    send_ref[...] = half_rows(c, 1 - half, ng_ref, heads_ref, got_ref).astype(BF)


def weights_body(ng_ref, heads_ref, got_ref, pair_ref, o_ref, first_ref, second_ref):
    c, half = place_bits()
    wg = half_rows(c, half, ng_ref, heads_ref, got_ref) + pair_ref[...].astype(F32)
    first_ref[:, :HD] = wg[:HD].T
    second_ref[:, :HD] = wg[HD:].T
    slabs = []
    for i in range(10):
        rows = pl.ds(i, R, stride=10)
        slabs += [first_ref[rows, :][:, :HD], second_ref[rows, :][:, :HD]]
    slabs.append(jnp.zeros((R, 2 * HALF - SUMS), F32))
    row = jnp.concatenate(slabs, axis=1).astype(BF)
    both = jnp.concatenate([row[:, :HALF], row[:, HALF:]], axis=0)
    out = sub((2 * R, 2 * R))
    both = dg(one_hot(lane((2 * R, 2 * R)) == out // 2 + R * (out % 2)), both, 1, 0)
    o_ref[...] = both.astype(BF)


def post_body(pn_ref, stat_ref, heads_ref, wg_ref, o_ref, sum_ref):
    pn = jnp.sum(pn_ref[:, :PN].astype(F32), axis=0)
    extra = jnp.sum(pn_ref[:, PN:].astype(F32), axis=0)
    sums = [jnp.concatenate([extra[t : t + 1] for t in range(k, k + 10)], axis=1) for k in (0, 10, 20, 30)]
    rows = high_low(sums[0] + sums[1]) + high_low(sums[2] + sums[3])
    sum_ref[:, :8] = jnp.concatenate(rows + [jnp.zeros((4, D), F32)], axis=0).T
    sums = [sum_ref[pl.ds(i, R, stride=10), :][:, :4] for i in range(10)]
    tiles = [pn[t * R : (t + 1) * R] for t in range(5)]
    both = jnp.concatenate(tiles, axis=1)
    diagonal = sub((R, R)) == lane((R, R))
    m1 = jnp.sum(jnp.where(diagonal, extra[40:41] + extra[41:42], 0.0), axis=1, keepdims=True)
    m2 = jnp.sum(jnp.where(diagonal, extra[42:43] + extra[43:44], 0.0), axis=1, keepdims=True)
    quarters = [heads_ref[(5 + t) * R : (6 + t) * R].astype(F32) for t in range(6)]
    x = jnp.concatenate(quarters[:3], axis=1)[:, :QW]
    g = jnp.concatenate(quarters[3:], axis=1)[:, :QW]
    mean = stat_ref[:R, 0:1]
    inv = stat_ref[:R, 64:65]
    xh = (x - mean) * inv
    enc = x + both[:, :QW]
    gain = jnp.concatenate([stat_ref[R + t : R + t + 1] for t in range(3)], axis=1)[:, :QW]
    grad = both[:, QW:] * gain - m1 - xh * m2
    grad = g + inv * grad
    at = SUMS - HALF - 64
    gap = jnp.zeros((R, 64), F32)
    row = jnp.concatenate([gap] + sums + [gap[:, :24], enc, grad], axis=1).astype(BF)
    odd = one_hot(sub((2 * R, R)) == 2 * lane((2 * R, R)) + 1)
    tail = dg(odd, row, 1, 0) + wg_ref[:, at:].astype(F32)
    o_ref[...] = jnp.concatenate([wg_ref[:, :at], tail.astype(BF)], axis=1).reshape(R, 2, HALF)


def final_body(odd_ref, b_ref, e_ref, i_ref, a_ref, w_ref, gain_ref, bias_ref):
    back = b_ref[...].reshape(2 * R, HALF)
    rows = dg(back[:, WG - HALF :], odd_ref[...], 0, 1).astype(BF)
    e_ref[...] = rows[:QW]
    i_ref[...] = rows[QW:]
    row = sub((16, 2 * R))
    src = lane((16, 2 * R)) // 2
    half = jnp.where(src % 2 == 0, (src // 2) % 2, (src // 16) % 2)
    mask = (row == 2 * half + src % 2) | (row == 8)
    first = lane((16, 2 * R)) % 2 == 0
    sums = jnp.concatenate(
        [
            dg(one_hot(mask & first), back, 1, 0),
            dg(one_hot(mask & ~first), back[:, : WG - HALF], 1, 0),
        ],
        axis=1,
    )
    for i in range(10):
        at = i * 2 * HD
        a_ref[i, 0] = sums[0:2, at : at + HD]
        a_ref[i, 1] = sums[0:2, at + HD : at + 2 * HD]
        a_ref[i, 2] = sums[2:4, at : at + HD]
        w_ref[i] = sums[2:4, at + HD : at + 2 * HD]
        at = SUMS + 4 * i
        gain_ref[:, i : i + 1] = sums[8:9, at : at + 1] + sums[8:9, at + 1 : at + 2]
        bias_ref[:, i : i + 1] = sums[8:9, at + 2 : at + 3] + sums[8:9, at + 3 : at + 4]


def local(patches, cotangent, send_order, recv_order, segment_ids, ln_gain, ln_bias, w_qkv, w_out):
    wq = w_qkv.transpose(1, 2, 3, 0).reshape(NQ, D)
    wo = w_out.reshape(NO, D)

    def swap(a, other):
        return lax.ppermute(a, "dp", [(i, other(i)) for i in range(128)])

    xg = jnp.concatenate([patches, cotangent], axis=0)
    xg, odd, same, gain, bias, wo = call(
        gather_body,
        [((R, 2, D), BF), ((R, 2 * R), BF), ((R, R), F32), ((1, D), F32), ((1, D), F32), ((NO, D), BF)],
        send_order, xg, recv_order, segment_ids, ln_gain, ln_bias, wo,
    )
    xg = lax.all_to_all(xg, "dp", 0, 0, tiled=True)
    pn, ng, heads, stat = call(
        block_body,
        [
            ((4, PNE, R), BF),
            ((2 * R, D), BF),
            ((8 * HD + 6 * R, R), BF),
            ((R + 8, R), F32),
        ],
        xg, same, gain, bias, wo, wq,
    )
    (send,) = call(other_body, [((4 * HD, D), BF)], ng, heads)
    got = swap(send, lambda i: i ^ 1)
    pn = lax.all_to_all(pn, "zero", 0, 0, tiled=True)
    (pair,) = call(pair_body, [((2 * HD, D), BF)], ng, heads, got)
    pair = swap(pair, partner)
    scratch = pltpu.VMEM((D, R), F32)
    (wg,) = call(
        weights_body, [((2 * R, HALF), BF)], ng, heads, got, pair, scratch=[scratch] * 2
    )
    (back,) = call(
        post_body, [((R, 2, HALF), BF)], pn, stat, heads, wg, scratch=[scratch]
    )
    back = lax.all_to_all(back, "dp", 0, 0, tiled=True)
    enc, grad, qkv_share, out_share, gain_grad, bias_grad = call(
        final_body,
        [
            ((QW, R), BF),
            ((QW, R), BF),
            ((10, 3, 2, HD), F32),
            ((10, 2, HD), F32),
            ((1, 10), F32),
            ((1, 10), F32),
        ],
        odd, back,
    )
    return (
        enc.T,
        grad.T,
        qkv_share.transpose(0, 2, 1, 3),
        out_share.transpose(1, 2, 0),
        gain_grad.reshape(10),
        bias_grad.reshape(10),
    )


def solution(mesh):
    return jax.shard_map(
        local,
        mesh=mesh,
        in_specs=(
            P("dp", None),
            P("dp", None),
            P("dp", None),
            P("dp", None),
            P("dp", None),
            P(),
            P(),
            P(None, "zero", None, None),
            P("zero", None, None),
        ),
        out_specs=(
            P("dp", "zero"),
            P("dp", "zero"),
            P("dp", "zero", None, None),
            P("zero", None, "dp"),
            P("dp"),
            P("dp"),
        ),
        check_vma=False,
    )
```

```python
import jax
import jax.numpy as jnp
from jax import lax
from jax.experimental import pallas as pl
from jax.experimental.pallas import tpu as pltpu
from jax.sharding import PartitionSpec as P

EPS = 1e-06
R = 128
D = 1280
HD = 80
HG = 2
NQ = HG * 3 * HD
NO = HG * HD
QW = D // 4
QP = 384
F32 = jnp.float32
BF = jnp.bfloat16
PN = 5 * R
PNE = PN + 48
SUMS = 20 * HD
WG = SUMS + 64
HALF = (WG + 2 * QW) // 2


def dg(a, b, ca, cb):
    return lax.dot_general(a, b, (((ca,), (cb,)), ((), ())), preferred_element_type=F32)


def call(body, outs, *args, scratch=()):
    vmem = pl.BlockSpec(memory_space=pltpu.VMEM)
    return pl.pallas_call(
        body,
        out_shape=tuple(jax.ShapeDtypeStruct(s, d) for s, d in outs),
        in_specs=[vmem] * len(args),
        out_specs=(vmem,) * len(outs),
        scratch_shapes=scratch,
        compiler_params=pltpu.CompilerParams(vmem_limit_bytes=16 * 1024 * 1024),
    )(*args)


def lane(shape):
    return lax.broadcasted_iota(jnp.int32, shape, 1)


def sub(shape):
    return lax.broadcasted_iota(jnp.int32, shape, 0)


def place_bits():
    dp = lax.axis_index("dp")
    core = lax.rem(dp, 2)
    return core, jnp.where(core == 0, lax.rem(dp // 2, 2), lax.rem(dp // 16, 2))


def partner(i):
    return i ^ (2 if i % 2 == 0 else 16)


def one_hot(cond):
    return cond.astype(F32).astype(BF)


def pair_picks(send_ref):
    spread = one_hot(lane((R, 2 * R)) // 2 == sub((R, 2 * R)))
    rows = jnp.broadcast_to(send_ref[...], (8, R)).astype(F32).astype(BF)
    target = dg(rows, spread, 1, 0)[0:1].astype(jnp.int32)
    hit = sub((R, 2 * R)) == target
    odd = lane((R, 2 * R)) % 2
    return one_hot(hit & (odd == 0)), one_hot(hit & (odd == 1))


def high_low(value):
    high = value.astype(BF).astype(F32)
    return [high, value - high]


def gather_body(
    send_ref, xg_ref, recv_ref, seg_ref, gain_ref, bias_ref, wo_ref,
    o_ref, odd_ref, same_ref, gain_out, bias_out, wo_out,
):
    even, odd = pair_picks(send_ref)
    odd_ref[...] = odd
    pick = jnp.concatenate([even, odd], axis=0)
    o_ref[...] = dg(pick, xg_ref[...], 0, 0).astype(BF).reshape(R, 2, D)
    hit = sub((R, R)) == recv_ref[...]
    seg = jnp.sum(jnp.where(hit, seg_ref[...], 0), axis=1, keepdims=True)
    group = one_hot(seg == lane((R, R)))
    same_ref[...] = dg(group, group, 1, 1)
    gain_out[...] = gain_ref[...].reshape(1, D)
    bias_out[...] = bias_ref[...].reshape(1, D)
    wo_out[...] = wo_ref[...]


def norm_stats(x):
    mean = jnp.mean(x, axis=1, keepdims=True)
    centred = x - mean
    inv = lax.rsqrt(jnp.mean(centred * centred, axis=1, keepdims=True) + EPS)
    return mean, inv, centred * inv


def block_body(
    xg_ref, same_ref, gain_ref, bias_ref, wo_ref, wq_ref,
    pn_ref, ng_ref, heads_ref, stat_ref,
):
    xg = xg_ref[...].reshape(2 * R, D)
    at = lane((R, 2 * R)) - 2 * sub((R, 2 * R))
    x = dg(one_hot(at == 0), xg, 1, 0)
    g32 = dg(one_hot(at == 1), xg, 1, 0)
    g = g32.astype(BF)
    dh = dg(wo_ref[...], g, 1, 1).astype(BF)
    ng_ref[R:, :] = g
    mean, inv, xh = norm_stats(x)
    normed = (xh * gain_ref[...] + bias_ref[...]).astype(BF)
    ng_ref[:R, :] = normed
    for i in range(4):

        @pl.when(lax.axis_index("zero") == i)
        def _(i=i):
            cols = slice(i * QW, (i + 1) * QW)
            pad = jnp.zeros((R, QP - QW), F32)
            both = jnp.concatenate([x[:, cols], pad, g32[:, cols], pad], axis=1).astype(BF)
            for t in range(6):
                heads_ref[(5 + t) * R : (6 + t) * R] = both[:, t * R : (t + 1) * R]
            line = jnp.concatenate([gain_ref[:, cols], jnp.zeros((1, QP - QW), F32)], axis=1)
            for t in range(3):
                stat_ref[R + t : R + t + 1] = line[:, t * R : (t + 1) * R]

    stat_ref[:R] = jnp.where(lane((R, R)) < 64, mean, inv)
    qkv = dg(wq_ref[...], normed, 1, 1).astype(BF)
    same = same_ref[...] > 0.5
    heads = range(HG)
    q = [qkv[h * 3 * HD : h * 3 * HD + HD] for h in heads]
    k = [qkv[h * 3 * HD + HD : h * 3 * HD + 2 * HD] for h in heads]
    v = [qkv[h * 3 * HD + 2 * HD : (h + 1) * 3 * HD] for h in heads]
    dhh = [dh[h * HD : (h + 1) * HD] for h in heads]
    s = [dg(q[h], k[h], 0, 0) for h in heads]
    pg = [dg(dhh[h], v[h], 0, 0) for h in heads]
    s = [jnp.where(same, s[h] * (HD**-0.5), -1e30) for h in heads]
    e = [jnp.exp(s[h] - jnp.max(s[h], axis=1, keepdims=True)) for h in heads]
    w = [e[h] / jnp.sum(e[h], axis=1, keepdims=True) for h in heads]
    w16 = [w[h].astype(BF) for h in heads]
    delta = [jnp.sum(pg[h] * w[h], axis=1, keepdims=True) for h in heads]
    sg = [(w[h] * (pg[h] - delta[h]) * (HD**-0.5)).astype(BF) for h in heads]
    ho = [dg(v[h], w16[h], 1, 1).astype(BF) for h in heads]
    dv = [dg(dhh[h], w16[h], 1, 0).astype(BF) for h in heads]
    dq = [dg(k[h], sg[h], 1, 1).astype(BF) for h in heads]
    dk = [dg(q[h], sg[h], 1, 0).astype(BF) for h in heads]
    rows = [part for h in heads for part in (dq[h], dk[h], dv[h], ho[h])]
    heads_ref[: 8 * HD] = jnp.concatenate(rows, axis=0)
    qg = jnp.concatenate(rows[0:3] + rows[4:7], axis=0)
    ho = jnp.concatenate([rows[3], rows[7]], axis=0)
    p = dg(ho, wo_ref[...], 0, 0)
    for i in range(4):
        for t in range(2):
            pn_ref[i, t * R : (t + 1) * R] = p[:, i * QW + t * R : i * QW + (t + 1) * R].astype(BF)
    n = dg(qg, wq_ref[...], 0, 0)
    u = n * gain_ref[...]
    m1 = jnp.sum(u, axis=1, keepdims=True) * (1.0 / D)
    m2 = jnp.sum(u * xh, axis=1, keepdims=True) * (1.0 / D)
    gain_row = jnp.sum(n * xh, axis=0, keepdims=True)
    bias_row = jnp.sum(n, axis=0, keepdims=True)
    extra = []
    for row in high_low(gain_row) + high_low(bias_row):
        extra += [row[:, t * R : (t + 1) * R] for t in range(10)]
    diagonal = sub((R, R)) == lane((R, R))
    for m in (m1, m2):
        extra += high_low(jnp.sum(jnp.where(diagonal, m, 0.0), axis=0, keepdims=True))
    extra.append(jnp.zeros((PNE - PN - 44, R), F32))
    extra = jnp.concatenate(extra, axis=0).astype(BF)
    for i in range(4):
        at = i * QW
        mixed = jnp.concatenate([p[:, at + 2 * R : at + QW], n[:, at : at + 64]], axis=1)
        pn_ref[i, 2 * R : 3 * R] = mixed.astype(BF)
        for t in range(2):
            cols = slice(at + 64 + t * R, at + 64 + (t + 1) * R)
            pn_ref[i, (3 + t) * R : (4 + t) * R] = n[:, cols].astype(BF)
        pn_ref[i, PN:] = extra


def other_body(ng_ref, heads_ref, send_ref):
    other = (1 - place_bits()[0]) * 4 * HD
    a = heads_ref[pl.ds(pl.multiple_of(other, 4 * HD), 3 * HD), :]
    b = heads_ref[pl.ds(pl.multiple_of(other + 3 * HD, HD), HD), :]
    send_ref[: 3 * HD, :] = dg(a, ng_ref[:R, :], 1, 0).astype(BF)
    send_ref[3 * HD :, :] = dg(b, ng_ref[R:, :], 1, 0).astype(BF)


def half_rows(c, half, ng_ref, heads_ref, got_ref):
    rows = heads_ref[pl.ds(pl.multiple_of((c * 2 + half) * 2 * HD, 2 * HD), 2 * HD), :]
    out = half.astype(F32) * (sub((2 * HD, R)) >= HD).astype(F32)
    rows = rows.astype(F32)
    left = jnp.concatenate([rows * (1.0 - out), rows * out], axis=1).astype(BF)
    got = got_ref[pl.ds(pl.multiple_of(half * 2 * HD, 2 * HD), 2 * HD), :]
    return dg(left, ng_ref[...], 1, 0) + got.astype(F32)


def pair_body(ng_ref, heads_ref, got_ref, send_ref):
    c, half = place_bits()
    send_ref[...] = half_rows(c, 1 - half, ng_ref, heads_ref, got_ref).astype(BF)


def own_body(ng_ref, heads_ref, got_ref, own_ref):
    c, half = place_bits()
    own_ref[...] = half_rows(c, half, ng_ref, heads_ref, got_ref)


def weights_body(own_ref, pair_ref, o_ref, first_ref, second_ref):
    wg = own_ref[...] + pair_ref[...].astype(F32)
    first_ref[:, :HD] = wg[:HD].T
    second_ref[:, :HD] = wg[HD:].T
    slabs = []
    for i in range(10):
        rows = pl.ds(i, R, stride=10)
        slabs += [first_ref[rows, :][:, :HD], second_ref[rows, :][:, :HD]]
    slabs.append(jnp.zeros((R, 2 * HALF - SUMS), F32))
    row = jnp.concatenate(slabs, axis=1).astype(BF)
    both = jnp.concatenate([row[:, :HALF], row[:, HALF:]], axis=0)
    out = sub((2 * R, 2 * R))
    both = dg(one_hot(lane((2 * R, 2 * R)) == out // 2 + R * (out % 2)), both, 1, 0)
    o_ref[...] = both.astype(BF)


def post_body(pn_ref, stat_ref, heads_ref, wg_ref, o_ref, sum_ref):
    pn = jnp.sum(pn_ref[:, :PN].astype(F32), axis=0)
    extra = jnp.sum(pn_ref[:, PN:].astype(F32), axis=0)
    sums = [jnp.concatenate([extra[t : t + 1] for t in range(k, k + 10)], axis=1) for k in (0, 10, 20, 30)]
    rows = high_low(sums[0] + sums[1]) + high_low(sums[2] + sums[3])
    sum_ref[:, :8] = jnp.concatenate(rows + [jnp.zeros((4, D), F32)], axis=0).T
    sums = [sum_ref[pl.ds(i, R, stride=10), :][:, :4] for i in range(10)]
    tiles = [pn[t * R : (t + 1) * R] for t in range(5)]
    both = jnp.concatenate(tiles, axis=1)
    diagonal = sub((R, R)) == lane((R, R))
    m1 = jnp.sum(jnp.where(diagonal, extra[40:41] + extra[41:42], 0.0), axis=1, keepdims=True)
    m2 = jnp.sum(jnp.where(diagonal, extra[42:43] + extra[43:44], 0.0), axis=1, keepdims=True)
    quarters = [heads_ref[(5 + t) * R : (6 + t) * R].astype(F32) for t in range(6)]
    x = jnp.concatenate(quarters[:3], axis=1)[:, :QW]
    g = jnp.concatenate(quarters[3:], axis=1)[:, :QW]
    mean = stat_ref[:R, 0:1]
    inv = stat_ref[:R, 64:65]
    xh = (x - mean) * inv
    enc = x + both[:, :QW]
    gain = jnp.concatenate([stat_ref[R + t : R + t + 1] for t in range(3)], axis=1)[:, :QW]
    grad = both[:, QW:] * gain - m1 - xh * m2
    grad = g + inv * grad
    at = SUMS - HALF - 64
    gap = jnp.zeros((R, 64), F32)
    row = jnp.concatenate([gap] + sums + [gap[:, :24], enc, grad], axis=1).astype(BF)
    odd = one_hot(sub((2 * R, R)) == 2 * lane((2 * R, R)) + 1)
    tail = dg(odd, row, 1, 0) + wg_ref[:, at:].astype(F32)
    o_ref[...] = jnp.concatenate([wg_ref[:, :at], tail.astype(BF)], axis=1).reshape(R, 2, HALF)


def final_body(odd_ref, b_ref, e_ref, i_ref, a_ref, w_ref, gain_ref, bias_ref):
    back = b_ref[...].reshape(2 * R, HALF)
    rows = dg(back[:, WG - HALF :], odd_ref[...], 0, 1).astype(BF)
    e_ref[...] = rows[:QW]
    i_ref[...] = rows[QW:]
    row = sub((16, 2 * R))
    src = lane((16, 2 * R)) // 2
    half = jnp.where(src % 2 == 0, (src // 2) % 2, (src // 16) % 2)
    mask = (row == 2 * half + src % 2) | (row == 8)
    first = lane((16, 2 * R)) % 2 == 0
    sums = jnp.concatenate(
        [
            dg(one_hot(mask & first), back, 1, 0),
            dg(one_hot(mask & ~first), back[:, : WG - HALF], 1, 0),
        ],
        axis=1,
    )
    for i in range(10):
        at = i * 2 * HD
        a_ref[i, 0] = sums[0:2, at : at + HD]
        a_ref[i, 1] = sums[0:2, at + HD : at + 2 * HD]
        a_ref[i, 2] = sums[2:4, at : at + HD]
        w_ref[i] = sums[2:4, at + HD : at + 2 * HD]
        at = SUMS + 4 * i
        gain_ref[:, i : i + 1] = sums[8:9, at : at + 1] + sums[8:9, at + 1 : at + 2]
        bias_ref[:, i : i + 1] = sums[8:9, at + 2 : at + 3] + sums[8:9, at + 3 : at + 4]


def local(patches, cotangent, send_order, recv_order, segment_ids, ln_gain, ln_bias, w_qkv, w_out):
    wq = w_qkv.transpose(1, 2, 3, 0).reshape(NQ, D)
    wo = w_out.reshape(NO, D)

    def swap(a, other):
        return lax.ppermute(a, "dp", [(i, other(i)) for i in range(128)])

    xg = jnp.concatenate([patches, cotangent], axis=0)
    xg, odd, same, gain, bias, wo = call(
        gather_body,
        [((R, 2, D), BF), ((R, 2 * R), BF), ((R, R), F32), ((1, D), F32), ((1, D), F32), ((NO, D), BF)],
        send_order, xg, recv_order, segment_ids, ln_gain, ln_bias, wo,
    )
    xg = lax.all_to_all(xg, "dp", 0, 0, tiled=True)
    pn, ng, heads, stat = call(
        block_body,
        [
            ((4, PNE, R), BF),
            ((2 * R, D), BF),
            ((8 * HD + 6 * R, R), BF),
            ((R + 8, R), F32),
        ],
        xg, same, gain, bias, wo, wq,
    )
    (send,) = call(other_body, [((4 * HD, D), BF)], ng, heads)
    got = swap(send, lambda i: i ^ 1)
    pn = lax.all_to_all(pn, "zero", 0, 0, tiled=True)
    (pair,) = call(pair_body, [((2 * HD, D), BF)], ng, heads, got)
    pair = swap(pair, partner)
    (own,) = call(own_body, [((2 * HD, D), F32)], ng, heads, got)
    scratch = pltpu.VMEM((D, R), F32)
    (wg,) = call(
        weights_body, [((2 * R, HALF), BF)], own, pair, scratch=[scratch] * 2
    )
    (back,) = call(
        post_body, [((R, 2, HALF), BF)], pn, stat, heads, wg, scratch=[scratch]
    )
    back = lax.all_to_all(back, "dp", 0, 0, tiled=True)
    enc, grad, qkv_share, out_share, gain_grad, bias_grad = call(
        final_body,
        [
            ((QW, R), BF),
            ((QW, R), BF),
            ((10, 3, 2, HD), F32),
            ((10, 2, HD), F32),
            ((1, 10), F32),
            ((1, 10), F32),
        ],
        odd, back,
    )
    return (
        enc.T,
        grad.T,
        qkv_share.transpose(0, 2, 1, 3),
        out_share.transpose(1, 2, 0),
        gain_grad.reshape(10),
        bias_grad.reshape(10),
    )


def solution(mesh):
    return jax.shard_map(
        local,
        mesh=mesh,
        in_specs=(
            P("dp", None),
            P("dp", None),
            P("dp", None),
            P("dp", None),
            P("dp", None),
            P(),
            P(),
            P(None, "zero", None, None),
            P("zero", None, None),
        ),
        out_specs=(
            P("dp", "zero"),
            P("dp", "zero"),
            P("dp", "zero", None, None),
            P("zero", None, "dp"),
            P("dp"),
            P("dp"),
        ),
        check_vma=False,
    )
```

```python
import jax
import jax.numpy as jnp
from jax import lax
from jax.experimental import pallas as pl
from jax.experimental.pallas import tpu as pltpu
from jax.sharding import PartitionSpec as P

EPS = 1e-06
R = 128
D = 1280
HD = 80
HG = 2
NQ = HG * 3 * HD
NO = HG * HD
QW = D // 4
QP = 384
F32 = jnp.float32
BF = jnp.bfloat16
PN = 5 * R
PNE = PN + 48
SUMS = 20 * HD
WG = SUMS + 64
HALF = (WG + 2 * QW) // 2


def dg(a, b, ca, cb):
    return lax.dot_general(a, b, (((ca,), (cb,)), ((), ())), preferred_element_type=F32)


def call(body, outs, *args, scratch=()):
    vmem = pl.BlockSpec(memory_space=pltpu.VMEM)
    return pl.pallas_call(
        body,
        out_shape=tuple(jax.ShapeDtypeStruct(s, d) for s, d in outs),
        in_specs=[vmem] * len(args),
        out_specs=(vmem,) * len(outs),
        scratch_shapes=scratch,
        compiler_params=pltpu.CompilerParams(vmem_limit_bytes=16 * 1024 * 1024),
    )(*args)


def lane(shape):
    return lax.broadcasted_iota(jnp.int32, shape, 1)


def sub(shape):
    return lax.broadcasted_iota(jnp.int32, shape, 0)


def place_bits():
    dp = lax.axis_index("dp")
    core = lax.rem(dp, 2)
    return core, jnp.where(core == 0, lax.rem(dp // 2, 2), lax.rem(dp // 16, 2))


def partner(i):
    return i ^ (2 if i % 2 == 0 else 16)


def one_hot(cond):
    return cond.astype(F32).astype(BF)


def pair_picks(send_ref):
    spread = one_hot(lane((R, 2 * R)) // 2 == sub((R, 2 * R)))
    rows = jnp.broadcast_to(send_ref[...], (8, R)).astype(F32).astype(BF)
    target = dg(rows, spread, 1, 0)[0:1].astype(jnp.int32)
    hit = sub((R, 2 * R)) == target
    odd = lane((R, 2 * R)) % 2
    return one_hot(hit & (odd == 0)), one_hot(hit & (odd == 1))


def high_low(value):
    high = value.astype(BF).astype(F32)
    return [high, value - high]


def gather_body(
    send_ref, xg_ref, recv_ref, seg_ref, gain_ref, bias_ref, wo_ref,
    o_ref, odd_ref, same_ref, gain_out, bias_out, wo_out,
):
    even, odd = pair_picks(send_ref)
    odd_ref[...] = odd
    pick = jnp.concatenate([even, odd], axis=0)
    o_ref[...] = dg(pick, xg_ref[...], 0, 0).astype(BF).reshape(R, 2, D)
    hit = sub((R, R)) == recv_ref[...]
    seg = jnp.sum(jnp.where(hit, seg_ref[...], 0), axis=1, keepdims=True)
    group = one_hot(seg == lane((R, R)))
    same_ref[...] = dg(group, group, 1, 1)
    gain_out[...] = gain_ref[...].reshape(1, D)
    bias_out[...] = bias_ref[...].reshape(1, D)
    wo_out[...] = wo_ref[...]


def norm_stats(x):
    mean = jnp.mean(x, axis=1, keepdims=True)
    centred = x - mean
    inv = lax.rsqrt(jnp.mean(centred * centred, axis=1, keepdims=True) + EPS)
    return mean, inv, centred * inv


def block_body(
    xg_ref, same_ref, gain_ref, bias_ref, wo_ref, wq_ref,
    pn_ref, ng_ref, heads_ref, stat_ref,
):
    xg = xg_ref[...].reshape(2 * R, D)
    at = lane((R, 2 * R)) - 2 * sub((R, 2 * R))
    x = dg(one_hot(at == 0), xg, 1, 0)
    g32 = dg(one_hot(at == 1), xg, 1, 0)
    g = g32.astype(BF)
    dh = dg(wo_ref[...], g, 1, 1).astype(BF)
    ng_ref[R:, :] = g
    mean, inv, xh = norm_stats(x)
    normed = (xh * gain_ref[...] + bias_ref[...]).astype(BF)
    ng_ref[:R, :] = normed
    for i in range(4):

        @pl.when(lax.axis_index("zero") == i)
        def _(i=i):
            cols = slice(i * QW, (i + 1) * QW)
            pad = jnp.zeros((R, QP - QW), F32)
            both = jnp.concatenate([x[:, cols], pad, g32[:, cols], pad], axis=1).astype(BF)
            for t in range(6):
                heads_ref[(5 + t) * R : (6 + t) * R] = both[:, t * R : (t + 1) * R]
            line = jnp.concatenate([gain_ref[:, cols], jnp.zeros((1, QP - QW), F32)], axis=1)
            for t in range(3):
                stat_ref[R + t : R + t + 1] = line[:, t * R : (t + 1) * R]

    stat_ref[:R] = jnp.where(lane((R, R)) < 64, mean, inv)
    qkv = dg(wq_ref[...], normed, 1, 1).astype(BF)
    same = same_ref[...] > 0.5
    heads = range(HG)
    q = [qkv[h * 3 * HD : h * 3 * HD + HD] for h in heads]
    k = [qkv[h * 3 * HD + HD : h * 3 * HD + 2 * HD] for h in heads]
    v = [qkv[h * 3 * HD + 2 * HD : (h + 1) * 3 * HD] for h in heads]
    dhh = [dh[h * HD : (h + 1) * HD] for h in heads]
    s = [dg(q[h], k[h], 0, 0) for h in heads]
    pg = [dg(dhh[h], v[h], 0, 0) for h in heads]
    s = [jnp.where(same, s[h] * (HD**-0.5), -1e30) for h in heads]
    e = [jnp.exp(s[h] - jnp.max(s[h], axis=1, keepdims=True)) for h in heads]
    w = [e[h] / jnp.sum(e[h], axis=1, keepdims=True) for h in heads]
    w16 = [w[h].astype(BF) for h in heads]
    delta = [jnp.sum(pg[h] * w[h], axis=1, keepdims=True) for h in heads]
    sg = [(w[h] * (pg[h] - delta[h]) * (HD**-0.5)).astype(BF) for h in heads]
    ho = [dg(v[h], w16[h], 1, 1).astype(BF) for h in heads]
    dv = [dg(dhh[h], w16[h], 1, 0).astype(BF) for h in heads]
    dq = [dg(k[h], sg[h], 1, 1).astype(BF) for h in heads]
    dk = [dg(q[h], sg[h], 1, 0).astype(BF) for h in heads]
    rows = [part for h in heads for part in (dq[h], dk[h], dv[h], ho[h])]
    heads_ref[: 8 * HD] = jnp.concatenate(rows, axis=0)
    qg = jnp.concatenate(rows[0:3] + rows[4:7], axis=0)
    ho = jnp.concatenate([rows[3], rows[7]], axis=0)
    p = dg(ho, wo_ref[...], 0, 0)
    for i in range(4):
        for t in range(2):
            pn_ref[i, t * R : (t + 1) * R] = p[:, i * QW + t * R : i * QW + (t + 1) * R].astype(BF)
    n = dg(qg, wq_ref[...], 0, 0)
    u = n * gain_ref[...]
    m1 = jnp.sum(u, axis=1, keepdims=True) * (1.0 / D)
    m2 = jnp.sum(u * xh, axis=1, keepdims=True) * (1.0 / D)
    gain_row = jnp.sum(n * xh, axis=0, keepdims=True)
    bias_row = jnp.sum(n, axis=0, keepdims=True)
    extra = []
    for row in high_low(gain_row) + high_low(bias_row):
        extra += [row[:, t * R : (t + 1) * R] for t in range(10)]
    diagonal = sub((R, R)) == lane((R, R))
    for m in (m1, m2):
        extra += high_low(jnp.sum(jnp.where(diagonal, m, 0.0), axis=0, keepdims=True))
    extra.append(jnp.zeros((PNE - PN - 44, R), F32))
    extra = jnp.concatenate(extra, axis=0).astype(BF)
    for i in range(4):
        at = i * QW
        mixed = jnp.concatenate([p[:, at + 2 * R : at + QW], n[:, at : at + 64]], axis=1)
        pn_ref[i, 2 * R : 3 * R] = mixed.astype(BF)
        for t in range(2):
            cols = slice(at + 64 + t * R, at + 64 + (t + 1) * R)
            pn_ref[i, (3 + t) * R : (4 + t) * R] = n[:, cols].astype(BF)
        pn_ref[i, PN:] = extra


def other_body(ng_ref, heads_ref, send_ref):
    other = (1 - place_bits()[0]) * 4 * HD
    a = heads_ref[pl.ds(pl.multiple_of(other, 4 * HD), 3 * HD), :]
    b = heads_ref[pl.ds(pl.multiple_of(other + 3 * HD, HD), HD), :]
    send_ref[: 3 * HD, :] = dg(a, ng_ref[:R, :], 1, 0).astype(BF)
    send_ref[3 * HD :, :] = dg(b, ng_ref[R:, :], 1, 0).astype(BF)


def half_rows(c, half, ng_ref, heads_ref, got_ref):
    rows = heads_ref[pl.ds(pl.multiple_of((c * 2 + half) * 2 * HD, 2 * HD), 2 * HD), :]
    out = half.astype(F32) * (sub((2 * HD, R)) >= HD).astype(F32)
    rows = rows.astype(F32)
    left = jnp.concatenate([rows * (1.0 - out), rows * out], axis=1).astype(BF)
    got = got_ref[pl.ds(pl.multiple_of(half * 2 * HD, 2 * HD), 2 * HD), :]
    return dg(left, ng_ref[...], 1, 0) + got.astype(F32)


def pair_body(ng_ref, heads_ref, got_ref, send_ref):
    c, half = place_bits()
    send_ref[...] = half_rows(c, 1 - half, ng_ref, heads_ref, got_ref).astype(BF)


def own_body(ng_ref, heads_ref, got_ref, first_ref, second_ref):
    c, half = place_bits()
    own = half_rows(c, half, ng_ref, heads_ref, got_ref)
    first_ref[:, :HD] = own[:HD].T
    second_ref[:, :HD] = own[HD:].T


def weights_body(own_first, own_second, pair_ref, o_ref, first_ref, second_ref):
    pair = pair_ref[...].astype(F32)
    first_ref[:, :HD] = own_first[:, :HD] + pair[:HD].T
    second_ref[:, :HD] = own_second[:, :HD] + pair[HD:].T
    slabs = []
    for i in range(10):
        rows = pl.ds(i, R, stride=10)
        slabs += [first_ref[rows, :][:, :HD], second_ref[rows, :][:, :HD]]
    slabs.append(jnp.zeros((R, 2 * HALF - SUMS), F32))
    row = jnp.concatenate(slabs, axis=1).astype(BF)
    both = jnp.concatenate([row[:, :HALF], row[:, HALF:]], axis=0)
    out = sub((2 * R, 2 * R))
    both = dg(one_hot(lane((2 * R, 2 * R)) == out // 2 + R * (out % 2)), both, 1, 0)
    o_ref[...] = both.astype(BF)


def post_body(pn_ref, stat_ref, heads_ref, wg_ref, o_ref, sum_ref):
    pn = jnp.sum(pn_ref[:, :PN].astype(F32), axis=0)
    extra = jnp.sum(pn_ref[:, PN:].astype(F32), axis=0)
    sums = [jnp.concatenate([extra[t : t + 1] for t in range(k, k + 10)], axis=1) for k in (0, 10, 20, 30)]
    rows = high_low(sums[0] + sums[1]) + high_low(sums[2] + sums[3])
    sum_ref[:, :8] = jnp.concatenate(rows + [jnp.zeros((4, D), F32)], axis=0).T
    sums = [sum_ref[pl.ds(i, R, stride=10), :][:, :4] for i in range(10)]
    tiles = [pn[t * R : (t + 1) * R] for t in range(5)]
    both = jnp.concatenate(tiles, axis=1)
    diagonal = sub((R, R)) == lane((R, R))
    m1 = jnp.sum(jnp.where(diagonal, extra[40:41] + extra[41:42], 0.0), axis=1, keepdims=True)
    m2 = jnp.sum(jnp.where(diagonal, extra[42:43] + extra[43:44], 0.0), axis=1, keepdims=True)
    quarters = [heads_ref[(5 + t) * R : (6 + t) * R].astype(F32) for t in range(6)]
    x = jnp.concatenate(quarters[:3], axis=1)[:, :QW]
    g = jnp.concatenate(quarters[3:], axis=1)[:, :QW]
    mean = stat_ref[:R, 0:1]
    inv = stat_ref[:R, 64:65]
    xh = (x - mean) * inv
    enc = x + both[:, :QW]
    gain = jnp.concatenate([stat_ref[R + t : R + t + 1] for t in range(3)], axis=1)[:, :QW]
    grad = both[:, QW:] * gain - m1 - xh * m2
    grad = g + inv * grad
    at = SUMS - HALF - 64
    gap = jnp.zeros((R, 64), F32)
    row = jnp.concatenate([gap] + sums + [gap[:, :24], enc, grad], axis=1).astype(BF)
    odd = one_hot(sub((2 * R, R)) == 2 * lane((2 * R, R)) + 1)
    tail = dg(odd, row, 1, 0) + wg_ref[:, at:].astype(F32)
    o_ref[...] = jnp.concatenate([wg_ref[:, :at], tail.astype(BF)], axis=1).reshape(R, 2, HALF)


def final_body(odd_ref, b_ref, e_ref, i_ref, a_ref, w_ref, gain_ref, bias_ref):
    back = b_ref[...].reshape(2 * R, HALF)
    rows = dg(back[:, WG - HALF :], odd_ref[...], 0, 1).astype(BF)
    e_ref[...] = rows[:QW]
    i_ref[...] = rows[QW:]
    row = sub((16, 2 * R))
    src = lane((16, 2 * R)) // 2
    half = jnp.where(src % 2 == 0, (src // 2) % 2, (src // 16) % 2)
    mask = (row == 2 * half + src % 2) | (row == 8)
    first = lane((16, 2 * R)) % 2 == 0
    sums = jnp.concatenate(
        [
            dg(one_hot(mask & first), back, 1, 0),
            dg(one_hot(mask & ~first), back[:, : WG - HALF], 1, 0),
        ],
        axis=1,
    )
    for i in range(10):
        at = i * 2 * HD
        a_ref[i, 0] = sums[0:2, at : at + HD]
        a_ref[i, 1] = sums[0:2, at + HD : at + 2 * HD]
        a_ref[i, 2] = sums[2:4, at : at + HD]
        w_ref[i] = sums[2:4, at + HD : at + 2 * HD]
        at = SUMS + 4 * i
        gain_ref[:, i : i + 1] = sums[8:9, at : at + 1] + sums[8:9, at + 1 : at + 2]
        bias_ref[:, i : i + 1] = sums[8:9, at + 2 : at + 3] + sums[8:9, at + 3 : at + 4]


def local(patches, cotangent, send_order, recv_order, segment_ids, ln_gain, ln_bias, w_qkv, w_out):
    wq = w_qkv.transpose(1, 2, 3, 0).reshape(NQ, D)
    wo = w_out.reshape(NO, D)

    def swap(a, other):
        return lax.ppermute(a, "dp", [(i, other(i)) for i in range(128)])

    xg = jnp.concatenate([patches, cotangent], axis=0)
    xg, odd, same, gain, bias, wo = call(
        gather_body,
        [((R, 2, D), BF), ((R, 2 * R), BF), ((R, R), F32), ((1, D), F32), ((1, D), F32), ((NO, D), BF)],
        send_order, xg, recv_order, segment_ids, ln_gain, ln_bias, wo,
    )
    xg = lax.all_to_all(xg, "dp", 0, 0, tiled=True)
    pn, ng, heads, stat = call(
        block_body,
        [
            ((4, PNE, R), BF),
            ((2 * R, D), BF),
            ((8 * HD + 6 * R, R), BF),
            ((R + 8, R), F32),
        ],
        xg, same, gain, bias, wo, wq,
    )
    (send,) = call(other_body, [((4 * HD, D), BF)], ng, heads)
    got = swap(send, lambda i: i ^ 1)
    pn = lax.all_to_all(pn, "zero", 0, 0, tiled=True)
    (pair,) = call(pair_body, [((2 * HD, D), BF)], ng, heads, got)
    pair = swap(pair, partner)
    own = call(own_body, [((D, R), F32)] * 2, ng, heads, got)
    scratch = pltpu.VMEM((D, R), F32)
    (wg,) = call(
        weights_body, [((2 * R, HALF), BF)], *own, pair, scratch=[scratch] * 2
    )
    (back,) = call(
        post_body, [((R, 2, HALF), BF)], pn, stat, heads, wg, scratch=[scratch]
    )
    back = lax.all_to_all(back, "dp", 0, 0, tiled=True)
    enc, grad, qkv_share, out_share, gain_grad, bias_grad = call(
        final_body,
        [
            ((QW, R), BF),
            ((QW, R), BF),
            ((10, 3, 2, HD), F32),
            ((10, 2, HD), F32),
            ((1, 10), F32),
            ((1, 10), F32),
        ],
        odd, back,
    )
    return (
        enc.T,
        grad.T,
        qkv_share.transpose(0, 2, 1, 3),
        out_share.transpose(1, 2, 0),
        gain_grad.reshape(10),
        bias_grad.reshape(10),
    )


def solution(mesh):
    return jax.shard_map(
        local,
        mesh=mesh,
        in_specs=(
            P("dp", None),
            P("dp", None),
            P("dp", None),
            P("dp", None),
            P("dp", None),
            P(),
            P(),
            P(None, "zero", None, None),
            P("zero", None, None),
        ),
        out_specs=(
            P("dp", "zero"),
            P("dp", "zero"),
            P("dp", "zero", None, None),
            P("zero", None, "dp"),
            P("dp"),
            P("dp"),
        ),
        check_vma=False,
    )
```
